32 devices in a mesh: row: 8 (over y, x, core), col: 4 (over z).
Axes of the slice: x: 2, y: 2, z: 4, core: 2. Of those that a mesh axis runs over, the one named last changes fastest.
Arguments:
- density: bfloat16 [1024, 1024], P('row', 'col'), as said below
- cotangent: bfloat16 [1024, 1024], P('row', 'col'), may hold values from -6 to 6
- block_pattern: int32 [16, 16], P('row', 'col'), may hold values from 0 to 1, as said below
- filter_pattern: int32 [16, 16], P('row', 'col'), may hold values from 0 to 1, as said below
Outputs:
- purified: bfloat16 [1024, 1024], P('row', 'col')
- gradient: bfloat16 [1024, 1024], P('row', 'col')
The draws below stay inside these ranges and needn't reach their ends.
Inputs may be any that keep to these rules, and one draw needn't show every extreme that they name: density is symmetric. `block_pattern`: symmetric, with ones on the diagonal. `filter_pattern`: symmetric, with ones on the diagonal.
All inputs are finite; a program needn't handle non-finite values.
Results may differ from the reference program's by a relative error of at most 0.0043.
Values may be sent and summed in bfloat16 or wider, within the bound.
No kernel may reach another device: no remote copies, remote signals or barrier semaphores. Data moves between devices by JAX's collectives and lax.ppermute only.
A program may use at most 64 MiB of HBM per device.

```python
import jax
import jax.numpy as jnp

BS = 64
N = 1024


def draw_density(key, part):
    raw = jax.random.normal(key, (N, N), jnp.float32)
    symmetric = (raw + raw.T) * 0.7071
    return (symmetric * (0.5 * N ** (-0.25))).astype(jnp.bfloat16)


def pattern_from(key, offset):
    block_count = N // BS
    upper = jax.random.randint(key, (block_count, block_count), 0, 100)
    row_index = jnp.arange(block_count)[:, None]
    col_index = jnp.arange(block_count)[None, :]
    symmetric = jnp.where(row_index <= col_index, upper, upper.T)
    threshold = 15 + offset + 60 * (row_index + col_index) // (2 * block_count - 1)
    chosen = (symmetric < threshold) | (row_index == col_index)
    return jnp.where(chosen, 1, 0).astype(jnp.int32)


def draw_block_pattern(key, part):
    return pattern_from(jax.random.fold_in(key, 11), 0)


def draw_filter_pattern(key, part):
    return pattern_from(jax.random.fold_in(key, 23), 20)


def levels(own_key, dims, shards, least, high):
    def one(axis_at, parts):
        heights = jax.random.uniform(jax.random.fold_in(jax.random.fold_in(own_key, 6), axis_at), (parts,), jnp.float32, least / len(shards), high / len(shards))
        return jnp.repeat(jnp.exp(heights), dims[axis_at] // parts).reshape((-1,) + (1,) * (len(dims) - axis_at - 1))

    gain = one(*shards[0])
    for cut in shards[1:]:
        gain = gain * one(*cut)
    return gain


def bell_draw(rng, extent, deviation, most, split=(), held_as=jnp.bfloat16):
    drawn = jax.random.normal(rng, extent, jnp.float32) * deviation
    if len(split) > 0:
        drawn = levels(rng, extent, split, -0.22, 0.18) * drawn
    return jnp.clip(drawn, min=-most, max=most).astype(held_as)


def setup_inputs(seed: int = 0) -> dict:
    key_list = jax.random.split(jax.random.key(seed), 5)
    density = draw_density(jax.random.fold_in(key_list[4], 71), 0)
    cotangent = bell_draw(key_list[1], (N, N), 1.0, 6.0, ((0, 8), (1, 4)))
    block_pattern = draw_block_pattern(jax.random.fold_in(key_list[4], 71), 0)
    filter_pattern = draw_filter_pattern(jax.random.fold_in(key_list[4], 71), 0)
    return {"density": density, "cotangent": cotangent, "block_pattern": block_pattern, "filter_pattern": filter_pattern}


def expand(pattern, block_size):
    spread = jnp.repeat(jnp.repeat(pattern, block_size, axis=0), block_size, axis=1)
    return spread.astype(jnp.float32)


def reference(density, cotangent, block_pattern, filter_pattern):
    keep_p = expand(block_pattern, BS)
    keep_f = expand(filter_pattern, BS)
    masked = (density.astype(jnp.float32) * keep_p).astype(jnp.bfloat16)
    square = (jnp.dot(masked, masked, preferred_element_type=jnp.float32) * keep_f).astype(jnp.bfloat16)
    cubic_term = jnp.dot(square, masked, preferred_element_type=jnp.float32) * keep_f
    purified = (3.0 * square.astype(jnp.float32) - 2.0 * cubic_term).astype(jnp.bfloat16)
    weighted = (-2.0 * cotangent.astype(jnp.float32) * keep_f).astype(jnp.bfloat16)
    back_term = jnp.dot(weighted, masked, preferred_element_type=jnp.float32)
    square_grad = ((3.0 * cotangent.astype(jnp.float32) + back_term) * keep_f).astype(jnp.bfloat16)
    summed = jnp.dot(square, weighted, preferred_element_type=jnp.float32)
    summed = summed + jnp.dot(square_grad, masked, preferred_element_type=jnp.float32)
    summed = summed + jnp.dot(masked, square_grad, preferred_element_type=jnp.float32)
    gradient = (summed * keep_p).astype(jnp.bfloat16)
    return purified, gradient
```

```python
import jax
import jax.numpy as jnp
from jax import lax
from jax.sharding import PartitionSpec as P


def expand(pattern, block_size):
    height, width = pattern.shape
    spread = jnp.broadcast_to(pattern[:, None, :, None], (height, block_size, width, block_size))
    return spread.reshape(height * block_size, width * block_size).astype(jnp.float32)


def dot(a, b):
    return jnp.dot(a, b, preferred_element_type=jnp.float32)


def on_device(density, cotangent, block_pattern, filter_pattern):
    block_size = density.shape[0] // block_pattern.shape[0]
    keep_p = expand(block_pattern, block_size)
    keep_f = expand(filter_pattern, block_size)
    masked = (density.astype(jnp.float32) * keep_p).astype(jnp.bfloat16)
    filtered = (cotangent.astype(jnp.float32) * keep_f).astype(jnp.bfloat16)
    pair = jnp.stack([masked, filtered])
    pair_rows = lax.all_gather(pair, "col", axis=2, tiled=True)
    pair_cols = lax.all_gather(pair, "row", axis=1, tiled=True)
    masked_cols, filtered_cols = pair_cols[0], pair_cols[1]
    masked_rows, filtered_rows = pair_rows[0], pair_rows[1]
    square = (dot(masked_rows, masked_cols) * keep_f).astype(jnp.bfloat16)
    back_term = -2.0 * dot(filtered_rows, masked_cols)
    square_grad = ((3.0 * cotangent.astype(jnp.float32) + back_term) * keep_f).astype(jnp.bfloat16)
    rows = lax.all_gather(jnp.stack([square, square_grad]), "col", axis=2, tiled=True)
    grad_cols = lax.all_gather(square_grad, "row", axis=0, tiled=True)
    square_rows, grad_rows = rows[0], rows[1]
    cubic_term = dot(square_rows, masked_cols) * keep_f
    purified = (3.0 * square.astype(jnp.float32) - 2.0 * cubic_term).astype(jnp.bfloat16)
    summed = -2.0 * dot(square_rows, filtered_cols) + dot(masked_rows, grad_cols) + dot(grad_rows, masked_cols)
    gradient = (summed * keep_p).astype(jnp.bfloat16)
    return (purified, gradient)


def solution(mesh):
    placed = (P("row", "col"), P("row", "col"), P("row", "col"), P("row", "col"))
    return jax.shard_map(
        on_device,
        mesh=mesh,
        in_specs=placed,
        out_specs=(P("row", "col"), P("row", "col")),
        check_vma=False,
    )
```

```python
import jax
import jax.numpy as jnp
from jax import lax
from jax.sharding import PartitionSpec as P


def expand(pattern, block_size):
    height, width = pattern.shape
    spread = jnp.broadcast_to(pattern[:, None, :, None], (height, block_size, width, block_size))
    return spread.reshape(height * block_size, width * block_size).astype(jnp.float32)


def dot(a, b):
    return jnp.dot(a, b, preferred_element_type=jnp.float32)


def send_all(part, axis_name, size):
    pieces = [part]
    for shift in range(1, size):
        pieces.append(lax.ppermute(part, axis_name, [(i, (i + shift) % size) for i in range(size)]))
    return pieces


def place(pieces, axis_name, size, axis):
    width = pieces[0].shape[axis]
    shape = list(pieces[0].shape)
    shape[axis] = width * size
    whole = jnp.zeros(shape, pieces[0].dtype)
    here = lax.axis_index(axis_name)
    for shift, piece in enumerate(pieces):
        at = lax.rem(here - shift + size, size) * width
        whole = lax.dynamic_update_slice_in_dim(whole, piece, at, axis)
    return whole


def on_device(n_row, n_col, density, cotangent, block_pattern, filter_pattern):
    block_size = density.shape[0] // block_pattern.shape[0]
    keep_p = expand(block_pattern, block_size)
    keep_f = expand(filter_pattern, block_size)
    masked = (density.astype(jnp.float32) * keep_p).astype(jnp.bfloat16)
    filtered = (cotangent.astype(jnp.float32) * keep_f).astype(jnp.bfloat16)
    pair = jnp.stack([masked, filtered])
    row_pieces = send_all(pair, "col", n_col)
    col_pieces = send_all(pair, "row", n_row)
    pair_rows = place(row_pieces, "col", n_col, 2)
    pair_cols = place(col_pieces, "row", n_row, 1)
    masked_cols, filtered_cols = pair_cols[0], pair_cols[1]
    masked_rows, filtered_rows = pair_rows[0], pair_rows[1]
    square = (dot(masked_rows, masked_cols) * keep_f).astype(jnp.bfloat16)
    back_term = -2.0 * dot(filtered_rows, masked_cols)
    square_grad = ((3.0 * cotangent.astype(jnp.float32) + back_term) * keep_f).astype(jnp.bfloat16)
    row_pieces = send_all(jnp.stack([square, square_grad]), "col", n_col)
    col_pieces = send_all(square_grad, "row", n_row)
    rows = place(row_pieces, "col", n_col, 2)
    grad_cols = place(col_pieces, "row", n_row, 0)
    square_rows, grad_rows = rows[0], rows[1]
    cubic_term = dot(square_rows, masked_cols) * keep_f
    purified = (3.0 * square.astype(jnp.float32) - 2.0 * cubic_term).astype(jnp.bfloat16)
    summed = -2.0 * dot(square_rows, filtered_cols) + dot(masked_rows, grad_cols) + dot(grad_rows, masked_cols)
    gradient = (summed * keep_p).astype(jnp.bfloat16)
    return (purified, gradient)


def solution(mesh):
    placed = (P("row", "col"), P("row", "col"), P("row", "col"), P("row", "col"))

    def local(*arrays):
        return on_device(mesh.shape["row"], mesh.shape["col"], *arrays)

    return jax.shard_map(
        local,
        mesh=mesh,
        in_specs=placed,
        out_specs=(P("row", "col"), P("row", "col")),
        check_vma=False,
    )
```

```python
import jax
import jax.numpy as jnp
from jax import lax
from jax.sharding import PartitionSpec as P


def expand(pattern, block_size):
    height, width = pattern.shape
    spread = jnp.broadcast_to(pattern[:, None, :, None], (height, block_size, width, block_size))
    return spread.reshape(height * block_size, width * block_size).astype(jnp.float32)


def dot(a, b):
    return jnp.dot(a, b, preferred_element_type=jnp.float32)


def spread_out(part, axis_name, size):
    copies = jnp.broadcast_to(part[None], (size,) + part.shape)
    return lax.all_to_all(copies, axis_name, split_axis=0, concat_axis=0)


def row_dot(pieces, cols):
    width = pieces.shape[2]
    total = dot(pieces[0], cols[:width])
    for k in range(1, pieces.shape[0]):
        total = total + dot(pieces[k], cols[k * width:(k + 1) * width])
    return total


def on_device(n_row, n_col, density, cotangent, block_pattern, filter_pattern):
    height, width = density.shape
    block_size = height // block_pattern.shape[0]
    keep_p = expand(block_pattern, block_size)
    keep_f = expand(filter_pattern, block_size)
    masked = (density.astype(jnp.float32) * keep_p).astype(jnp.bfloat16)
    filtered = (cotangent.astype(jnp.float32) * keep_f).astype(jnp.bfloat16)
    pair = jnp.stack([masked, filtered])
    pair_rows = spread_out(pair, "col", n_col)
    pair_cols = spread_out(pair, "row", n_row)
    masked_cols = pair_cols[:, 0].reshape(n_row * height, width)
    filtered_cols = pair_cols[:, 1].reshape(n_row * height, width)
    masked_rows, filtered_rows = pair_rows[:, 0], pair_rows[:, 1]
    square = (row_dot(masked_rows, masked_cols) * keep_f).astype(jnp.bfloat16)
    back_term = -2.0 * row_dot(filtered_rows, masked_cols)
    square_grad = ((3.0 * cotangent.astype(jnp.float32) + back_term) * keep_f).astype(jnp.bfloat16)
    rows = spread_out(jnp.stack([square, square_grad]), "col", n_col)
    grad_cols = spread_out(square_grad, "row", n_row).reshape(n_row * height, width)
    square_rows, grad_rows = rows[:, 0], rows[:, 1]
    cubic_term = row_dot(square_rows, masked_cols) * keep_f
    purified = (3.0 * square.astype(jnp.float32) - 2.0 * cubic_term).astype(jnp.bfloat16)
    summed = -2.0 * row_dot(square_rows, filtered_cols)
    summed = summed + row_dot(masked_rows, grad_cols) + row_dot(grad_rows, masked_cols)
    gradient = (summed * keep_p).astype(jnp.bfloat16)
    return (purified, gradient)


def solution(mesh):
    placed = (P("row", "col"), P("row", "col"), P("row", "col"), P("row", "col"))

    def local(*arrays):
        return on_device(mesh.shape["row"], mesh.shape["col"], *arrays)

    return jax.shard_map(
        local,
        mesh=mesh,
        in_specs=placed,
        out_specs=(P("row", "col"), P("row", "col")),
        check_vma=False,
    )
```

```python
import jax
import jax.numpy as jnp
from jax import lax
from jax.sharding import PartitionSpec as P


def dot(a, b):
    return jnp.dot(a, b, preferred_element_type=jnp.float32)


def expand(pattern, shape):
    block_rows, block_cols = pattern.shape
    row = lax.broadcasted_iota(jnp.int32, shape, 0) // (shape[0] // block_rows)
    col = lax.broadcasted_iota(jnp.int32, shape, 1) // (shape[1] // block_cols)
    kept = jnp.zeros(shape, jnp.int32)
    for i in range(block_rows):
        for j in range(block_cols):
            kept = jnp.where((row == i) & (col == j), pattern[i, j], kept)
    return kept != 0


def swap(part, axis_name, size, flip):
    return lax.ppermute(part, axis_name, [(i, i ^ flip) for i in range(size)])


def direct(part, axis_name, size):
    return [part] + [swap(part, axis_name, size, k) for k in range(1, size)]


def double(blocks, axis_name, size, flips):
    for flip in flips:
        blocks = jnp.concatenate([blocks, swap(blocks, axis_name, size, flip)])
    return blocks


def place(pieces, owners, axis):
    width = pieces[0].shape[axis]
    shape = list(pieces[0].shape)
    shape[axis] = width * len(pieces)
    whole = jnp.zeros(shape, pieces[0].dtype)
    for owner, piece in zip(owners, pieces):
        whole = lax.dynamic_update_slice_in_dim(whole, piece, owner * width, axis)
    return whole


def on_device(n_row, n_col, density, cotangent, block_pattern, filter_pattern):
    keep_p = expand(block_pattern, density.shape)
    keep_f = expand(filter_pattern, density.shape)
    zero = jnp.zeros((), jnp.bfloat16)
    masked = jnp.where(keep_p, density, zero)
    filtered = jnp.where(keep_f, cotangent, zero)
    pair = jnp.stack([masked, filtered])
    here_row, here_col = lax.axis_index("row"), lax.axis_index("col")

    flips = []
    while 2 ** len(flips) < n_row:
        flips.insert(0, 2 ** len(flips))
    offsets = [0]
    for flip in flips:
        offsets = offsets + [at + flip for at in offsets]
    row_owners = [here_row ^ at for at in offsets]
    col_owners = [here_col ^ at for at in range(n_col)]

    pair_rows = place(direct(pair, "col", n_col), col_owners, 2)
    pair_cols = double(pair[None], "row", n_row, flips[:-1])
    masked_blocks = double(pair_cols[:, 0], "row", n_row, flips[-1:])
    masked_cols = place(list(masked_blocks), row_owners, 0)
    masked_rows, filtered_rows = pair_rows[0], pair_rows[1]
    square = jnp.where(keep_f, dot(masked_rows, masked_cols), 0.0).astype(jnp.bfloat16)
    back_term = -2.0 * dot(filtered_rows, masked_cols)
    square_grad = 3.0 * filtered.astype(jnp.float32) + jnp.where(keep_f, back_term, 0.0)
    square_grad = square_grad.astype(jnp.bfloat16)

    rows = place(direct(jnp.stack([square, square_grad]), "col", n_col), col_owners, 2)
    grad_blocks = double(square_grad[None], "row", n_row, flips[:-1])
    late_blocks = double(jnp.stack([grad_blocks, pair_cols[:, 1]], 1), "row", n_row, flips[-1:])
    late_cols = place(list(late_blocks), row_owners, 1)
    grad_cols, filtered_cols = late_cols[0], late_cols[1]
    square_rows, grad_rows = rows[0], rows[1]
    cubic_term = jnp.where(keep_f, dot(square_rows, masked_cols), 0.0)
    purified = (3.0 * square.astype(jnp.float32) - 2.0 * cubic_term).astype(jnp.bfloat16)
    summed = -2.0 * dot(square_rows, filtered_cols) + dot(masked_rows, grad_cols) + dot(grad_rows, masked_cols)
    gradient = jnp.where(keep_p, summed, 0.0).astype(jnp.bfloat16)
    return (purified, gradient)


def solution(mesh):
    placed = (P("row", "col"), P("row", "col"), P("row", "col"), P("row", "col"))

    def local(*arrays):
        return on_device(mesh.shape["row"], mesh.shape["col"], *arrays)

    return jax.shard_map(
        local,
        mesh=mesh,
        in_specs=placed,
        out_specs=(P("row", "col"), P("row", "col")),
        check_vma=False,
    )
```

```python
import jax
import jax.numpy as jnp
from jax import lax
from jax.sharding import PartitionSpec as P


def dot(a, b):
    return jnp.dot(a, b, preferred_element_type=jnp.float32)


def expand(pattern, block_size):
    height, width = pattern.shape
    spread = jnp.broadcast_to(pattern[:, None, :, None], (height, block_size, width, block_size))
    return spread.reshape(height * block_size, width * block_size).astype(jnp.float32)


def flips_of(size):
    flips = []
    while 2 ** len(flips) < size:
        flips.insert(0, 2 ** len(flips))
    return flips


def gather(own, axis_name, size, flips):
    def swap(held, flip):
        exchange = [(i, i ^ flip) for i in range(size)]
        return [(at ^ flip, lax.ppermute(block, axis_name, exchange)) for at, block in held]

    held = [(0, own)]
    for flip in flips[:-2]:
        held = held + swap(held, flip)
    if len(flips) >= 2:
        far = swap(held, flips[-2])
        near = swap(held, flips[-1])
        held = held + far + near + swap(far, flips[-1])
    elif flips:
        held = held + swap(held, flips[-1])
    return held


def place(held, here, axis):
    width = held[0][1].shape[axis]
    shape = list(held[0][1].shape)
    shape[axis] = width * len(held)
    whole = jnp.zeros(shape, held[0][1].dtype)
    for at, block in held:
        whole = lax.dynamic_update_slice_in_dim(whole, block, (here ^ at) * width, axis)
    return whole


def last_hop(blocks, size):
    exchange = [(i, i ^ 1) for i in range(size)]
    return lax.ppermute(blocks, "row", exchange)


def on_device(n_row, n_col, density, cotangent, block_pattern, filter_pattern):
    block_size = density.shape[0] // block_pattern.shape[0]
    keep_p = expand(block_pattern, block_size)
    keep_f = expand(filter_pattern, block_size)
    masked = (density.astype(jnp.float32) * keep_p).astype(jnp.bfloat16)
    filtered = (cotangent.astype(jnp.float32) * keep_f).astype(jnp.bfloat16)
    pair = jnp.stack([masked, filtered])
    here_row, here_col = lax.axis_index("row"), lax.axis_index("col")
    col_flips, row_flips = flips_of(n_col), flips_of(n_row)

    pair_rows = place(gather(pair, "col", n_col, col_flips), here_col, 2)
    held = gather(pair, "row", n_row, row_flips[:-1])
    masked_held = [(at, block[0]) for at, block in held]
    other = last_hop(jnp.stack([block for _, block in masked_held]), n_row)
    masked_held = masked_held + [(at ^ 1, other[k]) for k, (at, _) in enumerate(held)]
    masked_cols = place(masked_held, here_row, 0)
    masked_rows, filtered_rows = pair_rows[0], pair_rows[1]
    square = (dot(masked_rows, masked_cols) * keep_f).astype(jnp.bfloat16)
    back_term = -2.0 * dot(filtered_rows, masked_cols)
    square_grad = ((3.0 * cotangent.astype(jnp.float32) + back_term) * keep_f).astype(jnp.bfloat16)

    rows = place(gather(jnp.stack([square, square_grad]), "col", n_col, col_flips), here_col, 2)
    grad_held = gather(square_grad, "row", n_row, row_flips[:-1])
    late_held = [(at, jnp.stack([grad, pair[1]])) for (at, grad), (_, pair) in zip(grad_held, held)]
    other = last_hop(jnp.stack([block for _, block in late_held]), n_row)
    late_held = late_held + [(at ^ 1, other[k]) for k, (at, _) in enumerate(held)]
    late_cols = place(late_held, here_row, 1)
    grad_cols, filtered_cols = late_cols[0], late_cols[1]
    square_rows, grad_rows = rows[0], rows[1]
    cubic_term = dot(square_rows, masked_cols) * keep_f
    purified = (3.0 * square.astype(jnp.float32) - 2.0 * cubic_term).astype(jnp.bfloat16)
    summed = -2.0 * dot(square_rows, filtered_cols) + dot(masked_rows, grad_cols) + dot(grad_rows, masked_cols)
    gradient = (summed * keep_p).astype(jnp.bfloat16)
    return (purified, gradient)


def solution(mesh):
    placed = (P("row", "col"), P("row", "col"), P("row", "col"), P("row", "col"))

    def local(*arrays):
        return on_device(mesh.shape["row"], mesh.shape["col"], *arrays)

    return jax.shard_map(
        local,
        mesh=mesh,
        in_specs=placed,
        out_specs=(P("row", "col"), P("row", "col")),
        check_vma=False,
    )
```

```python
import jax
import jax.numpy as jnp
from jax import lax
from jax.experimental import pallas as pl
from jax.experimental.pallas import tpu as pltpu
from jax.sharding import PartitionSpec as P


def dot(a, b):
    return jnp.dot(a, b, preferred_element_type=jnp.float32)


def mask_kernel(block_size, pattern_refs, dense_refs, pair_ref, kept_ref, pattern_held, dense_held, sems):
    copies = [pltpu.make_async_copy(ref, pattern_held.at[k], sems.at[k]) for k, ref in enumerate(pattern_refs)]
    copies += [pltpu.make_async_copy(ref, dense_held.at[k], sems.at[2 + k]) for k, ref in enumerate(dense_refs)]
    for copy in copies:
        copy.start()
    for copy in copies:
        copy.wait()
    _, height, width = dense_held.shape
    lane = lax.broadcasted_iota(jnp.int32, (block_size, width), 1) // block_size
    for k in range(2):
        for i in range(height // block_size):
            rows = pl.ds(i * block_size, block_size)
            kept = jnp.zeros((block_size, width), jnp.float32)
            for j in range(width // block_size):
                kept = jnp.where(lane == j, pattern_held[k, i, j].astype(jnp.float32), kept)
            kept_ref[k, rows, :] = kept
            pair_ref[k, rows, :] = (dense_held[k, rows, :].astype(jnp.float32) * kept).astype(pair_ref.dtype)


def mask(density, cotangent, block_pattern, filter_pattern):
    block_size = density.shape[0] // block_pattern.shape[0]

    def kernel(p_ref, f_ref, density_ref, cotangent_ref, *rest):
        mask_kernel(block_size, (p_ref, f_ref), (density_ref, cotangent_ref), *rest)

    return pl.pallas_call(
        kernel,
        out_shape=(
            jax.ShapeDtypeStruct((2,) + density.shape, density.dtype),
            jax.ShapeDtypeStruct((2,) + density.shape, jnp.float32),
        ),
        in_specs=[pl.BlockSpec(memory_space=pltpu.HBM)] * 4,
        out_specs=(pl.BlockSpec(memory_space=pltpu.VMEM), pl.BlockSpec(memory_space=pltpu.VMEM)),
        scratch_shapes=[
            pltpu.SMEM((2,) + block_pattern.shape, jnp.int32),
            pltpu.VMEM((2,) + density.shape, density.dtype),
            pltpu.SemaphoreType.DMA((4,)),
        ],
        name="mask",
    )(*(pltpu.with_memory_space_constraint(x, pltpu.HBM) for x in (block_pattern, filter_pattern, density, cotangent)))


def flips_of(size):
    flips = []
    while 2 ** len(flips) < size:
        flips.insert(0, 2 ** len(flips))
    return flips


def swap(held, axis_name, size, flips):
    return [
        (at ^ flip, lax.ppermute(block, axis_name, [(i, i ^ flip) for i in range(size)]))
        for flip in flips
        for at, block in held
    ]


def double(held, axis_name, size, flips):
    for flip in flips:
        both = jnp.stack([block for _, block in held])
        both = lax.ppermute(both, axis_name, [(i, i ^ flip) for i in range(size)])
        held = held + [(at ^ flip, both[k]) for k, (at, _) in enumerate(held)]
    return held


def forward(held, axis_name, size, flips):
    held = double(held, axis_name, size, flips[:-2])
    far = swap(held, axis_name, size, flips[-2:-1])
    near = swap(held, axis_name, size, flips[-1:])
    return held + far + near + swap(far, axis_name, size, flips[-1:])


def place(held, here, axis):
    width = held[0][1].shape[axis]
    shape = list(held[0][1].shape)
    shape[axis] = width * len(held)
    whole = jnp.zeros(shape, held[0][1].dtype)
    for at, block in held:
        whole = lax.dynamic_update_slice_in_dim(whole, block, (here ^ at) * width, axis)
    return whole


def on_device(n_row, n_col, density, cotangent, block_pattern, filter_pattern):
    pair, kept = mask(density, cotangent, block_pattern, filter_pattern)
    keep_p, keep_f = kept[0], kept[1]
    here_row, here_col = lax.axis_index("row"), lax.axis_index("col")

    col_flips, row_flips = flips_of(n_col), flips_of(n_row)
    col_held = forward([(0, pair)], "col", n_col, col_flips)
    masked_held = double([(0, pair[0])], "row", n_row, row_flips)
    masked_cols = place(masked_held, here_row, 0)
    pair_rows = place(col_held, here_col, 2)
    masked_rows, filtered_rows = pair_rows[0], pair_rows[1]
    square = (dot(masked_rows, masked_cols) * keep_f).astype(jnp.bfloat16)
    back_term = -2.0 * dot(filtered_rows, masked_cols)
    square_grad = ((3.0 * cotangent.astype(jnp.float32) + back_term) * keep_f).astype(jnp.bfloat16)

    col_held = forward([(0, jnp.stack([square, square_grad]))], "col", n_col, col_flips)
    late_held = forward([(0, jnp.stack([square_grad, pair[1]]))], "row", n_row, row_flips[:-1])
    late_held = double(late_held, "row", n_row, row_flips[-1:])
    late_cols = place(late_held, here_row, 1)
    grad_cols, filtered_cols = late_cols[0], late_cols[1]
    rows = place(col_held, here_col, 2)
    square_rows, grad_rows = rows[0], rows[1]
    cubic_term = dot(square_rows, masked_cols) * keep_f
    purified = (3.0 * square.astype(jnp.float32) - 2.0 * cubic_term).astype(jnp.bfloat16)
    summed = -2.0 * dot(square_rows, filtered_cols) + dot(masked_rows, grad_cols) + dot(grad_rows, masked_cols)
    gradient = (summed * keep_p).astype(jnp.bfloat16)
    return (purified, gradient)


def solution(mesh):
    placed = (P("row", "col"), P("row", "col"), P("row", "col"), P("row", "col"))

    def local(*arrays):
        return on_device(mesh.shape["row"], mesh.shape["col"], *arrays)

    return jax.shard_map(
        local,
        mesh=mesh,
        in_specs=placed,
        out_specs=(P("row", "col"), P("row", "col")),
        check_vma=False,
    )
```

```python
import jax
import jax.numpy as jnp
from jax import lax
from jax.experimental import pallas as pl
from jax.experimental.pallas import tpu as pltpu
from jax.sharding import PartitionSpec as P

IN_HBM = pl.BlockSpec(memory_space=pltpu.HBM)
IN_VMEM = pl.BlockSpec(memory_space=pltpu.VMEM)
IN_SMEM = pl.BlockSpec(memory_space=pltpu.SMEM)
EARLY = pl.CostEstimate(flops=6_000_000_000, bytes_accessed=0, transcendentals=0)


def dot(a, b):
    return jnp.dot(a, b, preferred_element_type=jnp.float32)


def mask(density, cotangent, block_pattern, filter_pattern):
    height, width = density.shape
    block_size = height // block_pattern.shape[0]

    def kernel(*refs):
        pattern_refs, dense_refs = refs[:2], refs[2:4]
        pair_ref, kept_ref, pattern_held, dense_held, sems = refs[4:]
        copies = []
        for k in range(2):
            copies.append(pltpu.make_async_copy(pattern_refs[k], pattern_held.at[k], sems.at[k]))
            copies.append(pltpu.make_async_copy(dense_refs[k], dense_held.at[k], sems.at[2 + k]))
        for copy in copies:
            copy.start()
        for copy in copies:
            copy.wait()
        lane = lax.broadcasted_iota(jnp.int32, (block_size, width), 1) // block_size
        for k in range(2):
            for i in range(height // block_size):
                rows = pl.ds(i * block_size, block_size)
                kept = jnp.zeros((block_size, width), jnp.float32)
                for j in range(width // block_size):
                    kept = jnp.where(lane == j, pattern_held[k, i, j].astype(jnp.float32), kept)
                kept_ref[k, rows, :] = kept
                pair_ref[k, rows, :] = (dense_held[k, rows, :].astype(jnp.float32) * kept).astype(pair_ref.dtype)

    inputs = (block_pattern, filter_pattern, density, cotangent)
    return pl.pallas_call(
        kernel,
        out_shape=(
            pltpu.VMEM((2, height, width), density.dtype),
            pltpu.VMEM((2, height, width), jnp.float32),
        ),
        in_specs=[IN_HBM] * 4,
        out_specs=(IN_VMEM, IN_VMEM),
        scratch_shapes=[
            pltpu.SMEM((2,) + block_pattern.shape, jnp.int32),
            pltpu.VMEM((2, height, width), density.dtype),
            pltpu.SemaphoreType.DMA((4,)),
        ],
        name="mask",
    )(*(pltpu.with_memory_space_constraint(x, pltpu.HBM) for x in inputs))


def settle(block):
    def kernel(block_ref, out_ref):
        out_ref[...] = block_ref[...]

    return pl.pallas_call(
        kernel,
        out_shape=pltpu.VMEM(block.shape, block.dtype),
        in_specs=[IN_VMEM],
        out_specs=IN_VMEM,
        cost_estimate=EARLY,
        name="settle",
    )(block)


def flips_of(size):
    flips = []
    while 2 ** len(flips) < size:
        flips.insert(0, 2 ** len(flips))
    return flips


def swap(held, axis_name, size, flips):
    return [
        ([at ^ flip for at in ats], lax.ppermute(blocks, axis_name, [(i, i ^ flip) for i in range(size)]))
        for flip in flips
        for ats, blocks in held
    ]


def double(held, axis_name, size, flips):
    for flip in flips:
        ats = [at for entry in held for at in entry[0]]
        blocks = held[0][1] if len(held) == 1 else jnp.concatenate([entry[1] for entry in held])
        held = held + swap([(ats, blocks)], axis_name, size, [flip])
    return held


def forward(held, axis_name, size, flips):
    held = double(held, axis_name, size, flips[:-2])
    far = swap(held, axis_name, size, flips[-2:-1])
    near = swap(held, axis_name, size, flips[-1:])
    return held + far + near + swap(far, axis_name, size, flips[-1:])


def pieces_of(held, refs):
    for (ats, _), ref in zip(held, refs):
        for k, at in enumerate(ats):
            yield at, ref.at[k]


def part(ref, owner, size):
    return ref.at[pl.ds(pl.multiple_of(owner * size, size), size), :]


def square_step(here, pair, kept, row_held, col_held):
    _, height, width = pair.shape
    n_row = sum(len(ats) for ats, _ in row_held)
    n_in = len(row_held) + len(col_held)

    def kernel(here_ref, pair_ref, kept_ref, *refs):
        row_refs, col_refs = refs[:len(row_held)], refs[len(row_held):n_in]
        both_ref, cols_ref = refs[n_in:]
        for at, block in pieces_of(row_held, row_refs):
            part(cols_ref, here_ref[0] ^ at, height)[...] = block[...]
        total = jnp.zeros((2 * height, width), jnp.float32)
        for at, piece in pieces_of(col_held, col_refs):
            rows = piece[...].reshape(2 * height, width)
            total = total + dot(rows, part(cols_ref, here_ref[1] ^ at, width)[...])
        both_ref[0] = (total[:height] * kept_ref[1]).astype(both_ref.dtype)
        grad = 3.0 * pair_ref[1].astype(jnp.float32) - 2.0 * total[height:]
        both_ref[1] = (grad * kept_ref[1]).astype(both_ref.dtype)

    return pl.pallas_call(
        kernel,
        out_shape=(
            pltpu.VMEM((2, height, width), pair.dtype),
            pltpu.VMEM((n_row * height, width), pair.dtype),
        ),
        in_specs=[IN_SMEM] + [IN_VMEM] * (2 + n_in),
        out_specs=(IN_VMEM, IN_VMEM),
        name="square_step",
    )(here, pair, kept, *(blocks for _, blocks in row_held + col_held))


def purify_step(here, both, kept, masked_cols, both_held):
    _, height, width = both.shape

    def kernel(here_ref, both_ref, kept_ref, masked_ref, *refs):
        both_refs, (purified_ref, back_ref) = refs[:-2], refs[-2:]
        total = jnp.zeros((2 * height, width), jnp.float32)
        for at, piece in pieces_of(both_held, both_refs):
            rows = piece[...].reshape(2 * height, width)
            total = total + dot(rows, part(masked_ref, here_ref[1] ^ at, width)[...])
        cubic = total[:height] * kept_ref[1]
        purified_ref[...] = (3.0 * both_ref[0].astype(jnp.float32) - 2.0 * cubic).astype(purified_ref.dtype)
        back_ref[...] = total[height:]

    return pl.pallas_call(
        kernel,
        out_shape=(
            jax.ShapeDtypeStruct((height, width), both.dtype),
            pltpu.VMEM((height, width), jnp.float32),
        ),
        in_specs=[IN_SMEM] + [IN_VMEM] * (3 + len(both_held)),
        out_specs=(IN_VMEM, IN_VMEM),
        cost_estimate=EARLY,
        name="purify_step",
    )(here, both, kept, masked_cols, *(blocks for _, blocks in both_held))


def gradient_step(here, kept, back, late_held, pair_held, both_held):
    height, width = back.shape
    n_row = sum(len(ats) for ats, _ in late_held)
    cuts = [len(late_held), len(late_held) + len(pair_held), len(late_held) + len(pair_held) + len(both_held)]

    def kernel(here_ref, kept_ref, back_ref, *refs):
        late_refs, pair_refs, both_refs = refs[:cuts[0]], refs[cuts[0]:cuts[1]], refs[cuts[1]:cuts[2]]
        gradient_ref, late_cols = refs[cuts[2]:]
        for at, block in pieces_of(late_held, late_refs):
            for k in range(2):
                part(late_cols.at[k], here_ref[0] ^ at, height)[...] = block[k]
        summed = back_ref[...]
        for at, piece in pieces_of(pair_held, pair_refs):
            summed = summed + dot(piece[0], part(late_cols.at[0], here_ref[1] ^ at, width)[...])
        with_cotangent = jnp.zeros((height, width), jnp.float32)
        for at, piece in pieces_of(both_held, both_refs):
            with_cotangent = with_cotangent + dot(piece[0], part(late_cols.at[1], here_ref[1] ^ at, width)[...])
        summed = summed - 2.0 * with_cotangent
        gradient_ref[...] = (summed * kept_ref[0]).astype(gradient_ref.dtype)

    return pl.pallas_call(
        kernel,
        out_shape=jax.ShapeDtypeStruct((height, width), late_held[0][1].dtype),
        in_specs=[IN_SMEM] + [IN_VMEM] * (2 + cuts[2]),
        out_specs=IN_VMEM,
        scratch_shapes=[pltpu.VMEM((2, n_row * height, width), late_held[0][1].dtype)],
        name="gradient_step",
    )(here, kept, back, *(blocks for _, blocks in late_held + pair_held + both_held))


def on_device(n_row, n_col, density, cotangent, block_pattern, filter_pattern):
    here = jnp.stack([lax.axis_index("row"), lax.axis_index("col")]).astype(jnp.int32)
    col_flips, row_flips = flips_of(n_col), flips_of(n_row)
    pair, kept = mask(density, cotangent, block_pattern, filter_pattern)

    pair_held = forward([([0], pair[None])], "col", n_col, col_flips)
    row_held = double([([0], pair[:1])], "row", n_row, row_flips)
    pair_held[-1] = (pair_held[-1][0], settle(pair_held[-1][1]))
    both, masked_cols = square_step(here, pair, kept, row_held, pair_held)

    both_held = forward([([0], both[None])], "col", n_col, col_flips)
    late_held = forward([([0], jnp.stack([both[1], pair[1]])[None])], "row", n_row, row_flips[:-1])
    late_held = double(late_held, "row", n_row, row_flips[-1:])
    purified, back = purify_step(here, both, kept, masked_cols, both_held)
    return purified, gradient_step(here, kept, back, late_held, pair_held, both_held)


def solution(mesh):
    placed = (P("row", "col"), P("row", "col"), P("row", "col"), P("row", "col"))

    def local(*arrays):
        return on_device(mesh.shape["row"], mesh.shape["col"], *arrays)

    return jax.shard_map(
        local,
        mesh=mesh,
        in_specs=placed,
        out_specs=(P("row", "col"), P("row", "col")),
        check_vma=False,
    )
```

```python
import jax
import jax.numpy as jnp
from jax import lax
from jax.experimental import pallas as pl
from jax.experimental.pallas import tpu as pltpu
from jax.sharding import PartitionSpec as P

IN_HBM = pl.BlockSpec(memory_space=pltpu.HBM)
IN_VMEM = pl.BlockSpec(memory_space=pltpu.VMEM)
IN_SMEM = pl.BlockSpec(memory_space=pltpu.SMEM)
LIMIT = pltpu.CompilerParams(vmem_limit_bytes=32 * 1024 * 1024)
EARLY = pl.CostEstimate(flops=6_000_000_000, bytes_accessed=0, transcendentals=0)


def dot(a, b):
    return jnp.dot(a, b, preferred_element_type=jnp.float32)


def mask(density, cotangent, block_pattern, filter_pattern):
    height, width = density.shape
    block_size = height // block_pattern.shape[0]

    def kernel(*refs):
        pattern_refs, dense_refs = refs[:2], refs[2:4]
        pair_ref, kept_ref, pattern_held, dense_held, sems = refs[4:]
        copies = []
        for k in range(2):
            copies.append(pltpu.make_async_copy(pattern_refs[k], pattern_held.at[k], sems.at[k]))
            copies.append(pltpu.make_async_copy(dense_refs[k], dense_held.at[k], sems.at[2 + k]))
        for copy in copies:
            copy.start()
        for copy in copies:
            copy.wait()
        lane = lax.broadcasted_iota(jnp.int32, (block_size, width), 1) // block_size
        for k in range(2):
            for i in range(height // block_size):
                rows = pl.ds(i * block_size, block_size)
                kept = jnp.zeros((block_size, width), jnp.float32)
                for j in range(width // block_size):
                    kept = jnp.where(lane == j, pattern_held[k, i, j].astype(jnp.float32), kept)
                kept_ref[k, rows, :] = kept
                pair_ref[k, rows, :] = (dense_held[k, rows, :].astype(jnp.float32) * kept).astype(pair_ref.dtype)

    inputs = (block_pattern, filter_pattern, density, cotangent)
    return pl.pallas_call(
        kernel,
        out_shape=(
            pltpu.VMEM((2, height, width), density.dtype),
            pltpu.VMEM((2, height, width), jnp.float32),
        ),
        in_specs=[IN_HBM] * 4,
        out_specs=(IN_VMEM, IN_VMEM),
        scratch_shapes=[
            pltpu.SMEM((2,) + block_pattern.shape, jnp.int32),
            pltpu.VMEM((2, height, width), density.dtype),
            pltpu.SemaphoreType.DMA((4,)),
        ],
        compiler_params=LIMIT,
        name="mask",
    )(*(pltpu.with_memory_space_constraint(x, pltpu.HBM) for x in inputs))


def settle(block):
    def kernel(block_ref, out_ref):
        out_ref[...] = block_ref[...]

    return pl.pallas_call(
        kernel,
        out_shape=pltpu.VMEM(block.shape, block.dtype),
        in_specs=[IN_VMEM],
        out_specs=IN_VMEM,
        cost_estimate=EARLY,
        compiler_params=LIMIT,
        name="settle",
    )(block)


def flips_of(size):
    flips = []
    while 2 ** len(flips) < size:
        flips.insert(0, 2 ** len(flips))
    return flips


def swap(held, axis_name, size, flips):
    return [
        ([at ^ flip for at in ats], lax.ppermute(blocks, axis_name, [(i, i ^ flip) for i in range(size)]))
        for flip in flips
        for ats, blocks in held
    ]


def double(held, axis_name, size, flips):
    for flip in flips:
        ats = [at for entry in held for at in entry[0]]
        blocks = held[0][1] if len(held) == 1 else jnp.concatenate([entry[1] for entry in held])
        held = held + swap([(ats, blocks)], axis_name, size, [flip])
    return held


def forward(held, axis_name, size, flips):
    held = double(held, axis_name, size, flips[:-2])
    far = swap(held, axis_name, size, flips[-2:-1])
    near = swap(held, axis_name, size, flips[-1:])
    return held + far + near + swap(far, axis_name, size, flips[-1:])


def pieces_of(held, refs):
    for (ats, _), ref in zip(held, refs):
        for k, at in enumerate(ats):
            yield at, ref.at[k]


def part(ref, owner, size):
    return ref.at[pl.ds(pl.multiple_of(owner * size, size), size), :]


def square_step(here, pair, kept, row_held, col_held):
    _, height, width = pair.shape
    n_row = sum(len(ats) for ats, _ in row_held)
    n_in = len(row_held) + len(col_held)

    def kernel(here_ref, pair_ref, kept_ref, *refs):
        row_refs, col_refs = refs[:len(row_held)], refs[len(row_held):n_in]
        both_ref, cols_ref = refs[n_in:]
        for at, block in pieces_of(row_held, row_refs):
            part(cols_ref, here_ref[0] ^ at, height)[...] = block[...]
        total = jnp.zeros((2 * height, width), jnp.float32)
        for at, piece in pieces_of(col_held, col_refs):
            rows = piece[...].reshape(2 * height, width)
            total = total + dot(rows, part(cols_ref, here_ref[1] ^ at, width)[...])
        both_ref[0] = (total[:height] * kept_ref[1]).astype(both_ref.dtype)
        grad = 3.0 * pair_ref[1].astype(jnp.float32) - 2.0 * total[height:]
        both_ref[1] = (grad * kept_ref[1]).astype(both_ref.dtype)

    return pl.pallas_call(
        kernel,
        out_shape=(
            pltpu.VMEM((2, height, width), pair.dtype),
            pltpu.VMEM((n_row * height, width), pair.dtype),
        ),
        in_specs=[IN_SMEM] + [IN_VMEM] * (2 + n_in),
        out_specs=(IN_VMEM, IN_VMEM),
        compiler_params=LIMIT,
        name="square_step",
    )(here, pair, kept, *(blocks for _, blocks in row_held + col_held))


def purify_step(here, both, kept, masked_cols, both_held):
    _, height, width = both.shape

    def kernel(here_ref, both_ref, kept_ref, masked_ref, *refs):
        both_refs, (purified_ref, back_ref) = refs[:-2], refs[-2:]
        total = jnp.zeros((2 * height, width), jnp.float32)
        for at, piece in pieces_of(both_held, both_refs):
            rows = piece[...].reshape(2 * height, width)
            total = total + dot(rows, part(masked_ref, here_ref[1] ^ at, width)[...])
        cubic = total[:height] * kept_ref[1]
        purified_ref[...] = (3.0 * both_ref[0].astype(jnp.float32) - 2.0 * cubic).astype(purified_ref.dtype)
        back_ref[...] = total[height:]

    return pl.pallas_call(
        kernel,
        out_shape=(
            jax.ShapeDtypeStruct((height, width), both.dtype),
            pltpu.VMEM((height, width), jnp.float32),
        ),
        in_specs=[IN_SMEM] + [IN_VMEM] * (3 + len(both_held)),
        out_specs=(IN_VMEM, IN_VMEM),
        cost_estimate=EARLY,
        compiler_params=LIMIT,
        name="purify_step",
    )(here, both, kept, masked_cols, *(blocks for _, blocks in both_held))


def gradient_step(here, kept, back, late_held, pair_held, both_held):
    height, width = back.shape
    n_row = sum(len(ats) for ats, _ in late_held)
    cuts = [len(late_held), len(late_held) + len(pair_held), len(late_held) + len(pair_held) + len(both_held)]

    def kernel(here_ref, kept_ref, back_ref, *refs):
        late_refs, pair_refs, both_refs = refs[:cuts[0]], refs[cuts[0]:cuts[1]], refs[cuts[1]:cuts[2]]
        gradient_ref, late_cols = refs[cuts[2]:]
        for at, block in pieces_of(late_held, late_refs):
            for k in range(2):
                part(late_cols.at[k], here_ref[0] ^ at, height)[...] = block[k]
        summed = back_ref[...]
        for at, piece in pieces_of(pair_held, pair_refs):
            summed = summed + dot(piece[0], part(late_cols.at[0], here_ref[1] ^ at, width)[...])
        with_cotangent = jnp.zeros((height, width), jnp.float32)
        for at, piece in pieces_of(both_held, both_refs):
            with_cotangent = with_cotangent + dot(piece[0], part(late_cols.at[1], here_ref[1] ^ at, width)[...])
        summed = summed - 2.0 * with_cotangent
        gradient_ref[...] = (summed * kept_ref[0]).astype(gradient_ref.dtype)

    return pl.pallas_call(
        kernel,
        out_shape=jax.ShapeDtypeStruct((height, width), late_held[0][1].dtype),
        in_specs=[IN_SMEM] + [IN_VMEM] * (2 + cuts[2]),
        out_specs=IN_VMEM,
        scratch_shapes=[pltpu.VMEM((2, n_row * height, width), late_held[0][1].dtype)],
        compiler_params=LIMIT,
        name="gradient_step",
    )(here, kept, back, *(blocks for _, blocks in late_held + pair_held + both_held))


def on_device(n_row, n_col, density, cotangent, block_pattern, filter_pattern):
    here = jnp.stack([lax.axis_index("row"), lax.axis_index("col")]).astype(jnp.int32)
    col_flips, row_flips = flips_of(n_col), flips_of(n_row)
    pair, kept = mask(density, cotangent, block_pattern, filter_pattern)

    pair_held = forward([([0], pair[None])], "col", n_col, col_flips)
    row_held = double([([0], pair[:1])], "row", n_row, row_flips)
    pair_held[-1] = (pair_held[-1][0], settle(pair_held[-1][1]))
    both, masked_cols = square_step(here, pair, kept, row_held, pair_held)

    both_held = forward([([0], both[None])], "col", n_col, col_flips)
    late_held = forward([([0], jnp.stack([both[1], pair[1]])[None])], "row", n_row, row_flips[:-1])
    late_held = double(late_held, "row", n_row, row_flips[-1:])
    purified, back = purify_step(here, both, kept, masked_cols, both_held)
    return purified, gradient_step(here, kept, back, late_held, pair_held, both_held)


def solution(mesh):
    placed = (P("row", "col"), P("row", "col"), P("row", "col"), P("row", "col"))

    def local(*arrays):
        return on_device(mesh.shape["row"], mesh.shape["col"], *arrays)

    return jax.shard_map(
        local,
        mesh=mesh,
        in_specs=placed,
        out_specs=(P("row", "col"), P("row", "col")),
        check_vma=False,
    )
```

```python
import jax
import jax.numpy as jnp
from jax import lax
from jax.experimental import pallas as pl
from jax.experimental.pallas import tpu as pltpu
from jax.sharding import PartitionSpec as P

IN_HBM = pl.BlockSpec(memory_space=pltpu.HBM)
IN_VMEM = pl.BlockSpec(memory_space=pltpu.VMEM)
IN_SMEM = pl.BlockSpec(memory_space=pltpu.SMEM)
LIMIT = pltpu.CompilerParams(vmem_limit_bytes=32 * 1024 * 1024)
EARLY = pl.CostEstimate(flops=6_000_000_000, bytes_accessed=0, transcendentals=0)


def dot(a, b):
    return jnp.dot(a, b, preferred_element_type=jnp.float32)


def mask(density, cotangent, block_pattern, filter_pattern):
    height, width = density.shape
    block_size = height // block_pattern.shape[0]

    def kernel(*refs):
        pattern_refs, dense_refs = refs[:2], refs[2:4]
        pair_ref, kept_ref, pattern_held, dense_held, sems = refs[4:]
        copies = []
        for k in range(2):
            copies.append(pltpu.make_async_copy(pattern_refs[k], pattern_held.at[k], sems.at[k]))
            copies.append(pltpu.make_async_copy(dense_refs[k], dense_held.at[k], sems.at[2 + k]))
        for copy in copies:
            copy.start()
        for copy in copies:
            copy.wait()
        lane = lax.broadcasted_iota(jnp.int32, (block_size, width), 1) // block_size
        for k in range(2):
            for i in range(height // block_size):
                rows = pl.ds(i * block_size, block_size)
                kept = jnp.zeros((block_size, width), jnp.float32)
                for j in range(width // block_size):
                    kept = jnp.where(lane == j, pattern_held[k, i, j].astype(jnp.float32), kept)
                kept_ref[k, rows, :] = kept
                pair_ref[k, rows, :] = (dense_held[k, rows, :].astype(jnp.float32) * kept).astype(pair_ref.dtype)

    inputs = (block_pattern, filter_pattern, density, cotangent)
    return pl.pallas_call(
        kernel,
        out_shape=(
            pltpu.VMEM((2, height, width), density.dtype),
            pltpu.VMEM((2, height, width), jnp.float32),
        ),
        in_specs=[IN_HBM] * 4,
        out_specs=(IN_VMEM, IN_VMEM),
        scratch_shapes=[
            pltpu.SMEM((2,) + block_pattern.shape, jnp.int32),
            pltpu.VMEM((2, height, width), density.dtype),
            pltpu.SemaphoreType.DMA((4,)),
        ],
        compiler_params=LIMIT,
        name="mask",
    )(*(pltpu.with_memory_space_constraint(x, pltpu.HBM) for x in inputs))


def settle(block):
    def kernel(block_ref, out_ref):
        out_ref[...] = block_ref[...]

    return pl.pallas_call(
        kernel,
        out_shape=pltpu.VMEM(block.shape, block.dtype),
        in_specs=[IN_VMEM],
        out_specs=IN_VMEM,
        cost_estimate=EARLY,
        compiler_params=LIMIT,
        name="settle",
    )(block)


def flips_of(size):
    flips = []
    while 2 ** len(flips) < size:
        flips.insert(0, 2 ** len(flips))
    return flips


def swap(held, axis_name, size, flips):
    return [
        ([at ^ flip for at in ats], lax.ppermute(blocks, axis_name, [(i, i ^ flip) for i in range(size)]))
        for flip in flips
        for ats, blocks in held
    ]


def double(held, axis_name, size, flips):
    for flip in flips:
        ats = [at for entry in held for at in entry[0]]
        blocks = held[0][1] if len(held) == 1 else jnp.concatenate([entry[1] for entry in held])
        held = held + swap([(ats, blocks)], axis_name, size, [flip])
    return held


def forward(held, axis_name, size, flips):
    held = double(held, axis_name, size, flips[:-2])
    far = swap(held, axis_name, size, flips[-2:-1])
    near = swap(held, axis_name, size, flips[-1:])
    return held + far + near + swap(far, axis_name, size, flips[-1:])


def ring(pair, axis_name, size):
    def shift(block, by):
        return lax.ppermute(block, axis_name, [(i, (i + by) % size) for i in range(size)])

    held = [(0, ((pair, 0), (pair, 1)))]
    up, down = pair, pair
    for step in range(1, size // 2 + 1):
        if 2 * step < size:
            up, down = shift(up, 1), shift(down, -1)
            held.append((size - step, ((up, 0), (up, 1))))
            held.append((step, ((down, 0), (down, 1))))
        elif size > 2:
            held.append((step, ((shift(down[:1], -1), 0), (shift(up[1:], 1), 0))))
        else:
            up = shift(pair, 1)
            held.append((step, ((up, 0), (up, 1))))
    return held


def pieces_of(held, refs):
    for (ats, _), ref in zip(held, refs):
        for k, at in enumerate(ats):
            yield at, ref.at[k]


def part(ref, owner, size):
    return ref.at[pl.ds(pl.multiple_of(owner * size, size), size), :]


def settle(block):
    def kernel(block_ref, out_ref):
        out_ref[...] = block_ref[...]

    return pl.pallas_call(
        kernel,
        out_shape=pltpu.VMEM(block.shape, block.dtype),
        in_specs=[IN_VMEM],
        out_specs=IN_VMEM,
        cost_estimate=EARLY,
        compiler_params=LIMIT,
        name="settle",
    )(block)


def call(kernel, name, here, fixed, helds, rings, out_shape, scratch=(), hint=None):
    arrays = [here, *fixed]
    for held in helds:
        arrays += [blocks for _, blocks in held]
    places = {}
    for entry in (entry for held in rings for entry in held):
        for array, _ in entry[1]:
            if id(array) not in places:
                places[id(array)] = len(arrays)
                arrays.append(array)

    def body(*refs):
        fixed_refs, at, lists = refs[1:1 + len(fixed)], 1 + len(fixed), []
        for held in helds:
            lists.append(refs[at:at + len(held)])
            at += len(held)
        ring_refs = [
            [(distance, [refs[places[id(array)]].at[k] for array, k in blocks]) for distance, blocks in held]
            for held in rings
        ]
        kernel(refs[0], fixed_refs, lists, ring_refs, refs[len(arrays):])

    return pl.pallas_call(
        body,
        out_shape=out_shape,
        in_specs=[IN_SMEM] + [IN_VMEM] * (len(arrays) - 1),
        out_specs=jax.tree.map(lambda _: IN_VMEM, out_shape),
        scratch_shapes=scratch,
        cost_estimate=hint,
        compiler_params=LIMIT,
        name=name,
    )(*arrays)


def product(pieces, which, cols_ref, here_col, n_col):
    width = cols_ref.shape[-1]
    total = None
    for distance, blocks in pieces:
        owner = lax.rem(here_col + distance, n_col)
        term = dot(blocks[which][...], part(cols_ref, owner, width)[...])
        total = term if total is None else total + term
    return total


def square_step(here, n_col, pair, kept, row_held, pair_ring):
    _, height, width = pair.shape
    n_row = sum(len(ats) for ats, _ in row_held)

    def kernel(here_ref, fixed, lists, rings, outs):
        pair_ref, kept_ref = fixed
        both_ref, cols_ref = outs
        for at, block in pieces_of(row_held, lists[0]):
            part(cols_ref, here_ref[0] ^ at, height)[...] = block[...]
        square = product(rings[0], 0, cols_ref, here_ref[1], n_col)
        both_ref[0] = (square * kept_ref[1]).astype(both_ref.dtype)
        back = product(rings[0], 1, cols_ref, here_ref[1], n_col)
        grad = 3.0 * pair_ref[1].astype(jnp.float32) - 2.0 * back
        both_ref[1] = (grad * kept_ref[1]).astype(both_ref.dtype)

    out = (
        pltpu.VMEM((2, height, width), pair.dtype),
        pltpu.VMEM((n_row * height, width), pair.dtype),
    )
    return call(kernel, "square_step", here, (pair, kept), (row_held,), (pair_ring,), out)


def purify_step(here, n_col, both, kept, masked_cols, both_ring):
    _, height, width = both.shape

    def kernel(here_ref, fixed, lists, rings, outs):
        both_ref, kept_ref, cols_ref = fixed
        purified_ref, back_ref = outs
        cubic = product(rings[0], 0, cols_ref, here_ref[1], n_col) * kept_ref[1]
        purified_ref[...] = (3.0 * both_ref[0].astype(jnp.float32) - 2.0 * cubic).astype(purified_ref.dtype)
        back_ref[...] = product(rings[0], 1, cols_ref, here_ref[1], n_col)

    out = (pltpu.VMEM((height, width), both.dtype), pltpu.VMEM((height, width), jnp.float32))
    return call(kernel, "purify_step", here, (both, kept, masked_cols), (), (both_ring,), out, hint=EARLY)


def last_step(here, n_col, kept, purified, back, late_held, pair_ring, both_ring):
    height, width = back.shape
    n_row = sum(len(ats) for ats, _ in late_held)

    def kernel(here_ref, fixed, lists, rings, outs):
        kept_ref, purified_ref, back_ref = fixed
        out_ref, gradient_ref, late_cols = outs
        out_ref[...] = purified_ref[...]
        for at, block in pieces_of(late_held, lists[0]):
            for k in range(2):
                part(late_cols.at[k], here_ref[0] ^ at, height)[...] = block[k]
        summed = back_ref[...] + product(rings[0], 0, late_cols.at[0], here_ref[1], n_col)
        summed = summed - 2.0 * product(rings[1], 0, late_cols.at[1], here_ref[1], n_col)
        gradient_ref[...] = (summed * kept_ref[0]).astype(gradient_ref.dtype)

    out = jax.ShapeDtypeStruct((height, width), purified.dtype)
    scratch = [pltpu.VMEM((2, n_row * height, width), purified.dtype)]
    fixed = (kept, purified, back)
    return call(kernel, "last_step", here, fixed, (late_held,), (pair_ring, both_ring), (out, out), scratch)


def on_device(n_row, n_col, density, cotangent, block_pattern, filter_pattern):
    here = jnp.stack([lax.axis_index("row"), lax.axis_index("col")]).astype(jnp.int32)
    chip_flips, core_flips = flips_of(n_row)[:-1], flips_of(n_row)[-1:]
    pair, kept = mask(density, cotangent, block_pattern, filter_pattern)

    pair_ring = ring(pair, "col", n_col)
    row_held = double([([0], pair[:1])], "row", n_row, chip_flips)
    row_held = double(row_held, "row", n_row, core_flips)
    (far, ((first, at), second)) = pair_ring[-1]
    pair_ring[-1] = (far, ((settle(first), at), second))
    both, masked_cols = square_step(here, n_col, pair, kept, row_held, pair_ring)

    both_ring = ring(both, "col", n_col)
    late_held = forward([([0], jnp.stack([both[1], pair[1]])[None])], "row", n_row, chip_flips)
    late_held = double(late_held, "row", n_row, core_flips)
    purified, back = purify_step(here, n_col, both, kept, masked_cols, both_ring)
    return last_step(here, n_col, kept, purified, back, late_held, pair_ring, both_ring)


def solution(mesh):
    placed = (P("row", "col"), P("row", "col"), P("row", "col"), P("row", "col"))

    def local(*arrays):
        return on_device(mesh.shape["row"], mesh.shape["col"], *arrays)

    return jax.shard_map(
        local,
        mesh=mesh,
        in_specs=placed,
        out_specs=(P("row", "col"), P("row", "col")),
        check_vma=False,
    )
```

```python
import jax
import jax.numpy as jnp
from jax import lax
from jax.experimental import pallas as pl
from jax.experimental.pallas import tpu as pltpu
from jax.sharding import PartitionSpec as P

IN_HBM = pl.BlockSpec(memory_space=pltpu.HBM)
IN_VMEM = pl.BlockSpec(memory_space=pltpu.VMEM)
IN_SMEM = pl.BlockSpec(memory_space=pltpu.SMEM)
LIMIT = pltpu.CompilerParams(vmem_limit_bytes=32 * 1024 * 1024)
EARLY = pl.CostEstimate(flops=6_000_000_000, bytes_accessed=0, transcendentals=0)


def dot(a, b):
    return jnp.dot(a, b, preferred_element_type=jnp.float32)


def mask(density, cotangent, block_pattern, filter_pattern):
    height, width = density.shape
    block_size = height // block_pattern.shape[0]

    def kernel(*refs):
        pattern_refs, dense_refs = refs[:2], refs[2:4]
        pair_ref, kept_ref, pattern_held, dense_held, sems = refs[4:]
        copies = []
        for k in range(2):
            copies.append(pltpu.make_async_copy(pattern_refs[k], pattern_held.at[k], sems.at[k]))
            copies.append(pltpu.make_async_copy(dense_refs[k], dense_held.at[k], sems.at[2 + k]))
        for copy in copies:
            copy.start()
        for copy in copies:
            copy.wait()
        lane = lax.broadcasted_iota(jnp.int32, (block_size, width), 1) // block_size
        for k in range(2):
            for i in range(height // block_size):
                rows = pl.ds(i * block_size, block_size)
                kept = jnp.zeros((block_size, width), jnp.float32)
                for j in range(width // block_size):
                    kept = jnp.where(lane == j, pattern_held[k, i, j].astype(jnp.float32), kept)
                kept_ref[k, rows, :] = kept
                pair_ref[k, rows, :] = (dense_held[k, rows, :].astype(jnp.float32) * kept).astype(pair_ref.dtype)

    inputs = (block_pattern, filter_pattern, density, cotangent)
    return pl.pallas_call(
        kernel,
        out_shape=(
            pltpu.VMEM((2, height, width), density.dtype),
            pltpu.VMEM((2, height, width), jnp.float32),
        ),
        in_specs=[IN_HBM] * 4,
        out_specs=(IN_VMEM, IN_VMEM),
        scratch_shapes=[
            pltpu.SMEM((2,) + block_pattern.shape, jnp.int32),
            pltpu.VMEM((2, height, width), density.dtype),
            pltpu.SemaphoreType.DMA((4,)),
        ],
        compiler_params=LIMIT,
        name="mask",
    )(*(pltpu.with_memory_space_constraint(x, pltpu.HBM) for x in inputs))


def settle(block):
    def kernel(block_ref, out_ref):
        out_ref[...] = block_ref[...]

    return pl.pallas_call(
        kernel,
        out_shape=pltpu.VMEM(block.shape, block.dtype),
        in_specs=[IN_VMEM],
        out_specs=IN_VMEM,
        cost_estimate=EARLY,
        compiler_params=LIMIT,
        name="settle",
    )(block)


def flips_of(size):
    flips = []
    while 2 ** len(flips) < size:
        flips.insert(0, 2 ** len(flips))
    return flips


def swap(held, axis_name, size, flips):
    return [
        ([at ^ flip for at in ats], lax.ppermute(blocks, axis_name, [(i, i ^ flip) for i in range(size)]))
        for flip in flips
        for ats, blocks in held
    ]


def double(held, axis_name, size, flips):
    for flip in flips:
        ats = [at for entry in held for at in entry[0]]
        blocks = held[0][1] if len(held) == 1 else jnp.concatenate([entry[1] for entry in held])
        held = held + swap([(ats, blocks)], axis_name, size, [flip])
    return held


def forward(held, axis_name, size, flips):
    held = double(held, axis_name, size, flips[:-2])
    far = swap(held, axis_name, size, flips[-2:-1])
    near = swap(held, axis_name, size, flips[-1:])
    return held + far + near + swap(far, axis_name, size, flips[-1:])


def exchange(pair, axis_name, size):
    flips = flips_of(size)
    held = double([([0], pair[None])], axis_name, size, flips[:-2])
    far = swap(held, axis_name, size, flips[-2:-1])
    near = swap(held, axis_name, size, flips[-1:])
    if far and near:
        (far_pairs, near_pairs) = lax.optimization_barrier((far[0][1], near[0][1]))
        far, near = [(far[0][0], far_pairs)], [(near[0][0], near_pairs)]
    held = held + far + near + swap(far, axis_name, size, flips[-1:])
    return [(at, ((pairs, (k, 0)), (pairs, (k, 1)))) for ats, pairs in held for k, at in enumerate(ats)]


def pieces_of(held, refs):
    for (ats, _), ref in zip(held, refs):
        for k, at in enumerate(ats):
            yield at, ref.at[k]


def part(ref, owner, size):
    return ref.at[pl.ds(pl.multiple_of(owner * size, size), size), :]


def settle(block):
    def kernel(block_ref, out_ref):
        out_ref[...] = block_ref[...]

    return pl.pallas_call(
        kernel,
        out_shape=pltpu.VMEM(block.shape, block.dtype),
        in_specs=[IN_VMEM],
        out_specs=IN_VMEM,
        cost_estimate=EARLY,
        compiler_params=LIMIT,
        name="settle",
    )(block)


def call(kernel, name, here, fixed, helds, cols, out_shape, scratch=(), hint=None):
    arrays = [here, *fixed]
    for held in helds:
        arrays += [blocks for _, blocks in held]
    places = {}
    for entry in (entry for held in cols for entry in held):
        for array, _ in entry[1]:
            if id(array) not in places:
                places[id(array)] = len(arrays)
                arrays.append(array)

    def body(*refs):
        fixed_refs, start, lists = refs[1:1 + len(fixed)], 1 + len(fixed), []
        for held in helds:
            lists.append(refs[start:start + len(held)])
            start += len(held)
        col_refs = [
            [(at, [refs[places[id(array)]].at[k] for array, k in blocks]) for at, blocks in held]
            for held in cols
        ]
        kernel(refs[0], fixed_refs, lists, col_refs, refs[len(arrays):])

    return pl.pallas_call(
        body,
        out_shape=out_shape,
        in_specs=[IN_SMEM] + [IN_VMEM] * (len(arrays) - 1),
        out_specs=jax.tree.map(lambda _: IN_VMEM, out_shape),
        scratch_shapes=scratch,
        cost_estimate=hint,
        compiler_params=LIMIT,
        name=name,
    )(*arrays)


def product(pieces, which, cols_ref, here_col):
    width = cols_ref.shape[-1]
    total = None
    for at, blocks in pieces:
        owner = here_col ^ at
        term = dot(blocks[which][...], part(cols_ref, owner, width)[...])
        total = term if total is None else total + term
    return total


def square_step(here, pair, kept, row_held, pair_held):
    _, height, width = pair.shape
    n_row = sum(len(ats) for ats, _ in row_held)

    def kernel(here_ref, fixed, lists, cols, outs):
        pair_ref, kept_ref = fixed
        both_ref, cols_ref = outs
        for at, block in pieces_of(row_held, lists[0]):
            part(cols_ref, here_ref[0] ^ at, height)[...] = block[...]
        square = product(cols[0], 0, cols_ref, here_ref[1])
        both_ref[0] = (square * kept_ref[1]).astype(both_ref.dtype)
        back = product(cols[0], 1, cols_ref, here_ref[1])
        grad = 3.0 * pair_ref[1].astype(jnp.float32) - 2.0 * back
        both_ref[1] = (grad * kept_ref[1]).astype(both_ref.dtype)

    out = (
        pltpu.VMEM((2, height, width), pair.dtype),
        pltpu.VMEM((n_row * height, width), pair.dtype),
    )
    return call(kernel, "square_step", here, (pair, kept), (row_held,), (pair_held,), out)


def purify_step(here, both, kept, masked_cols, both_held):
    _, height, width = both.shape

    def kernel(here_ref, fixed, lists, cols, outs):
        both_ref, kept_ref, cols_ref = fixed
        purified_ref, back_ref = outs
        cubic = product(cols[0], 0, cols_ref, here_ref[1]) * kept_ref[1]
        purified_ref[...] = (3.0 * both_ref[0].astype(jnp.float32) - 2.0 * cubic).astype(purified_ref.dtype)
        back_ref[...] = product(cols[0], 1, cols_ref, here_ref[1])

    out = (pltpu.VMEM((height, width), both.dtype), pltpu.VMEM((height, width), jnp.float32))
    return call(kernel, "purify_step", here, (both, kept, masked_cols), (), (both_held,), out, hint=EARLY)


def last_step(here, kept, purified, back, late_held, pair_held, both_held):
    height, width = back.shape
    n_row = sum(len(ats) for ats, _ in late_held)

    def kernel(here_ref, fixed, lists, cols, outs):
        kept_ref, purified_ref, back_ref = fixed
        out_ref, gradient_ref, late_cols = outs
        out_ref[...] = purified_ref[...]
        for at, block in pieces_of(late_held, lists[0]):
            for k in range(2):
                part(late_cols.at[k], here_ref[0] ^ at, height)[...] = block[k]
        summed = back_ref[...] + product(cols[0], 0, late_cols.at[0], here_ref[1])
        summed = summed - 2.0 * product(cols[1], 0, late_cols.at[1], here_ref[1])
        gradient_ref[...] = (summed * kept_ref[0]).astype(gradient_ref.dtype)

    out = jax.ShapeDtypeStruct((height, width), purified.dtype)
    scratch = [pltpu.VMEM((2, n_row * height, width), purified.dtype)]
    fixed = (kept, purified, back)
    return call(kernel, "last_step", here, fixed, (late_held,), (pair_held, both_held), (out, out), scratch)


def on_device(n_row, n_col, density, cotangent, block_pattern, filter_pattern):
    here = jnp.stack([lax.axis_index("row"), lax.axis_index("col")]).astype(jnp.int32)
    chip_flips, core_flips = flips_of(n_row)[:-1], flips_of(n_row)[-1:]
    pair, kept = mask(density, cotangent, block_pattern, filter_pattern)

    pair_held = exchange(pair, "col", n_col)
    row_held = forward([([0], pair[:1])], "row", n_row, chip_flips)
    row_held = double(row_held, "row", n_row, core_flips)
    at, ((pairs, _), _) = pair_held[-1]
    pairs = settle(pairs)
    pair_held[-1] = (at, ((pairs, (0, 0)), (pairs, (0, 1))))
    both, masked_cols = square_step(here, pair, kept, row_held, pair_held)

    both_held = exchange(both, "col", n_col)
    late_held = forward([([0], jnp.stack([both[1], pair[1]])[None])], "row", n_row, chip_flips)
    late_held = double(late_held, "row", n_row, core_flips)
    purified, back = purify_step(here, both, kept, masked_cols, both_held)
    return last_step(here, kept, purified, back, late_held, pair_held, both_held)


def solution(mesh):
    placed = (P("row", "col"), P("row", "col"), P("row", "col"), P("row", "col"))

    def local(*arrays):
        return on_device(mesh.shape["row"], mesh.shape["col"], *arrays)

    return jax.shard_map(
        local,
        mesh=mesh,
        in_specs=placed,
        out_specs=(P("row", "col"), P("row", "col")),
        check_vma=False,
    )
```

```python
import jax
import jax.numpy as jnp
from jax import lax
from jax.experimental import pallas as pl
from jax.experimental.pallas import tpu as pltpu
from jax.sharding import PartitionSpec as P

IN_HBM = pl.BlockSpec(memory_space=pltpu.HBM)
IN_VMEM = pl.BlockSpec(memory_space=pltpu.VMEM)
IN_SMEM = pl.BlockSpec(memory_space=pltpu.SMEM)
LIMIT = pltpu.CompilerParams(vmem_limit_bytes=32 * 1024 * 1024)
EARLY = pl.CostEstimate(flops=6_000_000_000, bytes_accessed=0, transcendentals=0)


def dot(a, b):
    return jnp.dot(a, b, preferred_element_type=jnp.float32)


def mask(density, cotangent, block_pattern, filter_pattern):
    height, width = density.shape
    block_size = height // block_pattern.shape[0]

    def kernel(*refs):
        pattern_refs, dense_refs = refs[:2], refs[2:4]
        pair_ref, kept_ref, pattern_held, dense_held, sems = refs[4:]
        copies = []
        for k in range(2):
            copies.append(pltpu.make_async_copy(pattern_refs[k], pattern_held.at[k], sems.at[k]))
            copies.append(pltpu.make_async_copy(dense_refs[k], dense_held.at[k], sems.at[2 + k]))
        for copy in copies:
            copy.start()
        for copy in copies:
            copy.wait()
        lane = lax.broadcasted_iota(jnp.int32, (block_size, width), 1) // block_size
        for k in range(2):
            for i in range(height // block_size):
                rows = pl.ds(i * block_size, block_size)
                kept = jnp.zeros((block_size, width), jnp.float32)
                for j in range(width // block_size):
                    kept = jnp.where(lane == j, pattern_held[k, i, j].astype(jnp.float32), kept)
                kept_ref[k, rows, :] = kept
                pair_ref[k, rows, :] = (dense_held[k, rows, :].astype(jnp.float32) * kept).astype(pair_ref.dtype)

    inputs = (block_pattern, filter_pattern, density, cotangent)
    return pl.pallas_call(
        kernel,
        out_shape=(
            pltpu.VMEM((2, height, width), density.dtype),
            pltpu.VMEM((2, height, width), jnp.float32),
        ),
        in_specs=[IN_HBM] * 4,
        out_specs=(IN_VMEM, IN_VMEM),
        scratch_shapes=[
            pltpu.SMEM((2,) + block_pattern.shape, jnp.int32),
            pltpu.VMEM((2, height, width), density.dtype),
            pltpu.SemaphoreType.DMA((4,)),
        ],
        compiler_params=LIMIT,
        name="mask",
    )(*(pltpu.with_memory_space_constraint(x, pltpu.HBM) for x in inputs))


def settle(block):
    def kernel(block_ref, out_ref):
        out_ref[...] = block_ref[...]

    return pl.pallas_call(
        kernel,
        out_shape=pltpu.VMEM(block.shape, block.dtype),
        in_specs=[IN_VMEM],
        out_specs=IN_VMEM,
        cost_estimate=EARLY,
        compiler_params=LIMIT,
        name="settle",
    )(block)


def flips_of(size):
    flips = []
    while 2 ** len(flips) < size:
        flips.insert(0, 2 ** len(flips))
    return flips


def swap(held, axis_name, size, flips):
    return [
        ([at ^ flip for at in ats], lax.ppermute(blocks, axis_name, [(i, i ^ flip) for i in range(size)]))
        for flip in flips
        for ats, blocks in held
    ]


def double(held, axis_name, size, flips):
    for flip in flips:
        ats = [at for entry in held for at in entry[0]]
        blocks = held[0][1] if len(held) == 1 else jnp.concatenate([entry[1] for entry in held])
        held = held + swap([(ats, blocks)], axis_name, size, [flip])
    return held


def forward(held, axis_name, size, flips):
    held = double(held, axis_name, size, flips[:-2])
    far = swap(held, axis_name, size, flips[-2:-1])
    near = swap(held, axis_name, size, flips[-1:])
    return held + far + near + swap(far, axis_name, size, flips[-1:])


def tie(helds):
    arrays = lax.optimization_barrier([[blocks for _, blocks in held] for held in helds])
    return [[(ats, block) for (ats, _), block in zip(held, blocks)] for held, blocks in zip(helds, arrays)]


def exchange(pair, block, n_row, n_col, later=()):
    col_flips, row_flips = flips_of(n_col), flips_of(n_row)
    pairs = double([([0], pair[None])], "col", n_col, col_flips[:-2])
    blocks = [([0], block)]
    far = swap(pairs, "col", n_col, col_flips[-2:-1])
    near = swap(pairs, "col", n_col, col_flips[-1:])
    first = swap(blocks, "row", n_row, row_flips[:1])
    far, near, first, later = tie([far, near, first, later])
    blocks = double(blocks + first, "row", n_row, row_flips[1:])
    pairs = pairs + far + near + swap(far, "col", n_col, col_flips[-1:])
    places = [(at, ((array, (k, 0)), (array, (k, 1)))) for ats, array in pairs for k, at in enumerate(ats)]
    return places, blocks, later


def pieces_of(held, refs):
    for (ats, _), ref in zip(held, refs):
        for k, at in enumerate(ats):
            yield at, ref.at[k]


def part(ref, owner, size):
    return ref.at[pl.ds(pl.multiple_of(owner * size, size), size), :]


def settle(block):
    def kernel(block_ref, out_ref):
        out_ref[...] = block_ref[...]

    return pl.pallas_call(
        kernel,
        out_shape=pltpu.VMEM(block.shape, block.dtype),
        in_specs=[IN_VMEM],
        out_specs=IN_VMEM,
        cost_estimate=EARLY,
        compiler_params=LIMIT,
        name="settle",
    )(block)


def call(kernel, name, here, fixed, helds, cols, out_shape, scratch=(), hint=None):
    arrays = [here, *fixed]
    for held in helds:
        arrays += [blocks for _, blocks in held]
    places = {}
    for entry in (entry for held in cols for entry in held):
        for array, _ in entry[1]:
            if id(array) not in places:
                places[id(array)] = len(arrays)
                arrays.append(array)

    def body(*refs):
        fixed_refs, start, lists = refs[1:1 + len(fixed)], 1 + len(fixed), []
        for held in helds:
            lists.append(refs[start:start + len(held)])
            start += len(held)
        col_refs = [
            [(at, [refs[places[id(array)]].at[k] for array, k in blocks]) for at, blocks in held]
            for held in cols
        ]
        kernel(refs[0], fixed_refs, lists, col_refs, refs[len(arrays):])

    return pl.pallas_call(
        body,
        out_shape=out_shape,
        in_specs=[IN_SMEM] + [IN_VMEM] * (len(arrays) - 1),
        out_specs=jax.tree.map(lambda _: IN_VMEM, out_shape),
        scratch_shapes=scratch,
        cost_estimate=hint,
        compiler_params=LIMIT,
        name=name,
    )(*arrays)


def product(pieces, which, cols_ref, here_col):
    width = cols_ref.shape[-1]
    total = None
    for at, blocks in pieces:
        owner = here_col ^ at
        term = dot(blocks[which][...], part(cols_ref, owner, width)[...])
        total = term if total is None else total + term
    return total


def fill(cols_ref, held, refs, here_row):
    height = held[0][1].shape[-2]
    for at, block in pieces_of(held, refs):
        part(cols_ref, here_row ^ at, height)[...] = block[...]


def square_step(here, pair, kept, row_held, pair_held):
    _, height, width = pair.shape
    n_row = sum(len(ats) for ats, _ in row_held)

    def kernel(here_ref, fixed, lists, cols, outs):
        pair_ref, kept_ref = fixed
        both_ref, masked_ref = outs
        fill(masked_ref, row_held, lists[0], here_ref[0])
        square = product(cols[0], 0, masked_ref, here_ref[1])
        both_ref[0] = (square * kept_ref[1]).astype(both_ref.dtype)
        back = product(cols[0], 1, masked_ref, here_ref[1])
        grad = 3.0 * pair_ref[1].astype(jnp.float32) - 2.0 * back
        both_ref[1] = (grad * kept_ref[1]).astype(both_ref.dtype)

    out = (
        pltpu.VMEM((2, height, width), pair.dtype),
        pltpu.VMEM((n_row * height, width), pair.dtype),
    )
    return call(kernel, "square_step", here, (pair, kept), (row_held,), (pair_held,), out)


def purify_step(here, both, kept, masked_cols, filtered_held, both_held):
    _, height, width = both.shape

    def kernel(here_ref, fixed, lists, cols, outs):
        both_ref, kept_ref, masked_ref = fixed
        purified_ref, total_ref, filtered_cols = outs
        fill(filtered_cols, filtered_held, lists[0], here_ref[0])
        cubic = product(cols[0], 0, masked_ref, here_ref[1]) * kept_ref[1]
        purified_ref[...] = (3.0 * both_ref[0].astype(jnp.float32) - 2.0 * cubic).astype(purified_ref.dtype)
        total = product(cols[0], 1, masked_ref, here_ref[1])
        total_ref[...] = total - 2.0 * product(cols[0], 0, filtered_cols, here_ref[1])

    out = (pltpu.VMEM((height, width), both.dtype), pltpu.VMEM((height, width), jnp.float32))
    scratch = [pltpu.VMEM(masked_cols.shape, masked_cols.dtype)]
    fixed = (both, kept, masked_cols)
    return call(kernel, "purify_step", here, fixed, (filtered_held,), (both_held,), out, scratch, hint=EARLY)


def last_step(here, kept, purified, total, row_held, pair_held):
    height, width = total.shape
    n_row = sum(len(ats) for ats, _ in row_held)

    def kernel(here_ref, fixed, lists, cols, outs):
        kept_ref, purified_ref, total_ref = fixed
        out_ref, gradient_ref, grad_cols = outs
        out_ref[...] = purified_ref[...]
        fill(grad_cols, row_held, lists[0], here_ref[0])
        summed = total_ref[...] + product(cols[0], 0, grad_cols, here_ref[1])
        gradient_ref[...] = (summed * kept_ref[0]).astype(gradient_ref.dtype)

    out = jax.ShapeDtypeStruct((height, width), purified.dtype)
    scratch = [pltpu.VMEM((n_row * height, width), purified.dtype)]
    fixed = (kept, purified, total)
    return call(kernel, "last_step", here, fixed, (row_held,), (pair_held,), (out, out), scratch)


def on_device(n_row, n_col, density, cotangent, block_pattern, filter_pattern):
    here = jnp.stack([lax.axis_index("row"), lax.axis_index("col")]).astype(jnp.int32)
    pair, kept = mask(density, cotangent, block_pattern, filter_pattern)

    pair_held, row_held, filtered = exchange(pair, pair[:1], n_row, n_col, [([0], pair[1:])])
    at, ((pairs, _), _) = pair_held[-1]
    pairs = settle(pairs)
    pair_held[-1] = (at, ((pairs, (0, 0)), (pairs, (0, 1))))
    both, masked_cols = square_step(here, pair, kept, row_held, pair_held)

    filtered_held = double(filtered, "row", n_row, flips_of(n_row))
    both_held, grad_held, _ = exchange(both, both[1:], n_row, n_col)
    at, ((pairs, _), _) = both_held[-1]
    pairs = settle(pairs)
    both_held[-1] = (at, ((pairs, (0, 0)), (pairs, (0, 1))))
    purified, total = purify_step(here, both, kept, masked_cols, filtered_held, both_held)
    return last_step(here, kept, purified, total, grad_held, pair_held)


def solution(mesh):
    placed = (P("row", "col"), P("row", "col"), P("row", "col"), P("row", "col"))

    def local(*arrays):
        return on_device(mesh.shape["row"], mesh.shape["col"], *arrays)

    return jax.shard_map(
        local,
        mesh=mesh,
        in_specs=placed,
        out_specs=(P("row", "col"), P("row", "col")),
        check_vma=False,
    )
```

```python
import jax
import jax.numpy as jnp
from jax import lax
from jax.experimental import pallas as pl
from jax.experimental.pallas import tpu as pltpu
from jax.sharding import PartitionSpec as P

IN_HBM = pl.BlockSpec(memory_space=pltpu.HBM)
IN_VMEM = pl.BlockSpec(memory_space=pltpu.VMEM)
IN_SMEM = pl.BlockSpec(memory_space=pltpu.SMEM)
LIMIT = pltpu.CompilerParams(vmem_limit_bytes=32 * 1024 * 1024)
EARLY = pl.CostEstimate(flops=6_000_000_000, bytes_accessed=0, transcendentals=0)


def dot(a, b):
    return jnp.dot(a, b, preferred_element_type=jnp.float32)


def mask(density, cotangent, block_pattern, filter_pattern):
    height, width = density.shape
    block_size = height // block_pattern.shape[0]

    def kernel(*refs):
        pattern_refs, dense_refs = refs[:2], refs[2:4]
        pair_ref, kept_ref, pattern_held, dense_held, sems = refs[4:]
        copies = []
        for k in range(2):
            copies.append(pltpu.make_async_copy(pattern_refs[k], pattern_held.at[k], sems.at[k]))
            copies.append(pltpu.make_async_copy(dense_refs[k], dense_held.at[k], sems.at[2 + k]))
        for copy in copies:
            copy.start()
        for copy in copies:
            copy.wait()
        lane = lax.broadcasted_iota(jnp.int32, (block_size, width), 1) // block_size
        for k in range(2):
            for i in range(height // block_size):
                rows = pl.ds(i * block_size, block_size)
                kept = jnp.zeros((block_size, width), jnp.float32)
                for j in range(width // block_size):
                    kept = jnp.where(lane == j, pattern_held[k, i, j].astype(jnp.float32), kept)
                kept_ref[k, rows, :] = kept
                pair_ref[k, rows, :] = (dense_held[k, rows, :].astype(jnp.float32) * kept).astype(pair_ref.dtype)

    inputs = (block_pattern, filter_pattern, density, cotangent)
    return pl.pallas_call(
        kernel,
        out_shape=(
            pltpu.VMEM((2, height, width), density.dtype),
            pltpu.VMEM((2, height, width), jnp.float32),
        ),
        in_specs=[IN_HBM] * 4,
        out_specs=(IN_VMEM, IN_VMEM),
        scratch_shapes=[
            pltpu.SMEM((2,) + block_pattern.shape, jnp.int32),
            pltpu.VMEM((2, height, width), density.dtype),
            pltpu.SemaphoreType.DMA((4,)),
        ],
        compiler_params=LIMIT,
        name="mask",
    )(*(pltpu.with_memory_space_constraint(x, pltpu.HBM) for x in inputs))


def settle(block):
    def kernel(block_ref, out_ref):
        out_ref[...] = block_ref[...]

    return pl.pallas_call(
        kernel,
        out_shape=pltpu.VMEM(block.shape, block.dtype),
        in_specs=[IN_VMEM],
        out_specs=IN_VMEM,
        cost_estimate=EARLY,
        compiler_params=LIMIT,
        name="settle",
    )(block)


def flips_of(size):
    flips = []
    while 2 ** len(flips) < size:
        flips.insert(0, 2 ** len(flips))
    return flips


def swap(held, axis_name, size, flips):
    return [
        ([at ^ flip for at in ats], lax.ppermute(blocks, axis_name, [(i, i ^ flip) for i in range(size)]))
        for flip in flips
        for ats, blocks in held
    ]


def double(held, axis_name, size, flips):
    for flip in flips:
        ats = [at for entry in held for at in entry[0]]
        blocks = held[0][1] if len(held) == 1 else jnp.concatenate([entry[1] for entry in held])
        held = held + swap([(ats, blocks)], axis_name, size, [flip])
    return held


def forward(held, axis_name, size, flips):
    held = double(held, axis_name, size, flips[:-2])
    far = swap(held, axis_name, size, flips[-2:-1])
    near = swap(held, axis_name, size, flips[-1:])
    return held + far + near + swap(far, axis_name, size, flips[-1:])


def tie(helds):
    arrays = lax.optimization_barrier([[blocks for _, blocks in held] for held in helds])
    return [[(ats, block) for (ats, _), block in zip(held, blocks)] for held, blocks in zip(helds, arrays)]


def exchange(pair, axis_name, size, settled):
    flips = flips_of(size)
    held = double([([0], pair[None])], axis_name, size, flips[:-2])
    far = swap(held, axis_name, size, flips[-2:-1])
    near = swap(held, axis_name, size, flips[-1:])
    near, far = tie([near, far])
    last = swap(far, axis_name, size, flips[-1:])
    if settled:
        last = [(ats, settle(pairs)) for ats, pairs in last]
    held = held + far + near + last
    return [(at, ((pairs, (k, 0)), (pairs, (k, 1)))) for ats, pairs in held for k, at in enumerate(ats)]


def pieces_of(held, refs):
    for (ats, _), ref in zip(held, refs):
        for k, at in enumerate(ats):
            yield at, ref.at[k]


def part(ref, owner, size):
    return ref.at[pl.ds(pl.multiple_of(owner * size, size), size), :]


def settle(block):
    def kernel(block_ref, out_ref):
        out_ref[...] = block_ref[...]

    return pl.pallas_call(
        kernel,
        out_shape=pltpu.VMEM(block.shape, block.dtype),
        in_specs=[IN_VMEM],
        out_specs=IN_VMEM,
        cost_estimate=EARLY,
        compiler_params=LIMIT,
        name="settle",
    )(block)


def call(kernel, name, here, fixed, helds, cols, out_shape, scratch=(), hint=None):
    arrays = [here, *fixed]
    for held in helds:
        arrays += [blocks for _, blocks in held]
    places = {}
    for entry in (entry for held in cols for entry in held):
        for array, _ in entry[1]:
            if id(array) not in places:
                places[id(array)] = len(arrays)
                arrays.append(array)

    def body(*refs):
        fixed_refs, start, lists = refs[1:1 + len(fixed)], 1 + len(fixed), []
        for held in helds:
            lists.append(refs[start:start + len(held)])
            start += len(held)
        col_refs = [
            [(at, [refs[places[id(array)]].at[k] for array, k in blocks]) for at, blocks in held]
            for held in cols
        ]
        kernel(refs[0], fixed_refs, lists, col_refs, refs[len(arrays):])

    return pl.pallas_call(
        body,
        out_shape=out_shape,
        in_specs=[IN_SMEM] + [IN_VMEM] * (len(arrays) - 1),
        out_specs=jax.tree.map(lambda _: IN_VMEM, out_shape),
        scratch_shapes=scratch,
        cost_estimate=hint,
        compiler_params=LIMIT,
        name=name,
    )(*arrays)


def fill_rows(rows_ref, pieces, here_col):
    height, width = rows_ref.shape[0] // 2, rows_ref.shape[1] // len(pieces)
    for at, blocks in pieces:
        columns = pl.ds(pl.multiple_of((here_col ^ at) * width, width), width)
        for k in range(2):
            rows_ref[k * height:(k + 1) * height, columns] = blocks[k][...]


def square_step(here, pair, kept, row_held, pair_held):
    _, height, width = pair.shape
    n_row = sum(len(ats) for ats, _ in row_held)

    def kernel(here_ref, fixed, lists, cols, outs):
        pair_ref, kept_ref = fixed
        both_ref, masked_ref, rows_ref = outs
        fill_rows(rows_ref, cols[0], here_ref[1])
        for at, block in pieces_of(row_held, lists[0]):
            part(masked_ref, here_ref[0] ^ at, height)[...] = block[...]
        total = dot(rows_ref[...], masked_ref[...])
        both_ref[0] = (total[:height] * kept_ref[1]).astype(both_ref.dtype)
        grad = 3.0 * pair_ref[1].astype(jnp.float32) - 2.0 * total[height:]
        both_ref[1] = (grad * kept_ref[1]).astype(both_ref.dtype)

    out = (
        pltpu.VMEM((2, height, width), pair.dtype),
        pltpu.VMEM((n_row * height, width), pair.dtype),
        pltpu.VMEM((2 * height, len(pair_held) * width), pair.dtype),
    )
    return call(kernel, "square_step", here, (pair, kept), (row_held,), (pair_held,), out)


def purify_step(here, both, kept, masked_cols, both_held):
    _, height, width = both.shape

    def kernel(here_ref, fixed, lists, cols, outs):
        both_ref, kept_ref, masked_ref = fixed
        purified_ref, back_ref, scaled_ref, rows_ref = outs
        fill_rows(rows_ref, cols[0], here_ref[1])
        total = dot(rows_ref[...], masked_ref[...])
        cubic = total[:height] * kept_ref[1]
        purified_ref[...] = (3.0 * both_ref[0].astype(jnp.float32) - 2.0 * cubic).astype(purified_ref.dtype)
        back_ref[...] = total[height:]
        scaled_ref[...] = (-2.0 * rows_ref[:height].astype(jnp.float32)).astype(scaled_ref.dtype)

    rows = (2 * height, len(both_held) * width)
    out = (
        pltpu.VMEM((height, width), both.dtype),
        pltpu.VMEM((height, width), jnp.float32),
        pltpu.VMEM((height, rows[1]), both.dtype),
    )
    scratch = [pltpu.VMEM(rows, both.dtype)]
    return call(kernel, "purify_step", here, (both, kept, masked_cols), (), (both_held,), out, scratch, hint=EARLY)


def last_step(here, kept, purified, back, pair_rows, scaled_rows, late_held):
    height, width = back.shape
    n_row = sum(len(ats) for ats, _ in late_held)

    def kernel(here_ref, fixed, lists, cols, outs):
        kept_ref, purified_ref, back_ref, pair_ref, scaled_ref = fixed
        out_ref, gradient_ref, late_cols = outs
        out_ref[...] = purified_ref[...]
        for at, block in pieces_of(late_held, lists[0]):
            for k in range(2):
                part(late_cols.at[k], here_ref[0] ^ at, height)[...] = block[k]
        summed = back_ref[...] + dot(pair_ref[:height], late_cols[0])
        summed = summed + dot(scaled_ref[...], late_cols[1])
        gradient_ref[...] = (summed * kept_ref[0]).astype(gradient_ref.dtype)

    out = jax.ShapeDtypeStruct((height, width), purified.dtype)
    scratch = [pltpu.VMEM((2, n_row * height, width), purified.dtype)]
    fixed = (kept, purified, back, pair_rows, scaled_rows)
    return call(kernel, "last_step", here, fixed, (late_held,), (), (out, out), scratch)


def on_device(n_row, n_col, density, cotangent, block_pattern, filter_pattern):
    here = jnp.stack([lax.axis_index("row"), lax.axis_index("col")]).astype(jnp.int32)
    chip_flips, core_flips = flips_of(n_row)[:-1], flips_of(n_row)[-1:]
    pair, kept = mask(density, cotangent, block_pattern, filter_pattern)

    pair_held = exchange(pair, "col", n_col, True)
    row_held = forward([([0], pair[:1])], "row", n_row, chip_flips)
    row_held = double(row_held, "row", n_row, core_flips)
    both, masked_cols, pair_rows = square_step(here, pair, kept, row_held, pair_held)

    both_held = exchange(both, "col", n_col, False)
    late_held = forward([([0], jnp.stack([both[1], pair[1]])[None])], "row", n_row, chip_flips)
    late_held = double(late_held, "row", n_row, core_flips)
    purified, back, scaled_rows = purify_step(here, both, kept, masked_cols, both_held)
    return last_step(here, kept, purified, back, pair_rows, scaled_rows, late_held)


def solution(mesh):
    placed = (P("row", "col"), P("row", "col"), P("row", "col"), P("row", "col"))

    def local(*arrays):
        return on_device(mesh.shape["row"], mesh.shape["col"], *arrays)

    return jax.shard_map(
        local,
        mesh=mesh,
        in_specs=placed,
        out_specs=(P("row", "col"), P("row", "col")),
        check_vma=False,
    )
```

```python
import jax
import jax.numpy as jnp
from jax import lax
from jax.experimental import pallas as pl
from jax.experimental.pallas import tpu as pltpu
from jax.sharding import PartitionSpec as P

IN_HBM = pl.BlockSpec(memory_space=pltpu.HBM)
IN_VMEM = pl.BlockSpec(memory_space=pltpu.VMEM)
LIMIT = pltpu.CompilerParams(vmem_limit_bytes=32 * 1024 * 1024)
EARLY = pl.CostEstimate(flops=6_000_000_000, bytes_accessed=0, transcendentals=0)


def dot(a, b):
    return jnp.dot(a, b, preferred_element_type=jnp.float32)


def mask(density, cotangent, block_pattern, filter_pattern):
    height, width = density.shape
    block_size = height // block_pattern.shape[0]

    def kernel(*refs):
        pattern_refs, dense_refs = refs[:2], refs[2:4]
        pair_ref, kept_ref, pattern_held, dense_held, sems = refs[4:]
        copies = []
        for k in range(2):
            copies.append(pltpu.make_async_copy(pattern_refs[k], pattern_held.at[k], sems.at[k]))
            copies.append(pltpu.make_async_copy(dense_refs[k], dense_held.at[k], sems.at[2 + k]))
        for copy in copies:
            copy.start()
        for copy in copies:
            copy.wait()
        lane = lax.broadcasted_iota(jnp.int32, (block_size, width), 1) // block_size
        for k in range(2):
            for i in range(height // block_size):
                rows = pl.ds(i * block_size, block_size)
                kept = jnp.zeros((block_size, width), jnp.float32)
                for j in range(width // block_size):
                    kept = jnp.where(lane == j, pattern_held[k, i, j].astype(jnp.float32), kept)
                kept_ref[k, rows, :] = kept
                pair_ref[k, rows, :] = (dense_held[k, rows, :].astype(jnp.float32) * kept).astype(pair_ref.dtype)

    inputs = (block_pattern, filter_pattern, density, cotangent)
    return pl.pallas_call(
        kernel,
        out_shape=(
            pltpu.VMEM((2, height, width), density.dtype),
            pltpu.VMEM((2, height, width), jnp.float32),
        ),
        in_specs=[IN_HBM] * 4,
        out_specs=(IN_VMEM, IN_VMEM),
        scratch_shapes=[
            pltpu.SMEM((2,) + block_pattern.shape, jnp.int32),
            pltpu.VMEM((2, height, width), density.dtype),
            pltpu.SemaphoreType.DMA((4,)),
        ],
        compiler_params=LIMIT,
        name="mask",
    )(*(pltpu.with_memory_space_constraint(x, pltpu.HBM) for x in inputs))


def settle(block):
    def kernel(block_ref, out_ref):
        out_ref[...] = block_ref[...]

    return pl.pallas_call(
        kernel,
        out_shape=pltpu.VMEM(block.shape, block.dtype),
        in_specs=[IN_VMEM],
        out_specs=IN_VMEM,
        cost_estimate=EARLY,
        compiler_params=LIMIT,
        name="settle",
    )(block)


def flips_of(size):
    flips = []
    while 2 ** len(flips) < size:
        flips.insert(0, 2 ** len(flips))
    return flips


def swap(held, axis_name, size, flips):
    return [
        ([at ^ flip for at in ats], lax.ppermute(blocks, axis_name, [(i, i ^ flip) for i in range(size)]))
        for flip in flips
        for ats, blocks in held
    ]


def double(held, axis_name, size, flips):
    for flip in flips:
        ats = [at for entry in held for at in entry[0]]
        blocks = held[0][1] if len(held) == 1 else jnp.concatenate([entry[1] for entry in held])
        held = held + swap([(ats, blocks)], axis_name, size, [flip])
    return held


def forward(held, axis_name, size, flips):
    held = double(held, axis_name, size, flips[:-2])
    far = swap(held, axis_name, size, flips[-2:-1])
    near = swap(held, axis_name, size, flips[-1:])
    return held + far + near + swap(far, axis_name, size, flips[-1:])


def tie(helds):
    arrays = lax.optimization_barrier([[blocks for _, blocks in held] for held in helds])
    return [[(ats, block) for (ats, _), block in zip(held, blocks)] for held, blocks in zip(helds, arrays)]


def exchange(pair, axis_name, size, settled):
    flips = flips_of(size)
    held = double([([0], pair[None])], axis_name, size, flips[:-2])
    far = swap(held, axis_name, size, flips[-2:-1])
    near = swap(held, axis_name, size, flips[-1:])
    near, far = tie([near, far])
    last = swap(far, axis_name, size, flips[-1:])
    if settled:
        last = [(ats, settle(pairs)) for ats, pairs in last]
    held = held + far + near + last
    return [(at, ((pairs, (k, 0)), (pairs, (k, 1)))) for ats, pairs in held for k, at in enumerate(ats)]


def pieces_of(held, refs):
    for (ats, _), ref in zip(held, refs):
        for k, at in enumerate(ats):
            yield at, ref.at[k]


def part(ref, owner, size):
    return ref.at[pl.ds(pl.multiple_of(owner * size, size), size), :]


def settle(block):
    def kernel(block_ref, out_ref):
        out_ref[...] = block_ref[...]

    return pl.pallas_call(
        kernel,
        out_shape=pltpu.VMEM(block.shape, block.dtype),
        in_specs=[IN_VMEM],
        out_specs=IN_VMEM,
        cost_estimate=EARLY,
        compiler_params=LIMIT,
        name="settle",
    )(block)


def call(kernel, name, fixed, helds, cols, out_shape, scratch=(), hint=None):
    arrays = [*fixed]
    for held in helds:
        arrays += [blocks for _, blocks in held]
    places = {}
    for entry in (entry for held in cols for entry in held):
        for array, _ in entry[1]:
            if id(array) not in places:
                places[id(array)] = len(arrays)
                arrays.append(array)

    def body(*refs):
        fixed_refs, start, lists = refs[:len(fixed)], len(fixed), []
        for held in helds:
            lists.append(refs[start:start + len(held)])
            start += len(held)
        col_refs = [
            [(at, [refs[places[id(array)]].at[k] for array, k in blocks]) for at, blocks in held]
            for held in cols
        ]
        here = (lax.axis_index("row"), lax.axis_index("col"))
        kernel(here, fixed_refs, lists, col_refs, refs[len(arrays):])

    return pl.pallas_call(
        body,
        out_shape=out_shape,
        in_specs=[IN_VMEM] * len(arrays),
        out_specs=jax.tree.map(lambda _: IN_VMEM, out_shape),
        scratch_shapes=scratch,
        cost_estimate=hint,
        compiler_params=LIMIT,
        name=name,
    )(*arrays)


def fill_rows(rows_ref, pieces, here_col):
    height, width = rows_ref.shape[0] // 2, rows_ref.shape[1] // len(pieces)
    for at, blocks in pieces:
        columns = pl.ds(pl.multiple_of((here_col ^ at) * width, width), width)
        for k in range(2):
            rows_ref[k * height:(k + 1) * height, columns] = blocks[k][...]


def square_step(pair, kept, row_held, pair_held):
    _, height, width = pair.shape
    n_row = sum(len(ats) for ats, _ in row_held)

    def kernel(here, fixed, lists, cols, outs):
        pair_ref, kept_ref = fixed
        both_ref, masked_ref, rows_ref = outs
        fill_rows(rows_ref, cols[0], here[1])
        for at, block in pieces_of(row_held, lists[0]):
            part(masked_ref, here[0] ^ at, height)[...] = block[...]
        total = dot(rows_ref[...], masked_ref[...])
        both_ref[0] = (total[:height] * kept_ref[1]).astype(both_ref.dtype)
        grad = 3.0 * pair_ref[1].astype(jnp.float32) - 2.0 * total[height:]
        both_ref[1] = (grad * kept_ref[1]).astype(both_ref.dtype)

    out = (
        pltpu.VMEM((2, height, width), pair.dtype),
        pltpu.VMEM((n_row * height, width), pair.dtype),
        pltpu.VMEM((2 * height, len(pair_held) * width), pair.dtype),
    )
    return call(kernel, "square_step", (pair, kept), (row_held,), (pair_held,), out)


def purify_step(both, kept, masked_cols, both_held):
    _, height, width = both.shape

    def kernel(here, fixed, lists, cols, outs):
        both_ref, kept_ref, masked_ref = fixed
        purified_ref, back_ref, scaled_ref, rows_ref = outs
        fill_rows(rows_ref, cols[0], here[1])
        total = dot(rows_ref[...], masked_ref[...])
        cubic = total[:height] * kept_ref[1]
        purified_ref[...] = (3.0 * both_ref[0].astype(jnp.float32) - 2.0 * cubic).astype(purified_ref.dtype)
        back_ref[...] = total[height:]
        scaled_ref[...] = (-2.0 * rows_ref[:height].astype(jnp.float32)).astype(scaled_ref.dtype)

    rows = (2 * height, len(both_held) * width)
    out = (
        pltpu.VMEM((height, width), both.dtype),
        pltpu.VMEM((height, width), jnp.float32),
        pltpu.VMEM((height, rows[1]), both.dtype),
    )
    scratch = [pltpu.VMEM(rows, both.dtype)]
    return call(kernel, "purify_step", (both, kept, masked_cols), (), (both_held,), out, scratch, hint=EARLY)


def last_step(kept, purified, back, pair_rows, scaled_rows, late_held):
    height, width = back.shape
    n_row = sum(len(ats) for ats, _ in late_held)

    def kernel(here, fixed, lists, cols, outs):
        kept_ref, purified_ref, back_ref, pair_ref, scaled_ref = fixed
        out_ref, gradient_ref, late_cols = outs
        out_ref[...] = purified_ref[...]
        for at, block in pieces_of(late_held, lists[0]):
            for k in range(2):
                part(late_cols.at[k], here[0] ^ at, height)[...] = block[k]
        summed = back_ref[...] + dot(pair_ref[:height], late_cols[0])
        summed = summed + dot(scaled_ref[...], late_cols[1])
        gradient_ref[...] = (summed * kept_ref[0]).astype(gradient_ref.dtype)

    out = jax.ShapeDtypeStruct((height, width), purified.dtype)
    scratch = [pltpu.VMEM((2, n_row * height, width), purified.dtype)]
    fixed = (kept, purified, back, pair_rows, scaled_rows)
    return call(kernel, "last_step", fixed, (late_held,), (), (out, out), scratch)


def on_device(n_row, n_col, density, cotangent, block_pattern, filter_pattern):
    chip_flips, core_flips = flips_of(n_row)[:-1], flips_of(n_row)[-1:]
    pair, kept = mask(density, cotangent, block_pattern, filter_pattern)

    pair_held = exchange(pair, "col", n_col, True)
    row_held = forward([([0], pair[:1])], "row", n_row, chip_flips)
    row_held = double(row_held, "row", n_row, core_flips)
    both, masked_cols, pair_rows = square_step(pair, kept, row_held, pair_held)

    both_held = exchange(both, "col", n_col, False)
    late_held = forward([([0], jnp.stack([both[1], pair[1]])[None])], "row", n_row, chip_flips)
    late_held = double(late_held, "row", n_row, core_flips)
    purified, back, scaled_rows = purify_step(both, kept, masked_cols, both_held)
    return last_step(kept, purified, back, pair_rows, scaled_rows, late_held)


def solution(mesh):
    placed = (P("row", "col"), P("row", "col"), P("row", "col"), P("row", "col"))

    def local(*arrays):
        return on_device(mesh.shape["row"], mesh.shape["col"], *arrays)

    return jax.shard_map(
        local,
        mesh=mesh,
        in_specs=placed,
        out_specs=(P("row", "col"), P("row", "col")),
        check_vma=False,
    )
```

```python
import jax
import jax.numpy as jnp
from jax import lax
from jax.experimental import pallas as pl
from jax.experimental.pallas import tpu as pltpu
from jax.sharding import PartitionSpec as P

IN_HBM = pl.BlockSpec(memory_space=pltpu.HBM)
IN_VMEM = pl.BlockSpec(memory_space=pltpu.VMEM)
LIMIT = pltpu.CompilerParams(vmem_limit_bytes=32 * 1024 * 1024)
EARLY = pl.CostEstimate(flops=6_000_000_000, bytes_accessed=0, transcendentals=0)


def dot(a, b):
    return jnp.dot(a, b, preferred_element_type=jnp.float32)


def mask(density, cotangent, block_pattern, filter_pattern):
    height, width = density.shape
    block_size = height // block_pattern.shape[0]

    def kernel(*refs):
        pattern_refs, dense_refs = refs[:2], refs[2:4]
        pair_ref, kept_ref, pattern_held, dense_held, sems = refs[4:]
        copies = []
        for k in range(2):
            copies.append(pltpu.make_async_copy(pattern_refs[k], pattern_held.at[k], sems.at[k]))
            copies.append(pltpu.make_async_copy(dense_refs[k], dense_held.at[k], sems.at[2 + k]))
        for copy in copies:
            copy.start()
        for copy in copies:
            copy.wait()
        lane = lax.broadcasted_iota(jnp.int32, (block_size, width), 1) // block_size
        for k in range(2):
            for i in range(height // block_size):
                rows = pl.ds(i * block_size, block_size)
                kept = jnp.zeros((block_size, width), jnp.float32)
                for j in range(width // block_size):
                    kept = jnp.where(lane == j, pattern_held[k, i, j].astype(jnp.float32), kept)
                kept_ref[k, rows, :] = kept
                pair_ref[k, rows, :] = (dense_held[k, rows, :].astype(jnp.float32) * kept).astype(pair_ref.dtype)

    inputs = (block_pattern, filter_pattern, density, cotangent)
    return pl.pallas_call(
        kernel,
        out_shape=(
            pltpu.VMEM((2, height, width), density.dtype),
            pltpu.VMEM((2, height, width), jnp.float32),
        ),
        in_specs=[IN_HBM] * 4,
        out_specs=(IN_VMEM, IN_VMEM),
        scratch_shapes=[
            pltpu.SMEM((2,) + block_pattern.shape, jnp.int32),
            pltpu.VMEM((2, height, width), density.dtype),
            pltpu.SemaphoreType.DMA((4,)),
        ],
        compiler_params=LIMIT,
        name="mask",
    )(*(pltpu.with_memory_space_constraint(x, pltpu.HBM) for x in inputs))


def settle(block):
    def kernel(block_ref, out_ref):
        out_ref[...] = block_ref[...]

    return pl.pallas_call(
        kernel,
        out_shape=pltpu.VMEM(block.shape, block.dtype),
        in_specs=[IN_VMEM],
        out_specs=IN_VMEM,
        cost_estimate=EARLY,
        compiler_params=LIMIT,
        name="settle",
    )(block)


def flips_of(size):
    flips = []
    while 2 ** len(flips) < size:
        flips.insert(0, 2 ** len(flips))
    return flips


def swap(held, axis_name, size, flips):
    return [
        ([at ^ flip for at in ats], lax.ppermute(blocks, axis_name, [(i, i ^ flip) for i in range(size)]))
        for flip in flips
        for ats, blocks in held
    ]


def double(held, axis_name, size, flips):
    for flip in flips:
        ats = [at for entry in held for at in entry[0]]
        blocks = held[0][1] if len(held) == 1 else jnp.concatenate([entry[1] for entry in held])
        held = held + swap([(ats, blocks)], axis_name, size, [flip])
    return held


def forward(held, axis_name, size, flips):
    held = double(held, axis_name, size, flips[:-2])
    far = swap(held, axis_name, size, flips[-2:-1])
    near = swap(held, axis_name, size, flips[-1:])
    return held + far + near + swap(far, axis_name, size, flips[-1:])


def tie(helds):
    arrays = lax.optimization_barrier([[blocks for _, blocks in held] for held in helds])
    return [[(ats, block) for (ats, _), block in zip(held, blocks)] for held, blocks in zip(helds, arrays)]


def exchange(pair, axis_name, size, settled):
    flips = flips_of(size)
    held = double([([0], pair[None])], axis_name, size, flips[:-2])
    far = swap(held, axis_name, size, flips[-2:-1])
    near = swap(held, axis_name, size, flips[-1:])
    near, far = tie([near, far])
    last = swap(far, axis_name, size, flips[-1:])
    if settled:
        last = [(ats, settle(pairs)) for ats, pairs in last]
    held = held + far + near + last
    return [(at, ((pairs, (k, 0)), (pairs, (k, 1)))) for ats, pairs in held for k, at in enumerate(ats)]


def part(ref, owner, size):
    return ref.at[pl.ds(pl.multiple_of(owner * size, size), size), :]


def settle(block):
    def kernel(block_ref, out_ref):
        out_ref[...] = block_ref[...]

    return pl.pallas_call(
        kernel,
        out_shape=pltpu.VMEM(block.shape, block.dtype),
        in_specs=[IN_VMEM],
        out_specs=IN_VMEM,
        cost_estimate=EARLY,
        compiler_params=LIMIT,
        name="settle",
    )(block)


def call(kernel, name, fixed, blocks, pairs, out_shape, scratch=(), hint=None):
    arrays, places = [*fixed], {}
    for array, _ in [block for _, block in blocks] + [block for _, two in pairs for block in two]:
        if id(array) not in places:
            places[id(array)] = len(arrays)
            arrays.append(array)

    def body(*refs):
        def ref_of(block):
            return refs[places[id(block[0])]].at[block[1]]

        here = (lax.axis_index("row"), lax.axis_index("col"))
        block_refs = [(at, ref_of(block)) for at, block in blocks]
        pair_refs = [(at, [ref_of(block) for block in two]) for at, two in pairs]
        kernel(here, refs[:len(fixed)], block_refs, pair_refs, refs[len(arrays):])

    return pl.pallas_call(
        body,
        out_shape=out_shape,
        in_specs=[IN_VMEM] * len(arrays),
        out_specs=jax.tree.map(lambda _: IN_VMEM, out_shape),
        scratch_shapes=scratch,
        cost_estimate=hint,
        compiler_params=LIMIT,
        name=name,
    )(*arrays)


def fill_rows(rows_ref, pieces, here_col):
    height, width = rows_ref.shape[0] // 2, rows_ref.shape[1] // len(pieces)
    for at, blocks in pieces:
        columns = pl.ds(pl.multiple_of((here_col ^ at) * width, width), width)
        for k in range(2):
            rows_ref[k * height:(k + 1) * height, columns] = blocks[k][...]


def square_step(pair, kept, masked_blocks, pair_held):
    _, height, width = pair.shape
    n_row = len(masked_blocks)

    def kernel(here, fixed, blocks, pairs, outs):
        pair_ref, kept_ref = fixed
        both_ref, masked_ref, rows_ref = outs
        fill_rows(rows_ref, pairs, here[1])
        for at, block in blocks:
            part(masked_ref, here[0] ^ at, height)[...] = block[...]
        total = dot(rows_ref[...], masked_ref[...])
        both_ref[0] = (total[:height] * kept_ref[1]).astype(both_ref.dtype)
        grad = 3.0 * pair_ref[1].astype(jnp.float32) - 2.0 * total[height:]
        both_ref[1] = (grad * kept_ref[1]).astype(both_ref.dtype)

    out = (
        pltpu.VMEM((2, height, width), pair.dtype),
        pltpu.VMEM((n_row * height, width), pair.dtype),
        pltpu.VMEM((2 * height, len(pair_held) * width), pair.dtype),
    )
    return call(kernel, "square_step", (pair, kept), masked_blocks, pair_held, out)


def purify_step(both, kept, masked_cols, both_held):
    _, height, width = both.shape

    def kernel(here, fixed, blocks, pairs, outs):
        both_ref, kept_ref, masked_ref = fixed
        purified_ref, back_ref, scaled_ref, rows_ref = outs
        fill_rows(rows_ref, pairs, here[1])
        total = dot(rows_ref[...], masked_ref[...])
        cubic = total[:height] * kept_ref[1]
        purified_ref[...] = (3.0 * both_ref[0].astype(jnp.float32) - 2.0 * cubic).astype(purified_ref.dtype)
        back_ref[...] = total[height:]
        scaled_ref[...] = (-2.0 * rows_ref[:height].astype(jnp.float32)).astype(scaled_ref.dtype)

    rows = (2 * height, len(both_held) * width)
    out = (
        pltpu.VMEM((height, width), both.dtype),
        pltpu.VMEM((height, width), jnp.float32),
        pltpu.VMEM((height, rows[1]), both.dtype),
    )
    scratch = [pltpu.VMEM(rows, both.dtype)]
    return call(kernel, "purify_step", (both, kept, masked_cols), [], both_held, out, scratch, hint=EARLY)


def last_step(kept, purified, back, pair_rows, scaled_rows, grad_blocks, filtered_blocks):
    height, width = back.shape
    n_row = len(grad_blocks)

    def kernel(here, fixed, blocks, pairs, outs):
        kept_ref, purified_ref, back_ref, pair_ref, scaled_ref = fixed
        out_ref, gradient_ref, late_cols = outs
        out_ref[...] = purified_ref[...]
        for i, (at, block) in enumerate(blocks):
            part(late_cols.at[i // n_row], here[0] ^ at, height)[...] = block[...]
        summed = back_ref[...] + dot(pair_ref[:height], late_cols[0])
        summed = summed + dot(scaled_ref[...], late_cols[1])
        gradient_ref[...] = (summed * kept_ref[0]).astype(gradient_ref.dtype)

    out = jax.ShapeDtypeStruct((height, width), purified.dtype)
    scratch = [pltpu.VMEM((2, n_row * height, width), purified.dtype)]
    fixed = (kept, purified, back, pair_rows, scaled_rows)
    return call(kernel, "last_step", fixed, grad_blocks + filtered_blocks, [], (out, out), scratch)


def take(held, *inner):
    return [(at, (array, (k,) + inner)) for ats, array in held for k, at in enumerate(ats)]


def cut(held, k):
    return [(ats, array[:, k]) for ats, array in held]


def pairs_of(one, two):
    return [(ats, jnp.stack([first, second], 1)) for (ats, first), (_, second) in zip(one, two)]


def across_cores(lists, n_row):
    ats = [[at for ats, _ in held for at in ats] for held in lists]
    assert all(sorted(a) == sorted(ats[0]) for a in ats)
    flips = flips_of(n_row)[-1:]
    sent = jnp.stack([jnp.concatenate([array for _, array in held]) for held in lists])
    got = [lax.ppermute(sent, "row", [(i, i ^ flip) for i in range(n_row)]) for flip in flips]
    return [
        take(held) + [(at ^ flip, (array, (k, i))) for flip, array in zip(flips, got) for i, at in enumerate(own)]
        for k, (held, own) in enumerate(zip(lists, ats))
    ]


def on_device(n_row, n_col, density, cotangent, block_pattern, filter_pattern):
    chip_flips = flips_of(n_row)[:-1]
    lead, first, second = chip_flips[:-2], chip_flips[-2:-1], chip_flips[-1:]
    pair, kept = mask(density, cotangent, block_pattern, filter_pattern)

    pair_held = exchange(pair, "col", n_col, True)
    own = double([([0], pair[None])], "row", n_row, lead)
    masked = cut(own, 0)
    far = swap(masked, "row", n_row, first)
    near = swap(own, "row", n_row, second)
    masked = masked + far + cut(near, 0) + swap(far, "row", n_row, second)
    (masked_blocks,) = across_cores([masked], n_row)
    both, masked_cols, pair_rows = square_step(pair, kept, masked_blocks, pair_held)

    both_held = exchange(both, "col", n_col, False)
    grad = double([([0], both[1:])], "row", n_row, lead)
    far = swap(grad, "row", n_row, second)
    left = swap(pairs_of(grad, cut(own, 1)), "row", n_row, first)
    right = swap(pairs_of(far, cut(near, 1)), "row", n_row, first)
    grad = grad + far + cut(left, 0) + cut(right, 0)
    filtered = cut(own, 1) + cut(near, 1) + cut(left, 1) + cut(right, 1)
    grad_blocks, filtered_blocks = across_cores([grad, filtered], n_row)
    purified, back, scaled_rows = purify_step(both, kept, masked_cols, both_held)
    return last_step(kept, purified, back, pair_rows, scaled_rows, grad_blocks, filtered_blocks)


def solution(mesh):
    placed = (P("row", "col"), P("row", "col"), P("row", "col"), P("row", "col"))

    def local(*arrays):
        return on_device(mesh.shape["row"], mesh.shape["col"], *arrays)

    return jax.shard_map(
        local,
        mesh=mesh,
        in_specs=placed,
        out_specs=(P("row", "col"), P("row", "col")),
        check_vma=False,
    )
```

```python
import jax
import jax.numpy as jnp
from jax import lax
from jax.experimental import pallas as pl
from jax.experimental.pallas import tpu as pltpu
from jax.sharding import PartitionSpec as P

IN_HBM = pl.BlockSpec(memory_space=pltpu.HBM)
IN_VMEM = pl.BlockSpec(memory_space=pltpu.VMEM)
LIMIT = pltpu.CompilerParams(vmem_limit_bytes=32 * 1024 * 1024)
EARLY = pl.CostEstimate(flops=6_000_000_000, bytes_accessed=0, transcendentals=0)


def dot(a, b):
    return jnp.dot(a, b, preferred_element_type=jnp.float32)


def mask(density, cotangent, block_pattern, filter_pattern):
    height, width = density.shape
    block_size = height // block_pattern.shape[0]

    def kernel(*refs):
        pattern_refs, dense_refs = refs[:2], refs[2:4]
        pair_ref, kept_ref, pattern_held, dense_held, sems = refs[4:]
        copies = []
        for k in range(2):
            copies.append(pltpu.make_async_copy(pattern_refs[k], pattern_held.at[k], sems.at[k]))
            copies.append(pltpu.make_async_copy(dense_refs[k], dense_held.at[k], sems.at[2 + k]))
        for copy in copies:
            copy.start()
        for copy in copies:
            copy.wait()
        lane = lax.broadcasted_iota(jnp.int32, (block_size, width), 1) // block_size
        for k in range(2):
            for i in range(height // block_size):
                rows = pl.ds(i * block_size, block_size)
                kept = jnp.zeros((block_size, width), jnp.float32)
                for j in range(width // block_size):
                    kept = jnp.where(lane == j, pattern_held[k, i, j].astype(jnp.float32), kept)
                kept_ref[k, rows, :] = kept
                pair_ref[k, rows, :] = (dense_held[k, rows, :].astype(jnp.float32) * kept).astype(pair_ref.dtype)

    inputs = (block_pattern, filter_pattern, density, cotangent)
    return pl.pallas_call(
        kernel,
        out_shape=(
            pltpu.VMEM((2, height, width), density.dtype),
            pltpu.VMEM((2, height, width), jnp.float32),
        ),
        in_specs=[IN_HBM] * 4,
        out_specs=(IN_VMEM, IN_VMEM),
        scratch_shapes=[
            pltpu.SMEM((2,) + block_pattern.shape, jnp.int32),
            pltpu.VMEM((2, height, width), density.dtype),
            pltpu.SemaphoreType.DMA((4,)),
        ],
        compiler_params=LIMIT,
        name="mask",
    )(*(pltpu.with_memory_space_constraint(x, pltpu.HBM) for x in inputs))


def settle(block):
    def kernel(block_ref, out_ref):
        out_ref[...] = block_ref[...]

    return pl.pallas_call(
        kernel,
        out_shape=pltpu.VMEM(block.shape, block.dtype),
        in_specs=[IN_VMEM],
        out_specs=IN_VMEM,
        cost_estimate=EARLY,
        compiler_params=LIMIT,
        name="settle",
    )(block)


def flips_of(size):
    flips = []
    while 2 ** len(flips) < size:
        flips.insert(0, 2 ** len(flips))
    return flips


def pairs_across(size, flip):
    order = range(size) if flip.bit_length() % 2 == 0 else reversed(range(size))
    return [(i, i ^ flip) for i in order]


def swap(held, axis_name, size, flips):
    return [
        ([at ^ flip for at in ats], lax.ppermute(blocks, axis_name, pairs_across(size, flip)))
        for flip in flips
        for ats, blocks in held
    ]


def double(held, axis_name, size, flips):
    for flip in flips:
        ats = [at for entry in held for at in entry[0]]
        blocks = held[0][1] if len(held) == 1 else jnp.concatenate([entry[1] for entry in held])
        held = held + swap([(ats, blocks)], axis_name, size, [flip])
    return held


def forward(held, axis_name, size, flips):
    held = double(held, axis_name, size, flips[:-2])
    far = swap(held, axis_name, size, flips[-2:-1])
    near = swap(held, axis_name, size, flips[-1:])
    return held + far + near + swap(far, axis_name, size, flips[-1:])


def tie(helds):
    arrays = lax.optimization_barrier([[blocks for _, blocks in held] for held in helds])
    return [[(ats, block) for (ats, _), block in zip(held, blocks)] for held, blocks in zip(helds, arrays)]


def exchange(pair, axis_name, size, settled):
    flips = flips_of(size)
    held = double([([0], pair[None])], axis_name, size, flips[:-2])
    far = swap(held, axis_name, size, flips[-2:-1])
    near = swap(held, axis_name, size, flips[-1:])
    near, far = tie([near, far])
    last = swap(far, axis_name, size, flips[-1:])
    if settled:
        last = [(ats, settle(pairs)) for ats, pairs in last]
    held = held + far + near + last
    return [(at, ((pairs, (k, 0)), (pairs, (k, 1)))) for ats, pairs in held for k, at in enumerate(ats)]


def pieces_of(held, refs):
    for (ats, _), ref in zip(held, refs):
        for k, at in enumerate(ats):
            yield at, ref.at[k]


def part(ref, owner, size):
    return ref.at[pl.ds(pl.multiple_of(owner * size, size), size), :]


def settle(block):
    def kernel(block_ref, out_ref):
        out_ref[...] = block_ref[...]

    return pl.pallas_call(
        kernel,
        out_shape=pltpu.VMEM(block.shape, block.dtype),
        in_specs=[IN_VMEM],
        out_specs=IN_VMEM,
        cost_estimate=EARLY,
        compiler_params=LIMIT,
        name="settle",
    )(block)


def call(kernel, name, fixed, helds, cols, out_shape, scratch=(), hint=None):
    arrays = [*fixed]
    for held in helds:
        arrays += [blocks for _, blocks in held]
    places = {}
    for entry in (entry for held in cols for entry in held):
        for array, _ in entry[1]:
            if id(array) not in places:
                places[id(array)] = len(arrays)
                arrays.append(array)

    def body(*refs):
        fixed_refs, start, lists = refs[:len(fixed)], len(fixed), []
        for held in helds:
            lists.append(refs[start:start + len(held)])
            start += len(held)
        col_refs = [
            [(at, [refs[places[id(array)]].at[k] for array, k in blocks]) for at, blocks in held]
            for held in cols
        ]
        here = (lax.axis_index("row"), lax.axis_index("col"))
        kernel(here, fixed_refs, lists, col_refs, refs[len(arrays):])

    return pl.pallas_call(
        body,
        out_shape=out_shape,
        in_specs=[IN_VMEM] * len(arrays),
        out_specs=jax.tree.map(lambda _: IN_VMEM, out_shape),
        scratch_shapes=scratch,
        cost_estimate=hint,
        compiler_params=LIMIT,
        name=name,
    )(*arrays)


def fill_rows(rows_ref, pieces, here_col):
    height, width = rows_ref.shape[0] // 2, rows_ref.shape[1] // len(pieces)
    for at, blocks in pieces:
        columns = pl.ds(pl.multiple_of((here_col ^ at) * width, width), width)
        for k in range(2):
            rows_ref[k * height:(k + 1) * height, columns] = blocks[k][...]


def square_step(pair, kept, row_held, pair_held):
    _, height, width = pair.shape
    n_row = sum(len(ats) for ats, _ in row_held)

    def kernel(here, fixed, lists, cols, outs):
        pair_ref, kept_ref = fixed
        both_ref, masked_ref, rows_ref = outs
        fill_rows(rows_ref, cols[0], here[1])
        for at, block in pieces_of(row_held, lists[0]):
            part(masked_ref, here[0] ^ at, height)[...] = block[...]
        total = dot(rows_ref[...], masked_ref[...])
        both_ref[0] = (total[:height] * kept_ref[1]).astype(both_ref.dtype)
        grad = 3.0 * pair_ref[1].astype(jnp.float32) - 2.0 * total[height:]
        both_ref[1] = (grad * kept_ref[1]).astype(both_ref.dtype)

    out = (
        pltpu.VMEM((2, height, width), pair.dtype),
        pltpu.VMEM((n_row * height, width), pair.dtype),
        pltpu.VMEM((2 * height, len(pair_held) * width), pair.dtype),
    )
    return call(kernel, "square_step", (pair, kept), (row_held,), (pair_held,), out)


def purify_step(both, kept, masked_cols, both_held):
    _, height, width = both.shape

    def kernel(here, fixed, lists, cols, outs):
        both_ref, kept_ref, masked_ref = fixed
        purified_ref, back_ref, scaled_ref, rows_ref = outs
        fill_rows(rows_ref, cols[0], here[1])
        total = dot(rows_ref[...], masked_ref[...])
        cubic = total[:height] * kept_ref[1]
        purified_ref[...] = (3.0 * both_ref[0].astype(jnp.float32) - 2.0 * cubic).astype(purified_ref.dtype)
        back_ref[...] = total[height:]
        scaled_ref[...] = (-2.0 * rows_ref[:height].astype(jnp.float32)).astype(scaled_ref.dtype)

    rows = (2 * height, len(both_held) * width)
    out = (
        pltpu.VMEM((height, width), both.dtype),
        pltpu.VMEM((height, width), jnp.float32),
        pltpu.VMEM((height, rows[1]), both.dtype),
    )
    scratch = [pltpu.VMEM(rows, both.dtype)]
    return call(kernel, "purify_step", (both, kept, masked_cols), (), (both_held,), out, scratch, hint=EARLY)


def last_step(kept, purified, back, pair_rows, scaled_rows, late_held):
    height, width = back.shape
    n_row = sum(len(ats) for ats, _ in late_held)

    def kernel(here, fixed, lists, cols, outs):
        kept_ref, purified_ref, back_ref, pair_ref, scaled_ref = fixed
        out_ref, gradient_ref, late_cols = outs
        out_ref[...] = purified_ref[...]
        for at, block in pieces_of(late_held, lists[0]):
            for k in range(2):
                part(late_cols.at[k], here[0] ^ at, height)[...] = block[k]
        summed = back_ref[...] + dot(pair_ref[:height], late_cols[0])
        summed = summed + dot(scaled_ref[...], late_cols[1])
        gradient_ref[...] = (summed * kept_ref[0]).astype(gradient_ref.dtype)

    out = jax.ShapeDtypeStruct((height, width), purified.dtype)
    scratch = [pltpu.VMEM((2, n_row * height, width), purified.dtype)]
    fixed = (kept, purified, back, pair_rows, scaled_rows)
    return call(kernel, "last_step", fixed, (late_held,), (), (out, out), scratch)


def on_device(n_row, n_col, density, cotangent, block_pattern, filter_pattern):
    chip_flips, core_flips = flips_of(n_row)[:-1], flips_of(n_row)[-1:]
    pair, kept = mask(density, cotangent, block_pattern, filter_pattern)

    pair_held = exchange(pair, "col", n_col, True)
    row_held = forward([([0], pair[:1])], "row", n_row, chip_flips)
    row_held = double(row_held, "row", n_row, core_flips)
    both, masked_cols, pair_rows = square_step(pair, kept, row_held, pair_held)

    both_held = exchange(both, "col", n_col, False)
    late_held = forward([([0], jnp.stack([both[1], pair[1]])[None])], "row", n_row, chip_flips)
    late_held = double(late_held, "row", n_row, core_flips)
    purified, back, scaled_rows = purify_step(both, kept, masked_cols, both_held)
    return last_step(kept, purified, back, pair_rows, scaled_rows, late_held)


def solution(mesh):
    placed = (P("row", "col"), P("row", "col"), P("row", "col"), P("row", "col"))

    def local(*arrays):
        return on_device(mesh.shape["row"], mesh.shape["col"], *arrays)

    return jax.shard_map(
        local,
        mesh=mesh,
        in_specs=placed,
        out_specs=(P("row", "col"), P("row", "col")),
        check_vma=False,
    )
```

```python
import jax
import jax.numpy as jnp
from jax import lax
from jax.experimental import pallas as pl
from jax.experimental.pallas import tpu as pltpu
from jax.sharding import PartitionSpec as P

IN_HBM = pl.BlockSpec(memory_space=pltpu.HBM)
IN_VMEM = pl.BlockSpec(memory_space=pltpu.VMEM)
LIMIT = pltpu.CompilerParams(vmem_limit_bytes=32 * 1024 * 1024)
EARLY = pl.CostEstimate(flops=6_000_000_000, bytes_accessed=0, transcendentals=0)


def dot(a, b):
    return jnp.dot(a, b, preferred_element_type=jnp.float32)


def mask(density, cotangent, block_pattern, filter_pattern):
    height, width = density.shape
    block_size = height // block_pattern.shape[0]

    def kernel(*refs):
        pattern_refs, dense_refs = refs[:2], refs[2:4]
        pair_ref, kept_ref, pattern_held, dense_held, sems = refs[4:]
        copies = []
        for k in range(2):
            copies.append(pltpu.make_async_copy(pattern_refs[k], pattern_held.at[k], sems.at[k]))
            copies.append(pltpu.make_async_copy(dense_refs[k], dense_held.at[k], sems.at[2 + k]))
        for copy in copies:
            copy.start()
        for copy in copies:
            copy.wait()
        lane = lax.broadcasted_iota(jnp.int32, (block_size, width), 1) // block_size
        for k in range(2):
            for i in range(height // block_size):
                rows = pl.ds(i * block_size, block_size)
                kept = jnp.zeros((block_size, width), jnp.float32)
                for j in range(width // block_size):
                    kept = jnp.where(lane == j, pattern_held[k, i, j].astype(jnp.float32), kept)
                kept_ref[k, rows, :] = kept
                pair_ref[k, rows, :] = (dense_held[k, rows, :].astype(jnp.float32) * kept).astype(pair_ref.dtype)

    inputs = (block_pattern, filter_pattern, density, cotangent)
    return pl.pallas_call(
        kernel,
        out_shape=(
            pltpu.VMEM((2, height, width), density.dtype),
            pltpu.VMEM((2, height, width), jnp.float32),
        ),
        in_specs=[IN_HBM] * 4,
        out_specs=(IN_VMEM, IN_VMEM),
        scratch_shapes=[
            pltpu.SMEM((2,) + block_pattern.shape, jnp.int32),
            pltpu.VMEM((2, height, width), density.dtype),
            pltpu.SemaphoreType.DMA((4,)),
        ],
        compiler_params=LIMIT,
        name="mask",
    )(*(pltpu.with_memory_space_constraint(x, pltpu.HBM) for x in inputs))


def settle(block):
    def kernel(block_ref, out_ref):
        out_ref[...] = block_ref[...]

    return pl.pallas_call(
        kernel,
        out_shape=pltpu.VMEM(block.shape, block.dtype),
        in_specs=[IN_VMEM],
        out_specs=IN_VMEM,
        cost_estimate=EARLY,
        compiler_params=LIMIT,
        name="settle",
    )(block)


def flips_of(size):
    flips = []
    while 2 ** len(flips) < size:
        flips.insert(0, 2 ** len(flips))
    return flips


def swap(held, axis_name, size, flips):
    return [
        ([at ^ flip for at in ats], lax.ppermute(blocks, axis_name, [(i, i ^ flip) for i in range(size)]))
        for flip in flips
        for ats, blocks in held
    ]


def double(held, axis_name, size, flips):
    for flip in flips:
        ats = [at for entry in held for at in entry[0]]
        blocks = held[0][1] if len(held) == 1 else jnp.concatenate([entry[1] for entry in held])
        held = held + swap([(ats, blocks)], axis_name, size, [flip])
    return held


def forward(held, axis_name, size, flips):
    held = double(held, axis_name, size, flips[:-2])
    far = swap(held, axis_name, size, flips[-2:-1])
    near = swap(held, axis_name, size, flips[-1:])
    return held + far + near + swap(far, axis_name, size, flips[-1:])


def tie(helds):
    arrays = lax.optimization_barrier([[blocks for _, blocks in held] for held in helds])
    return [[(ats, block) for (ats, _), block in zip(held, blocks)] for held, blocks in zip(helds, arrays)]


def exchange(pair, axis_name, size, settled, later=()):
    flips = flips_of(size)
    held = double([([0], pair[None])], axis_name, size, flips[:-2])
    far = swap(held, axis_name, size, flips[-2:-1])
    near = swap(held, axis_name, size, flips[-1:])
    near, far = tie([near, far])
    _, later = tie([far, later])
    last = swap(far, axis_name, size, flips[-1:])
    if settled:
        last = [(ats, settle(pairs)) for ats, pairs in last]
    held = held + far + near + last
    return [(at, ((pairs, (k, 0)), (pairs, (k, 1)))) for ats, pairs in held for k, at in enumerate(ats)], later


def part(ref, owner, size):
    return ref.at[pl.ds(pl.multiple_of(owner * size, size), size), :]


def settle(block):
    def kernel(block_ref, out_ref):
        out_ref[...] = block_ref[...]

    return pl.pallas_call(
        kernel,
        out_shape=pltpu.VMEM(block.shape, block.dtype),
        in_specs=[IN_VMEM],
        out_specs=IN_VMEM,
        cost_estimate=EARLY,
        compiler_params=LIMIT,
        name="settle",
    )(block)


def call(kernel, name, fixed, blocks, pairs, out_shape, scratch=(), hint=None):
    arrays, places = [*fixed], {}
    for array, _ in [block for _, block in blocks] + [block for _, two in pairs for block in two]:
        if id(array) not in places:
            places[id(array)] = len(arrays)
            arrays.append(array)

    def body(*refs):
        def ref_of(block):
            return refs[places[id(block[0])]].at[block[1]]

        here = (lax.axis_index("row"), lax.axis_index("col"))
        block_refs = [(at, ref_of(block)) for at, block in blocks]
        pair_refs = [(at, [ref_of(block) for block in two]) for at, two in pairs]
        kernel(here, refs[:len(fixed)], block_refs, pair_refs, refs[len(arrays):])

    return pl.pallas_call(
        body,
        out_shape=out_shape,
        in_specs=[IN_VMEM] * len(arrays),
        out_specs=jax.tree.map(lambda _: IN_VMEM, out_shape),
        scratch_shapes=scratch,
        cost_estimate=hint,
        compiler_params=LIMIT,
        name=name,
    )(*arrays)


def fill_rows(rows_ref, pieces, here_col):
    height, width = rows_ref.shape[0] // 2, rows_ref.shape[1] // len(pieces)
    for at, blocks in pieces:
        columns = pl.ds(pl.multiple_of((here_col ^ at) * width, width), width)
        for k in range(2):
            rows_ref[k * height:(k + 1) * height, columns] = blocks[k][...]


def square_step(pair, kept, masked_blocks, pair_held):
    _, height, width = pair.shape
    n_row = len(masked_blocks)

    def kernel(here, fixed, blocks, pairs, outs):
        pair_ref, kept_ref = fixed
        both_ref, masked_ref, rows_ref = outs
        fill_rows(rows_ref, pairs, here[1])
        for at, block in blocks:
            part(masked_ref, here[0] ^ at, height)[...] = block[...]
        total = dot(rows_ref[...], masked_ref[...])
        both_ref[0] = (total[:height] * kept_ref[1]).astype(both_ref.dtype)
        grad = 3.0 * pair_ref[1].astype(jnp.float32) - 2.0 * total[height:]
        both_ref[1] = (grad * kept_ref[1]).astype(both_ref.dtype)

    out = (
        pltpu.VMEM((2, height, width), pair.dtype),
        pltpu.VMEM((n_row * height, width), pair.dtype),
        pltpu.VMEM((2 * height, len(pair_held) * width), pair.dtype),
    )
    return call(kernel, "square_step", (pair, kept), masked_blocks, pair_held, out)


def purify_step(both, kept, masked_cols, both_held):
    _, height, width = both.shape

    def kernel(here, fixed, blocks, pairs, outs):
        both_ref, kept_ref, masked_ref = fixed
        purified_ref, back_ref, scaled_ref, rows_ref = outs
        fill_rows(rows_ref, pairs, here[1])
        total = dot(rows_ref[...], masked_ref[...])
        cubic = total[:height] * kept_ref[1]
        purified_ref[...] = (3.0 * both_ref[0].astype(jnp.float32) - 2.0 * cubic).astype(purified_ref.dtype)
        back_ref[...] = total[height:]
        scaled_ref[...] = (-2.0 * rows_ref[:height].astype(jnp.float32)).astype(scaled_ref.dtype)

    rows = (2 * height, len(both_held) * width)
    out = (
        pltpu.VMEM((height, width), both.dtype),
        pltpu.VMEM((height, width), jnp.float32),
        pltpu.VMEM((height, rows[1]), both.dtype),
    )
    scratch = [pltpu.VMEM(rows, both.dtype)]
    return call(kernel, "purify_step", (both, kept, masked_cols), [], both_held, out, scratch, hint=EARLY)


def last_step(kept, purified, back, pair_rows, scaled_rows, grad_blocks, filtered_blocks):
    height, width = back.shape
    n_row = len(grad_blocks)

    def kernel(here, fixed, blocks, pairs, outs):
        kept_ref, purified_ref, back_ref, pair_ref, scaled_ref = fixed
        out_ref, gradient_ref, late_cols = outs
        out_ref[...] = purified_ref[...]
        for i, (at, block) in enumerate(blocks):
            part(late_cols.at[i // n_row], here[0] ^ at, height)[...] = block[...]
        summed = back_ref[...] + dot(pair_ref[:height], late_cols[0])
        summed = summed + dot(scaled_ref[...], late_cols[1])
        gradient_ref[...] = (summed * kept_ref[0]).astype(gradient_ref.dtype)

    out = jax.ShapeDtypeStruct((height, width), purified.dtype)
    scratch = [pltpu.VMEM((2, n_row * height, width), purified.dtype)]
    fixed = (kept, purified, back, pair_rows, scaled_rows)
    return call(kernel, "last_step", fixed, grad_blocks + filtered_blocks, [], (out, out), scratch)


def take(held, *inner):
    return [(at, (array, (k,) + inner)) for ats, array in held for k, at in enumerate(ats)]


def cut(held, k):
    return [(ats, array[:, k]) for ats, array in held]


def pairs_of(one, two):
    return [(ats, jnp.stack([first, second], 1)) for (ats, first), (_, second) in zip(one, two)]


def across_cores(lists, n_row):
    ats = [[at for ats, _ in held for at in ats] for held in lists]
    assert all(sorted(a) == sorted(ats[0]) for a in ats)
    flips = flips_of(n_row)[-1:]
    sent = jnp.stack([jnp.concatenate([array for _, array in held]) for held in lists])
    got = [lax.ppermute(sent, "row", [(i, i ^ flip) for i in range(n_row)]) for flip in flips]
    return [
        take(held) + [(at ^ flip, (array, (k, i))) for flip, array in zip(flips, got) for i, at in enumerate(own)]
        for k, (held, own) in enumerate(zip(lists, ats))
    ]


def on_device(n_row, n_col, density, cotangent, block_pattern, filter_pattern):
    chip_flips = flips_of(n_row)[:-1]
    lead, first, second = chip_flips[:-2], chip_flips[-2:-1], chip_flips[-1:]
    pair, kept = mask(density, cotangent, block_pattern, filter_pattern)

    own = double([([0], pair[None])], "row", n_row, lead)
    masked, filtered = cut(own, 0), cut(own, 1)
    pair_held, later = exchange(pair, "col", n_col, True, filtered)
    far = swap(masked, "row", n_row, first)
    near = swap(masked, "row", n_row, second)
    masked = masked + far + near + swap(far, "row", n_row, second)
    other = swap(later, "row", n_row, second)
    (masked_blocks,) = across_cores([masked], n_row)
    both, masked_cols, pair_rows = square_step(pair, kept, masked_blocks, pair_held)

    both_held, _ = exchange(both, "col", n_col, False)
    grad = double([([0], both[1:])], "row", n_row, lead)
    far = swap(grad, "row", n_row, second)
    left = swap(pairs_of(grad, filtered), "row", n_row, first)
    right = swap(pairs_of(far, other), "row", n_row, first)
    grad = grad + far + cut(left, 0) + cut(right, 0)
    filtered = filtered + other + cut(left, 1) + cut(right, 1)
    grad_blocks, filtered_blocks = across_cores([grad, filtered], n_row)
    purified, back, scaled_rows = purify_step(both, kept, masked_cols, both_held)
    return last_step(kept, purified, back, pair_rows, scaled_rows, grad_blocks, filtered_blocks)


def solution(mesh):
    placed = (P("row", "col"), P("row", "col"), P("row", "col"), P("row", "col"))

    def local(*arrays):
        return on_device(mesh.shape["row"], mesh.shape["col"], *arrays)

    return jax.shard_map(
        local,
        mesh=mesh,
        in_specs=placed,
        out_specs=(P("row", "col"), P("row", "col")),
        check_vma=False,
    )
```

```python
import jax
import jax.numpy as jnp
from jax import lax
from jax.experimental import pallas as pl
from jax.experimental.pallas import tpu as pltpu
from jax.sharding import PartitionSpec as P

IN_HBM = pl.BlockSpec(memory_space=pltpu.HBM)
IN_VMEM = pl.BlockSpec(memory_space=pltpu.VMEM)
SOON = pl.CostEstimate(flops=100_000_000, bytes_accessed=0, transcendentals=0)
LIMIT = pltpu.CompilerParams(vmem_limit_bytes=32 * 1024 * 1024)
EARLY = pl.CostEstimate(flops=6_000_000_000, bytes_accessed=0, transcendentals=0)


def dot(a, b):
    return jnp.dot(a, b, preferred_element_type=jnp.float32)


def mask(density, cotangent, block_pattern, filter_pattern):
    height, width = density.shape
    block_size = height // block_pattern.shape[0]

    def kernel(*refs):
        pattern_refs, dense_refs = refs[:2], refs[2:4]
        pair_ref, kept_ref, pattern_held, dense_held, sems = refs[4:]
        copies = []
        for k in range(2):
            copies.append(pltpu.make_async_copy(pattern_refs[k], pattern_held.at[k], sems.at[k]))
            copies.append(pltpu.make_async_copy(dense_refs[k], dense_held.at[k], sems.at[2 + k]))
        for copy in copies:
            copy.start()
        for copy in copies:
            copy.wait()
        lane = lax.broadcasted_iota(jnp.int32, (block_size, width), 1) // block_size
        for k in range(2):
            for i in range(height // block_size):
                rows = pl.ds(i * block_size, block_size)
                kept = jnp.zeros((block_size, width), jnp.float32)
                for j in range(width // block_size):
                    kept = jnp.where(lane == j, pattern_held[k, i, j].astype(jnp.float32), kept)
                kept_ref[k, rows, :] = kept
                pair_ref[k, rows, :] = (dense_held[k, rows, :].astype(jnp.float32) * kept).astype(pair_ref.dtype)

    inputs = (block_pattern, filter_pattern, density, cotangent)
    return pl.pallas_call(
        kernel,
        out_shape=(
            pltpu.VMEM((2, height, width), density.dtype),
            pltpu.VMEM((2, height, width), jnp.float32),
        ),
        in_specs=[IN_HBM] * 4,
        out_specs=(IN_VMEM, IN_VMEM),
        scratch_shapes=[
            pltpu.SMEM((2,) + block_pattern.shape, jnp.int32),
            pltpu.VMEM((2, height, width), density.dtype),
            pltpu.SemaphoreType.DMA((4,)),
        ],
        compiler_params=LIMIT,
        name="mask",
    )(*(pltpu.with_memory_space_constraint(x, pltpu.HBM) for x in inputs))


def settle(block):
    def kernel(block_ref, out_ref):
        out_ref[...] = block_ref[...]

    return pl.pallas_call(
        kernel,
        out_shape=pltpu.VMEM(block.shape, block.dtype),
        in_specs=[IN_VMEM],
        out_specs=IN_VMEM,
        cost_estimate=hint,
        compiler_params=LIMIT,
        name="settle",
    )(block)


def flips_of(size):
    flips = []
    while 2 ** len(flips) < size:
        flips.insert(0, 2 ** len(flips))
    return flips


def swap(held, axis_name, size, flips):
    return [
        ([at ^ flip for at in ats], lax.ppermute(blocks, axis_name, [(i, i ^ flip) for i in range(size)]))
        for flip in flips
        for ats, blocks in held
    ]


def double(held, axis_name, size, flips):
    for flip in flips:
        ats = [at for entry in held for at in entry[0]]
        blocks = held[0][1] if len(held) == 1 else jnp.concatenate([entry[1] for entry in held])
        held = held + swap([(ats, blocks)], axis_name, size, [flip])
    return held


def forward(held, axis_name, size, flips):
    held = double(held, axis_name, size, flips[:-2])
    far = swap(held, axis_name, size, flips[-2:-1])
    near = swap(held, axis_name, size, flips[-1:])
    return held + far + near + swap(far, axis_name, size, flips[-1:])


def tie(helds):
    arrays = lax.optimization_barrier([[blocks for _, blocks in held] for held in helds])
    return [[(ats, block) for (ats, _), block in zip(held, blocks)] for held, blocks in zip(helds, arrays)]


def exchange(pair, axis_name, size, settled, later=()):
    flips = flips_of(size)
    held = double([([0], pair[None])], axis_name, size, flips[:-2])
    far = swap(held, axis_name, size, flips[-2:-1])
    near = swap(held, axis_name, size, flips[-1:])
    _, later = tie([far, later])
    if settled:
        near = [(ats, settle(pairs, SOON)) for ats, pairs in near]
    else:
        near, far = tie([near, far])
    last = swap(far, axis_name, size, flips[-1:])
    if settled:
        last = [(ats, settle(pairs, EARLY)) for ats, pairs in last]
    held = held + far + near + last
    return [(at, ((pairs, (k, 0)), (pairs, (k, 1)))) for ats, pairs in held for k, at in enumerate(ats)], later


def part(ref, owner, size):
    return ref.at[pl.ds(pl.multiple_of(owner * size, size), size), :]


def settle(block, hint):
    def kernel(block_ref, out_ref):
        out_ref[...] = block_ref[...]

    return pl.pallas_call(
        kernel,
        out_shape=pltpu.VMEM(block.shape, block.dtype),
        in_specs=[IN_VMEM],
        out_specs=IN_VMEM,
        cost_estimate=hint,
        compiler_params=LIMIT,
        name="settle",
    )(block)


def call(kernel, name, fixed, blocks, pairs, out_shape, scratch=(), hint=None):
    arrays, places = [*fixed], {}
    for array, _ in [block for _, block in blocks] + [block for _, two in pairs for block in two]:
        if id(array) not in places:
            places[id(array)] = len(arrays)
            arrays.append(array)

    def body(*refs):
        def ref_of(block):
            return refs[places[id(block[0])]].at[block[1]]

        here = (lax.axis_index("row"), lax.axis_index("col"))
        block_refs = [(at, ref_of(block)) for at, block in blocks]
        pair_refs = [(at, [ref_of(block) for block in two]) for at, two in pairs]
        kernel(here, refs[:len(fixed)], block_refs, pair_refs, refs[len(arrays):])

    return pl.pallas_call(
        body,
        out_shape=out_shape,
        in_specs=[IN_VMEM] * len(arrays),
        out_specs=jax.tree.map(lambda _: IN_VMEM, out_shape),
        scratch_shapes=scratch,
        cost_estimate=hint,
        compiler_params=LIMIT,
        name=name,
    )(*arrays)


def fill_rows(rows_ref, pieces, here_col):
    height, width = rows_ref.shape[0] // 2, rows_ref.shape[1] // len(pieces)
    for at, blocks in pieces:
        columns = pl.ds(pl.multiple_of((here_col ^ at) * width, width), width)
        for k in range(2):
            rows_ref[k * height:(k + 1) * height, columns] = blocks[k][...]


def square_step(pair, kept, masked_blocks, pair_held):
    _, height, width = pair.shape
    n_row = len(masked_blocks)

    def kernel(here, fixed, blocks, pairs, outs):
        pair_ref, kept_ref = fixed
        both_ref, masked_ref, rows_ref = outs
        fill_rows(rows_ref, pairs, here[1])
        for at, block in blocks:
            part(masked_ref, here[0] ^ at, height)[...] = block[...]
        total = dot(rows_ref[...], masked_ref[...])
        both_ref[0] = (total[:height] * kept_ref[1]).astype(both_ref.dtype)
        grad = 3.0 * pair_ref[1].astype(jnp.float32) - 2.0 * total[height:]
        both_ref[1] = (grad * kept_ref[1]).astype(both_ref.dtype)

    out = (
        pltpu.VMEM((2, height, width), pair.dtype),
        pltpu.VMEM((n_row * height, width), pair.dtype),
        pltpu.VMEM((2 * height, len(pair_held) * width), pair.dtype),
    )
    return call(kernel, "square_step", (pair, kept), masked_blocks, pair_held, out)


def purify_step(both, kept, masked_cols, both_held):
    _, height, width = both.shape

    def kernel(here, fixed, blocks, pairs, outs):
        both_ref, kept_ref, masked_ref = fixed
        purified_ref, back_ref, scaled_ref, rows_ref = outs
        fill_rows(rows_ref, pairs, here[1])
        total = dot(rows_ref[...], masked_ref[...])
        cubic = total[:height] * kept_ref[1]
        purified_ref[...] = (3.0 * both_ref[0].astype(jnp.float32) - 2.0 * cubic).astype(purified_ref.dtype)
        back_ref[...] = total[height:]
        scaled_ref[...] = (-2.0 * rows_ref[:height].astype(jnp.float32)).astype(scaled_ref.dtype)

    rows = (2 * height, len(both_held) * width)
    out = (
        pltpu.VMEM((height, width), both.dtype),
        pltpu.VMEM((height, width), jnp.float32),
        pltpu.VMEM((height, rows[1]), both.dtype),
    )
    scratch = [pltpu.VMEM(rows, both.dtype)]
    return call(kernel, "purify_step", (both, kept, masked_cols), [], both_held, out, scratch, hint=EARLY)


def last_step(kept, purified, back, pair_rows, scaled_rows, grad_blocks, filtered_blocks):
    height, width = back.shape
    n_row = len(grad_blocks)

    def kernel(here, fixed, blocks, pairs, outs):
        kept_ref, purified_ref, back_ref, pair_ref, scaled_ref = fixed
        out_ref, gradient_ref, late_cols = outs
        out_ref[...] = purified_ref[...]
        for i, (at, block) in enumerate(blocks):
            part(late_cols.at[i // n_row], here[0] ^ at, height)[...] = block[...]
        summed = back_ref[...] + dot(pair_ref[:height], late_cols[0])
        summed = summed + dot(scaled_ref[...], late_cols[1])
        gradient_ref[...] = (summed * kept_ref[0]).astype(gradient_ref.dtype)

    out = jax.ShapeDtypeStruct((height, width), purified.dtype)
    scratch = [pltpu.VMEM((2, n_row * height, width), purified.dtype)]
    fixed = (kept, purified, back, pair_rows, scaled_rows)
    return call(kernel, "last_step", fixed, grad_blocks + filtered_blocks, [], (out, out), scratch)


def take(held, *inner):
    return [(at, (array, (k,) + inner)) for ats, array in held for k, at in enumerate(ats)]


def cut(held, k):
    return [(ats, array[:, k]) for ats, array in held]


def pairs_of(one, two):
    return [(ats, jnp.stack([first, second], 1)) for (ats, first), (_, second) in zip(one, two)]


def across_cores(lists, n_row):
    ats = [[at for ats, _ in held for at in ats] for held in lists]
    assert all(sorted(a) == sorted(ats[0]) for a in ats)
    flips = flips_of(n_row)[-1:]
    sent = jnp.stack([jnp.concatenate([array for _, array in held]) for held in lists])
    got = [lax.ppermute(sent, "row", [(i, i ^ flip) for i in range(n_row)]) for flip in flips]
    return [
        take(held) + [(at ^ flip, (array, (k, i))) for flip, array in zip(flips, got) for i, at in enumerate(own)]
        for k, (held, own) in enumerate(zip(lists, ats))
    ]


def on_device(n_row, n_col, density, cotangent, block_pattern, filter_pattern):
    chip_flips = flips_of(n_row)[:-1]
    lead, first, second = chip_flips[:-2], chip_flips[-2:-1], chip_flips[-1:]
    pair, kept = mask(density, cotangent, block_pattern, filter_pattern)

    own = double([([0], pair[None])], "row", n_row, lead)
    masked, filtered = cut(own, 0), cut(own, 1)
    pair_held, later = exchange(pair, "col", n_col, True, filtered)
    far = swap(masked, "row", n_row, first)
    near = swap(masked, "row", n_row, second)
    masked = masked + far + near + swap(far, "row", n_row, second)
    other = swap(later, "row", n_row, second)
    (masked_blocks,) = across_cores([masked], n_row)
    both, masked_cols, pair_rows = square_step(pair, kept, masked_blocks, pair_held)

    both_held, _ = exchange(both, "col", n_col, False)
    grad = double([([0], both[1:])], "row", n_row, lead)
    far = swap(grad, "row", n_row, second)
    left = swap(pairs_of(grad, filtered), "row", n_row, first)
    right = swap(pairs_of(far, other), "row", n_row, first)
    grad = grad + far + cut(left, 0) + cut(right, 0)
    filtered = filtered + other + cut(left, 1) + cut(right, 1)
    grad_blocks, filtered_blocks = across_cores([grad, filtered], n_row)
    purified, back, scaled_rows = purify_step(both, kept, masked_cols, both_held)
    return last_step(kept, purified, back, pair_rows, scaled_rows, grad_blocks, filtered_blocks)


def solution(mesh):
    placed = (P("row", "col"), P("row", "col"), P("row", "col"), P("row", "col"))

    def local(*arrays):
        return on_device(mesh.shape["row"], mesh.shape["col"], *arrays)

    return jax.shard_map(
        local,
        mesh=mesh,
        in_specs=placed,
        out_specs=(P("row", "col"), P("row", "col")),
        check_vma=False,
    )
```

```python
import jax
import jax.numpy as jnp
from jax import lax
from jax.experimental import pallas as pl
from jax.experimental.pallas import tpu as pltpu
from jax.sharding import PartitionSpec as P

IN_HBM = pl.BlockSpec(memory_space=pltpu.HBM)
IN_VMEM = pl.BlockSpec(memory_space=pltpu.VMEM)
LIMIT = pltpu.CompilerParams(vmem_limit_bytes=32 * 1024 * 1024)
EARLY = pl.CostEstimate(flops=6_000_000_000, bytes_accessed=0, transcendentals=0)


def dot(a, b):
    return jnp.dot(a, b, preferred_element_type=jnp.float32)


def mask(density, cotangent, block_pattern, filter_pattern):
    height, width = density.shape
    block_size = height // block_pattern.shape[0]

    def kernel(*refs):
        pattern_refs, dense_refs = refs[:2], refs[2:4]
        pair_ref, kept_ref, pattern_held, dense_held, sems = refs[4:]
        copies = []
        for k in range(2):
            copies.append(pltpu.make_async_copy(pattern_refs[k], pattern_held.at[k], sems.at[k]))
            copies.append(pltpu.make_async_copy(dense_refs[k], dense_held.at[k], sems.at[2 + k]))
        for copy in copies:
            copy.start()
        for copy in copies:
            copy.wait()
        lane = lax.broadcasted_iota(jnp.int32, (block_size, width), 1) // block_size
        for k in range(2):
            for i in range(height // block_size):
                rows = pl.ds(i * block_size, block_size)
                kept = jnp.zeros((block_size, width), jnp.float32)
                for j in range(width // block_size):
                    kept = jnp.where(lane == j, pattern_held[k, i, j].astype(jnp.float32), kept)
                kept_ref[k, rows, :] = kept
                pair_ref[k, rows, :] = (dense_held[k, rows, :].astype(jnp.float32) * kept).astype(pair_ref.dtype)

    inputs = (block_pattern, filter_pattern, density, cotangent)
    return pl.pallas_call(
        kernel,
        out_shape=(
            pltpu.VMEM((2, height, width), density.dtype),
            pltpu.VMEM((2, height, width), jnp.float32),
        ),
        in_specs=[IN_HBM] * 4,
        out_specs=(IN_VMEM, IN_VMEM),
        scratch_shapes=[
            pltpu.SMEM((2,) + block_pattern.shape, jnp.int32),
            pltpu.VMEM((2, height, width), density.dtype),
            pltpu.SemaphoreType.DMA((4,)),
        ],
        compiler_params=LIMIT,
        name="mask",
    )(*(pltpu.with_memory_space_constraint(x, pltpu.HBM) for x in inputs))


def settle(block):
    def kernel(block_ref, out_ref):
        out_ref[...] = block_ref[...]

    return pl.pallas_call(
        kernel,
        out_shape=pltpu.VMEM(block.shape, block.dtype),
        in_specs=[IN_VMEM],
        out_specs=IN_VMEM,
        cost_estimate=hint,
        compiler_params=LIMIT,
        name="settle",
    )(block)


def flips_of(size):
    flips = []
    while 2 ** len(flips) < size:
        flips.insert(0, 2 ** len(flips))
    return flips


def swap(held, axis_name, size, flips):
    return [
        ([at ^ flip for at in ats], lax.ppermute(blocks, axis_name, [(i, i ^ flip) for i in range(size)]))
        for flip in flips
        for ats, blocks in held
    ]


def double(held, axis_name, size, flips):
    for flip in flips:
        ats = [at for entry in held for at in entry[0]]
        blocks = held[0][1] if len(held) == 1 else jnp.concatenate([entry[1] for entry in held])
        held = held + swap([(ats, blocks)], axis_name, size, [flip])
    return held


def forward(held, axis_name, size, flips):
    held = double(held, axis_name, size, flips[:-2])
    far = swap(held, axis_name, size, flips[-2:-1])
    near = swap(held, axis_name, size, flips[-1:])
    return held + far + near + swap(far, axis_name, size, flips[-1:])


def tie(helds):
    arrays = lax.optimization_barrier([[blocks for _, blocks in held] for held in helds])
    return [[(ats, block) for (ats, _), block in zip(held, blocks)] for held, blocks in zip(helds, arrays)]


def exchange(pair, axis_name, size, settled, later=()):
    flips = flips_of(size)
    held = double([([0], pair[None])], axis_name, size, flips[:-2])
    far = swap(held, axis_name, size, flips[-2:-1])
    near = swap(held, axis_name, size, flips[-1:])
    _, later = tie([far, later])
    near, far = tie([near, far])
    last = swap(far, axis_name, size, flips[-1:])
    if settled:
        last = [(ats, settle(pairs, EARLY)) for ats, pairs in last]
    held = held + far + near + last
    return [(at, ((pairs, (k, 0)), (pairs, (k, 1)))) for ats, pairs in held for k, at in enumerate(ats)], later


def part(ref, owner, size):
    return ref.at[pl.ds(pl.multiple_of(owner * size, size), size), :]


def settle(block, hint):
    def kernel(block_ref, out_ref):
        out_ref[...] = block_ref[...]

    return pl.pallas_call(
        kernel,
        out_shape=pltpu.VMEM(block.shape, block.dtype),
        in_specs=[IN_VMEM],
        out_specs=IN_VMEM,
        cost_estimate=hint,
        compiler_params=LIMIT,
        name="settle",
    )(block)


def call(kernel, name, fixed, blocks, pairs, out_shape, scratch=(), hint=None):
    arrays, places = [*fixed], {}
    for array, _ in [block for _, block in blocks] + [block for _, two in pairs for block in two]:
        if id(array) not in places:
            places[id(array)] = len(arrays)
            arrays.append(array)

    def body(*refs):
        def ref_of(block):
            return refs[places[id(block[0])]].at[block[1]]

        here = (lax.axis_index("row"), lax.axis_index("col"))
        block_refs = [(at, ref_of(block)) for at, block in blocks]
        pair_refs = [(at, [ref_of(block) for block in two]) for at, two in pairs]
        kernel(here, refs[:len(fixed)], block_refs, pair_refs, refs[len(arrays):])

    return pl.pallas_call(
        body,
        out_shape=out_shape,
        in_specs=[IN_VMEM] * len(arrays),
        out_specs=jax.tree.map(lambda _: IN_VMEM, out_shape),
        scratch_shapes=scratch,
        cost_estimate=hint,
        compiler_params=LIMIT,
        name=name,
    )(*arrays)


def fill_rows(rows_ref, pieces, here_col):
    height, width = rows_ref.shape[0] // 2, rows_ref.shape[1] // len(pieces)
    for at, blocks in pieces:
        columns = pl.ds(pl.multiple_of((here_col ^ at) * width, width), width)
        for k in range(2):
            rows_ref[k * height:(k + 1) * height, columns] = blocks[k][...]


def square_step(pair, kept, masked_blocks, pair_held):
    _, height, width = pair.shape
    n_row = len(masked_blocks)

    def kernel(here, fixed, blocks, pairs, outs):
        pair_ref, kept_ref = fixed
        both_ref, masked_ref, rows_ref = outs
        fill_rows(rows_ref, pairs, here[1])
        for at, block in blocks:
            part(masked_ref, here[0] ^ at, height)[...] = block[...]
        total = dot(rows_ref[...], masked_ref[...])
        both_ref[0] = (total[:height] * kept_ref[1]).astype(both_ref.dtype)
        grad = 3.0 * pair_ref[1].astype(jnp.float32) - 2.0 * total[height:]
        both_ref[1] = (grad * kept_ref[1]).astype(both_ref.dtype)

    out = (
        pltpu.VMEM((2, height, width), pair.dtype),
        pltpu.VMEM((n_row * height, width), pair.dtype),
        pltpu.VMEM((2 * height, len(pair_held) * width), pair.dtype),
    )
    return call(kernel, "square_step", (pair, kept), masked_blocks, pair_held, out)


def purify_step(both, kept, masked_cols, both_held):
    _, height, width = both.shape

    def kernel(here, fixed, blocks, pairs, outs):
        both_ref, kept_ref, masked_ref = fixed
        purified_ref, back_ref, scaled_ref, rows_ref = outs
        fill_rows(rows_ref, pairs, here[1])
        total = dot(rows_ref[...], masked_ref[...])
        cubic = total[:height] * kept_ref[1]
        purified_ref[...] = (3.0 * both_ref[0].astype(jnp.float32) - 2.0 * cubic).astype(purified_ref.dtype)
        back_ref[...] = total[height:]
        scaled_ref[...] = (-2.0 * rows_ref[:height].astype(jnp.float32)).astype(scaled_ref.dtype)

    rows = (2 * height, len(both_held) * width)
    out = (
        pltpu.VMEM((height, width), both.dtype),
        pltpu.VMEM((height, width), jnp.float32),
        pltpu.VMEM((height, rows[1]), both.dtype),
    )
    scratch = [pltpu.VMEM(rows, both.dtype)]
    return call(kernel, "purify_step", (both, kept, masked_cols), [], both_held, out, scratch, hint=EARLY)


def last_step(kept, purified, back, pair_rows, scaled_rows, grad_blocks, filtered_blocks):
    height, width = back.shape
    n_row = len(grad_blocks)

    def kernel(here, fixed, blocks, pairs, outs):
        kept_ref, purified_ref, back_ref, pair_ref, scaled_ref = fixed
        out_ref, gradient_ref, late_cols = outs
        out_ref[...] = purified_ref[...]
        for i, (at, block) in enumerate(blocks):
            part(late_cols.at[i // n_row], here[0] ^ at, height)[...] = block[...]
        summed = back_ref[...] + dot(pair_ref[:height], late_cols[0])
        summed = summed + dot(scaled_ref[...], late_cols[1])
        gradient_ref[...] = (summed * kept_ref[0]).astype(gradient_ref.dtype)

    out = jax.ShapeDtypeStruct((height, width), purified.dtype)
    scratch = [pltpu.VMEM((2, n_row * height, width), purified.dtype)]
    fixed = (kept, purified, back, pair_rows, scaled_rows)
    return call(kernel, "last_step", fixed, grad_blocks + filtered_blocks, [], (out, out), scratch)


def take(held, *inner):
    return [(at, (array, (k,) + inner)) for ats, array in held for k, at in enumerate(ats)]


def cut(held, k):
    return [(ats, array[:, k]) for ats, array in held]


def pairs_of(one, two):
    return [(ats, jnp.stack([first, second], 1)) for (ats, first), (_, second) in zip(one, two)]


def across_cores(lists, n_row):
    ats = [[at for ats, _ in held for at in ats] for held in lists]
    assert all(sorted(a) == sorted(ats[0]) for a in ats)
    flips = flips_of(n_row)[-1:]
    sent = jnp.stack([jnp.concatenate([array for _, array in held]) for held in lists])
    got = [lax.ppermute(sent, "row", [(i, i ^ flip) for i in range(n_row)]) for flip in flips]
    return [
        take(held) + [(at ^ flip, (array, (k, i))) for flip, array in zip(flips, got) for i, at in enumerate(own)]
        for k, (held, own) in enumerate(zip(lists, ats))
    ]


def on_device(n_row, n_col, density, cotangent, block_pattern, filter_pattern):
    chip_flips = flips_of(n_row)[:-1]
    lead, first, second = chip_flips[:-2], chip_flips[-2:-1], chip_flips[-1:]
    pair, kept = mask(density, cotangent, block_pattern, filter_pattern)

    own = double([([0], pair[None])], "row", n_row, lead)
    masked, filtered = cut(own, 0), cut(own, 1)
    pair_held, later = exchange(pair, "col", n_col, True, filtered)
    masked = double(masked, "row", n_row, first + second)
    other = swap(later, "row", n_row, second)
    (masked_blocks,) = across_cores([masked], n_row)
    both, masked_cols, pair_rows = square_step(pair, kept, masked_blocks, pair_held)

    both_held, _ = exchange(both, "col", n_col, False)
    grad = double([([0], both[1:])], "row", n_row, lead)
    far = swap(grad, "row", n_row, second)
    left = swap(pairs_of(grad, filtered), "row", n_row, first)
    right = swap(pairs_of(far, other), "row", n_row, first)
    grad = grad + far + cut(left, 0) + cut(right, 0)
    filtered = filtered + other + cut(left, 1) + cut(right, 1)
    grad_blocks, filtered_blocks = across_cores([grad, filtered], n_row)
    purified, back, scaled_rows = purify_step(both, kept, masked_cols, both_held)
    return last_step(kept, purified, back, pair_rows, scaled_rows, grad_blocks, filtered_blocks)


def solution(mesh):
    placed = (P("row", "col"), P("row", "col"), P("row", "col"), P("row", "col"))

    def local(*arrays):
        return on_device(mesh.shape["row"], mesh.shape["col"], *arrays)

    return jax.shard_map(
        local,
        mesh=mesh,
        in_specs=placed,
        out_specs=(P("row", "col"), P("row", "col")),
        check_vma=False,
    )
```

```python
import jax
import jax.numpy as jnp
from jax import lax
from jax.experimental import pallas as pl
from jax.experimental.pallas import tpu as pltpu
from jax.sharding import PartitionSpec as P

IN_HBM = pl.BlockSpec(memory_space=pltpu.HBM)
IN_VMEM = pl.BlockSpec(memory_space=pltpu.VMEM)
LIMIT = pltpu.CompilerParams(vmem_limit_bytes=32 * 1024 * 1024)
EARLY = pl.CostEstimate(flops=6_000_000_000, bytes_accessed=0, transcendentals=0)


def dot(a, b):
    return jnp.dot(a, b, preferred_element_type=jnp.float32)


def mask(density, cotangent, block_pattern, filter_pattern):
    height, width = density.shape
    block_size = height // block_pattern.shape[0]

    def kernel(*refs):
        pattern_refs, dense_refs = refs[:2], refs[2:4]
        pair_ref, kept_ref, pattern_held, dense_held, sems = refs[4:]
        copies = []
        for k in range(2):
            copies.append(pltpu.make_async_copy(pattern_refs[k], pattern_held.at[k], sems.at[k]))
            copies.append(pltpu.make_async_copy(dense_refs[k], dense_held.at[k], sems.at[2 + k]))
        for copy in copies:
            copy.start()
        for copy in copies:
            copy.wait()
        lane = lax.broadcasted_iota(jnp.int32, (block_size, width), 1) // block_size
        for k in range(2):
            for i in range(height // block_size):
                rows = pl.ds(i * block_size, block_size)
                kept = jnp.zeros((block_size, width), jnp.float32)
                for j in range(width // block_size):
                    kept = jnp.where(lane == j, pattern_held[k, i:i + 1, j:j + 1].astype(jnp.float32), kept)
                kept_ref[k, rows, :] = kept
                pair_ref[k, rows, :] = (dense_held[k, rows, :].astype(jnp.float32) * kept).astype(pair_ref.dtype)

    inputs = (block_pattern, filter_pattern, density, cotangent)
    return pl.pallas_call(
        kernel,
        out_shape=(
            pltpu.VMEM((2, height, width), density.dtype),
            pltpu.VMEM((2, height, width), jnp.float32),
        ),
        in_specs=[IN_HBM] * 4,
        out_specs=(IN_VMEM, IN_VMEM),
        scratch_shapes=[
            pltpu.VMEM((2,) + block_pattern.shape, jnp.int32),
            pltpu.VMEM((2, height, width), density.dtype),
            pltpu.SemaphoreType.DMA((4,)),
        ],
        compiler_params=LIMIT,
        name="mask",
    )(*(pltpu.with_memory_space_constraint(x, pltpu.HBM) for x in inputs))


def settle(block):
    def kernel(block_ref, out_ref):
        out_ref[...] = block_ref[...]

    return pl.pallas_call(
        kernel,
        out_shape=pltpu.VMEM(block.shape, block.dtype),
        in_specs=[IN_VMEM],
        out_specs=IN_VMEM,
        cost_estimate=EARLY,
        compiler_params=LIMIT,
        name="settle",
    )(block)


def flips_of(size):
    flips = []
    while 2 ** len(flips) < size:
        flips.insert(0, 2 ** len(flips))
    return flips


def swap(held, axis_name, size, flips):
    return [
        ([at ^ flip for at in ats], lax.ppermute(blocks, axis_name, [(i, i ^ flip) for i in range(size)]))
        for flip in flips
        for ats, blocks in held
    ]


def double(held, axis_name, size, flips):
    for flip in flips:
        ats = [at for entry in held for at in entry[0]]
        blocks = held[0][1] if len(held) == 1 else jnp.concatenate([entry[1] for entry in held])
        held = held + swap([(ats, blocks)], axis_name, size, [flip])
    return held


def forward(held, axis_name, size, flips):
    held = double(held, axis_name, size, flips[:-2])
    far = swap(held, axis_name, size, flips[-2:-1])
    near = swap(held, axis_name, size, flips[-1:])
    return held + far + near + swap(far, axis_name, size, flips[-1:])


def tie(helds):
    arrays = lax.optimization_barrier([[blocks for _, blocks in held] for held in helds])
    return [[(ats, block) for (ats, _), block in zip(held, blocks)] for held, blocks in zip(helds, arrays)]


def exchange(pair, axis_name, size, settled, later=()):
    flips = flips_of(size)
    held = double([([0], pair[None])], axis_name, size, flips[:-2])
    far = swap(held, axis_name, size, flips[-2:-1])
    near = swap(held, axis_name, size, flips[-1:])
    near, far = tie([near, far])
    _, later = tie([far, later])
    last = swap(far, axis_name, size, flips[-1:])
    if settled:
        last = [(ats, settle(pairs)) for ats, pairs in last]
    held = held + far + near + last
    return [(at, ((pairs, (k, 0)), (pairs, (k, 1)))) for ats, pairs in held for k, at in enumerate(ats)], later


def part(ref, owner, size):
    return ref.at[pl.ds(pl.multiple_of(owner * size, size), size), :]


def settle(block):
    def kernel(block_ref, out_ref):
        out_ref[...] = block_ref[...]

    return pl.pallas_call(
        kernel,
        out_shape=pltpu.VMEM(block.shape, block.dtype),
        in_specs=[IN_VMEM],
        out_specs=IN_VMEM,
        cost_estimate=EARLY,
        compiler_params=LIMIT,
        name="settle",
    )(block)


def call(kernel, name, fixed, blocks, pairs, out_shape, scratch=(), hint=None):
    arrays, places = [*fixed], {}
    for array, _ in [block for _, block in blocks] + [block for _, two in pairs for block in two]:
        if id(array) not in places:
            places[id(array)] = len(arrays)
            arrays.append(array)

    def body(*refs):
        def ref_of(block):
            return refs[places[id(block[0])]].at[block[1]]

        here = (lax.axis_index("row"), lax.axis_index("col"))
        block_refs = [(at, ref_of(block)) for at, block in blocks]
        pair_refs = [(at, [ref_of(block) for block in two]) for at, two in pairs]
        kernel(here, refs[:len(fixed)], block_refs, pair_refs, refs[len(arrays):])

    return pl.pallas_call(
        body,
        out_shape=out_shape,
        in_specs=[IN_VMEM] * len(arrays),
        out_specs=jax.tree.map(lambda _: IN_VMEM, out_shape),
        scratch_shapes=scratch,
        cost_estimate=hint,
        compiler_params=LIMIT,
        name=name,
    )(*arrays)


def fill_rows(rows_ref, pieces, here_col):
    height, width = rows_ref.shape[0] // 2, rows_ref.shape[1] // len(pieces)
    for at, blocks in pieces:
        columns = pl.ds(pl.multiple_of((here_col ^ at) * width, width), width)
        for k in range(2):
            rows_ref[k * height:(k + 1) * height, columns] = blocks[k][...]


def square_step(pair, kept, masked_blocks, pair_held):
    _, height, width = pair.shape
    n_row = len(masked_blocks)

    def kernel(here, fixed, blocks, pairs, outs):
        pair_ref, kept_ref = fixed
        both_ref, masked_ref, rows_ref = outs
        fill_rows(rows_ref, pairs, here[1])
        for at, block in blocks:
            part(masked_ref, here[0] ^ at, height)[...] = block[...]
        total = dot(rows_ref[...], masked_ref[...])
        both_ref[0] = (total[:height] * kept_ref[1]).astype(both_ref.dtype)
        grad = 3.0 * pair_ref[1].astype(jnp.float32) - 2.0 * total[height:]
        both_ref[1] = (grad * kept_ref[1]).astype(both_ref.dtype)

    out = (
        pltpu.VMEM((2, height, width), pair.dtype),
        pltpu.VMEM((n_row * height, width), pair.dtype),
        pltpu.VMEM((2 * height, len(pair_held) * width), pair.dtype),
    )
    return call(kernel, "square_step", (pair, kept), masked_blocks, pair_held, out)


def purify_step(both, kept, masked_cols, both_held):
    _, height, width = both.shape

    def kernel(here, fixed, blocks, pairs, outs):
        both_ref, kept_ref, masked_ref = fixed
        purified_ref, back_ref, scaled_ref, rows_ref = outs
        fill_rows(rows_ref, pairs, here[1])
        total = dot(rows_ref[...], masked_ref[...])
        cubic = total[:height] * kept_ref[1]
        purified_ref[...] = (3.0 * both_ref[0].astype(jnp.float32) - 2.0 * cubic).astype(purified_ref.dtype)
        back_ref[...] = total[height:]
        scaled_ref[...] = (-2.0 * rows_ref[:height].astype(jnp.float32)).astype(scaled_ref.dtype)

    rows = (2 * height, len(both_held) * width)
    out = (
        pltpu.VMEM((height, width), both.dtype),
        pltpu.VMEM((height, width), jnp.float32),
        pltpu.VMEM((height, rows[1]), both.dtype),
    )
    scratch = [pltpu.VMEM(rows, both.dtype)]
    return call(kernel, "purify_step", (both, kept, masked_cols), [], both_held, out, scratch, hint=EARLY)


def last_step(kept, purified, back, pair_rows, scaled_rows, grad_blocks, filtered_blocks):
    height, width = back.shape
    n_row = len(grad_blocks)

    def kernel(here, fixed, blocks, pairs, outs):
        kept_ref, purified_ref, back_ref, pair_ref, scaled_ref = fixed
        out_ref, gradient_ref, late_cols = outs
        out_ref[...] = purified_ref[...]
        for i, (at, block) in enumerate(blocks):
            part(late_cols.at[i // n_row], here[0] ^ at, height)[...] = block[...]
        summed = back_ref[...] + dot(pair_ref[:height], late_cols[0])
        summed = summed + dot(scaled_ref[...], late_cols[1])
        gradient_ref[...] = (summed * kept_ref[0]).astype(gradient_ref.dtype)

    out = jax.ShapeDtypeStruct((height, width), purified.dtype)
    scratch = [pltpu.VMEM((2, n_row * height, width), purified.dtype)]
    fixed = (kept, purified, back, pair_rows, scaled_rows)
    return call(kernel, "last_step", fixed, grad_blocks + filtered_blocks, [], (out, out), scratch)


def take(held, *inner):
    return [(at, (array, (k,) + inner)) for ats, array in held for k, at in enumerate(ats)]


def cut(held, k):
    return [(ats, array[:, k]) for ats, array in held]


def pairs_of(one, two):
    return [(ats, jnp.stack([first, second], 1)) for (ats, first), (_, second) in zip(one, two)]


def across_cores(lists, n_row):
    ats = [[at for ats, _ in held for at in ats] for held in lists]
    assert all(sorted(a) == sorted(ats[0]) for a in ats)
    flips = flips_of(n_row)[-1:]
    sent = jnp.stack([jnp.concatenate([array for _, array in held]) for held in lists])
    got = [lax.ppermute(sent, "row", [(i, i ^ flip) for i in range(n_row)]) for flip in flips]
    return [
        take(held) + [(at ^ flip, (array, (k, i))) for flip, array in zip(flips, got) for i, at in enumerate(own)]
        for k, (held, own) in enumerate(zip(lists, ats))
    ]


def on_device(n_row, n_col, density, cotangent, block_pattern, filter_pattern):
    chip_flips = flips_of(n_row)[:-1]
    lead, first, second = chip_flips[:-2], chip_flips[-2:-1], chip_flips[-1:]
    pair, kept = mask(density, cotangent, block_pattern, filter_pattern)

    own = double([([0], pair[None])], "row", n_row, lead)
    masked, filtered = cut(own, 0), cut(own, 1)
    pair_held, later = exchange(pair, "col", n_col, True, filtered)
    far = swap(masked, "row", n_row, first)
    near = swap(masked, "row", n_row, second)
    masked = masked + far + near + swap(far, "row", n_row, second)
    other = swap(later, "row", n_row, second)
    (masked_blocks,) = across_cores([masked], n_row)
    both, masked_cols, pair_rows = square_step(pair, kept, masked_blocks, pair_held)

    both_held, _ = exchange(both, "col", n_col, False)
    grad = double([([0], both[1:])], "row", n_row, lead)
    far = swap(grad, "row", n_row, second)
    left = swap(pairs_of(grad, filtered), "row", n_row, first)
    right = swap(pairs_of(far, other), "row", n_row, first)
    grad = grad + far + cut(left, 0) + cut(right, 0)
    filtered = filtered + other + cut(left, 1) + cut(right, 1)
    grad_blocks, filtered_blocks = across_cores([grad, filtered], n_row)
    purified, back, scaled_rows = purify_step(both, kept, masked_cols, both_held)
    return last_step(kept, purified, back, pair_rows, scaled_rows, grad_blocks, filtered_blocks)


def solution(mesh):
    placed = (P("row", "col"), P("row", "col"), P("row", "col"), P("row", "col"))

    def local(*arrays):
        return on_device(mesh.shape["row"], mesh.shape["col"], *arrays)

    return jax.shard_map(
        local,
        mesh=mesh,
        in_specs=placed,
        out_specs=(P("row", "col"), P("row", "col")),
        check_vma=False,
    )
```

```python
import jax
import jax.numpy as jnp
from jax import lax
from jax.experimental import pallas as pl
from jax.experimental.pallas import tpu as pltpu
from jax.sharding import PartitionSpec as P

IN_HBM = pl.BlockSpec(memory_space=pltpu.HBM)
IN_VMEM = pl.BlockSpec(memory_space=pltpu.VMEM)
LIMIT = pltpu.CompilerParams(vmem_limit_bytes=32 * 1024 * 1024)
EARLY = pl.CostEstimate(flops=6_000_000_000, bytes_accessed=0, transcendentals=0)


def dot(a, b):
    return jnp.dot(a, b, preferred_element_type=jnp.float32)


def mask(density, cotangent, block_pattern, filter_pattern):
    height, width = density.shape
    block_size = height // block_pattern.shape[0]

    def kernel(*refs):
        pattern_refs, dense_refs = refs[:2], refs[2:4]
        pair_ref, kept_ref, pattern_held, dense_held, sems = refs[4:]
        copies = []
        for k in range(2):
            copies.append(pltpu.make_async_copy(pattern_refs[k], pattern_held.at[k], sems.at[k]))
            copies.append(pltpu.make_async_copy(dense_refs[k], dense_held.at[k], sems.at[2 + k]))
        for copy in copies:
            copy.start()
        for copy in copies:
            copy.wait()
        lane = lax.broadcasted_iota(jnp.int32, (block_size, width), 1) // block_size
        for k in range(2):
            for i in range(height // block_size):
                rows = pl.ds(i * block_size, block_size)
                kept = jnp.zeros((block_size, width), jnp.float32)
                for j in range(width // block_size):
                    kept = jnp.where(lane == j, pattern_held[k, i, j].astype(jnp.float32), kept)
                kept_ref[k, rows, :] = kept
                pair_ref[k, rows, :] = (dense_held[k, rows, :].astype(jnp.float32) * kept).astype(pair_ref.dtype)

    inputs = (block_pattern, filter_pattern, density, cotangent)
    return pl.pallas_call(
        kernel,
        out_shape=(
            pltpu.VMEM((2, height, width), density.dtype),
            pltpu.VMEM((2, height, width), jnp.float32),
        ),
        in_specs=[IN_HBM] * 4,
        out_specs=(IN_VMEM, IN_VMEM),
        scratch_shapes=[
            pltpu.SMEM((2,) + block_pattern.shape, jnp.int32),
            pltpu.VMEM((2, height, width), density.dtype),
            pltpu.SemaphoreType.DMA((4,)),
        ],
        compiler_params=LIMIT,
        name="mask",
    )(*(pltpu.with_memory_space_constraint(x, pltpu.HBM) for x in inputs))


def settle(block):
    def kernel(block_ref, out_ref):
        out_ref[...] = block_ref[...]

    return pl.pallas_call(
        kernel,
        out_shape=pltpu.VMEM(block.shape, block.dtype),
        in_specs=[IN_VMEM],
        out_specs=IN_VMEM,
        cost_estimate=EARLY,
        compiler_params=LIMIT,
        name="settle",
    )(block)


def flips_of(size):
    flips = []
    while 2 ** len(flips) < size:
        flips.insert(0, 2 ** len(flips))
    return flips


def swap(held, axis_name, size, flips):
    return [
        ([at ^ flip for at in ats], lax.ppermute(blocks, axis_name, [(i, i ^ flip) for i in range(size)]))
        for flip in flips
        for ats, blocks in held
    ]


def double(held, axis_name, size, flips):
    for flip in flips:
        ats = [at for entry in held for at in entry[0]]
        blocks = held[0][1] if len(held) == 1 else jnp.concatenate([entry[1] for entry in held])
        held = held + swap([(ats, blocks)], axis_name, size, [flip])
    return held


def forward(held, axis_name, size, flips):
    held = double(held, axis_name, size, flips[:-2])
    far = swap(held, axis_name, size, flips[-2:-1])
    near = swap(held, axis_name, size, flips[-1:])
    return held + far + near + swap(far, axis_name, size, flips[-1:])


def tie(helds):
    arrays = lax.optimization_barrier([[blocks for _, blocks in held] for held in helds])
    return [[(ats, block) for (ats, _), block in zip(held, blocks)] for held, blocks in zip(helds, arrays)]


def exchange(pair, axis_name, size, settled, later=()):
    flips = flips_of(size)
    held = double([([0], pair[None])], axis_name, size, flips[:-2])
    far = swap(held, axis_name, size, flips[-2:-1])
    near = swap(held, axis_name, size, flips[-1:])
    far, near = tie([far, near])
    _, later = tie([far, later])
    last = swap(far, axis_name, size, flips[-1:])
    if settled:
        last = [(ats, settle(pairs)) for ats, pairs in last]
    held = held + far + near + last
    return [(at, ((pairs, (k, 0)), (pairs, (k, 1)))) for ats, pairs in held for k, at in enumerate(ats)], later


def part(ref, owner, size):
    return ref.at[pl.ds(pl.multiple_of(owner * size, size), size), :]


def settle(block):
    def kernel(block_ref, out_ref):
        out_ref[...] = block_ref[...]

    return pl.pallas_call(
        kernel,
        out_shape=pltpu.VMEM(block.shape, block.dtype),
        in_specs=[IN_VMEM],
        out_specs=IN_VMEM,
        cost_estimate=EARLY,
        compiler_params=LIMIT,
        name="settle",
    )(block)


def call(kernel, name, fixed, blocks, pairs, out_shape, scratch=(), hint=None):
    arrays, places = [*fixed], {}
    for array, _ in [block for _, block in blocks] + [block for _, two in pairs for block in two]:
        if id(array) not in places:
            places[id(array)] = len(arrays)
            arrays.append(array)

    def body(*refs):
        def ref_of(block):
            return refs[places[id(block[0])]].at[block[1]]

        here = (lax.axis_index("row"), lax.axis_index("col"))
        block_refs = [(at, ref_of(block)) for at, block in blocks]
        pair_refs = [(at, [ref_of(block) for block in two]) for at, two in pairs]
        kernel(here, refs[:len(fixed)], block_refs, pair_refs, refs[len(arrays):])

    return pl.pallas_call(
        body,
        out_shape=out_shape,
        in_specs=[IN_VMEM] * len(arrays),
        out_specs=jax.tree.map(lambda _: IN_VMEM, out_shape),
        scratch_shapes=scratch,
        cost_estimate=hint,
        compiler_params=LIMIT,
        name=name,
    )(*arrays)


def fill_rows(rows_ref, pieces, here_col):
    height, width = rows_ref.shape[0] // 2, rows_ref.shape[1] // len(pieces)
    for at, blocks in pieces:
        columns = pl.ds(pl.multiple_of((here_col ^ at) * width, width), width)
        for k in range(2):
            rows_ref[k * height:(k + 1) * height, columns] = blocks[k][...]


def square_step(pair, kept, masked_blocks, pair_held):
    _, height, width = pair.shape
    n_row = len(masked_blocks)

    def kernel(here, fixed, blocks, pairs, outs):
        pair_ref, kept_ref = fixed
        both_ref, masked_ref, rows_ref = outs
        fill_rows(rows_ref, pairs, here[1])
        for at, block in blocks:
            part(masked_ref, here[0] ^ at, height)[...] = block[...]
        total = dot(rows_ref[...], masked_ref[...])
        both_ref[0] = (total[:height] * kept_ref[1]).astype(both_ref.dtype)
        grad = 3.0 * pair_ref[1].astype(jnp.float32) - 2.0 * total[height:]
        both_ref[1] = (grad * kept_ref[1]).astype(both_ref.dtype)

    out = (
        pltpu.VMEM((2, height, width), pair.dtype),
        pltpu.VMEM((n_row * height, width), pair.dtype),
        pltpu.VMEM((2 * height, len(pair_held) * width), pair.dtype),
    )
    return call(kernel, "square_step", (pair, kept), masked_blocks, pair_held, out)


def last_step(both, kept, masked_cols, pair_rows, both_held, grad_blocks, filtered_blocks):
    _, height, width = both.shape
    n_row = len(grad_blocks)

    def kernel(here, fixed, blocks, pairs, outs):
        both_ref, kept_ref, masked_ref, pair_ref = fixed
        purified_ref, gradient_ref, rows_ref, late_cols = outs
        fill_rows(rows_ref, pairs, here[1])
        for i, (at, block) in enumerate(blocks):
            part(late_cols.at[i // n_row], here[0] ^ at, height)[...] = block[...]
        total = dot(rows_ref[...], masked_ref[...])
        cubic = total[:height] * kept_ref[1]
        purified_ref[...] = (3.0 * both_ref[0].astype(jnp.float32) - 2.0 * cubic).astype(purified_ref.dtype)
        summed = total[height:] + dot(pair_ref[:height], late_cols[0])
        summed = summed - 2.0 * dot(rows_ref[:height], late_cols[1])
        gradient_ref[...] = (summed * kept_ref[0]).astype(gradient_ref.dtype)

    out = jax.ShapeDtypeStruct((height, width), both.dtype)
    scratch = [
        pltpu.VMEM((2 * height, len(both_held) * width), both.dtype),
        pltpu.VMEM((2, n_row * height, width), both.dtype),
    ]
    fixed = (both, kept, masked_cols, pair_rows)
    return call(kernel, "last_step", fixed, grad_blocks + filtered_blocks, both_held, (out, out), scratch)


def take(held, *inner):
    return [(at, (array, (k,) + inner)) for ats, array in held for k, at in enumerate(ats)]


def cut(held, k):
    return [(ats, array[:, k]) for ats, array in held]


def pairs_of(one, two):
    return [(ats, jnp.stack([first, second], 1)) for (ats, first), (_, second) in zip(one, two)]


def across_cores(lists, n_row):
    ats = [[at for ats, _ in held for at in ats] for held in lists]
    assert all(sorted(a) == sorted(ats[0]) for a in ats)
    flips = flips_of(n_row)[-1:]
    sent = jnp.stack([jnp.concatenate([array for _, array in held]) for held in lists])
    got = [lax.ppermute(sent, "row", [(i, i ^ flip) for i in range(n_row)]) for flip in flips]
    return [
        take(held) + [(at ^ flip, (array, (k, i))) for flip, array in zip(flips, got) for i, at in enumerate(own)]
        for k, (held, own) in enumerate(zip(lists, ats))
    ]


def on_device(n_row, n_col, density, cotangent, block_pattern, filter_pattern):
    chip_flips = flips_of(n_row)[:-1]
    lead, first, second = chip_flips[:-2], chip_flips[-2:-1], chip_flips[-1:]
    pair, kept = mask(density, cotangent, block_pattern, filter_pattern)

    own = double([([0], pair[None])], "row", n_row, lead)
    masked, filtered = cut(own, 0), cut(own, 1)
    pair_held, later = exchange(pair, "col", n_col, True, filtered)
    far = swap(masked, "row", n_row, first)
    near = swap(masked, "row", n_row, second)
    masked = masked + far + near + swap(far, "row", n_row, second)
    other = swap(later, "row", n_row, second)
    (masked_blocks,) = across_cores([masked], n_row)
    both, masked_cols, pair_rows = square_step(pair, kept, masked_blocks, pair_held)

    both_held, _ = exchange(both, "col", n_col, True)
    grad = double([([0], both[1:])], "row", n_row, lead)
    far = swap(grad, "row", n_row, second)
    left = swap(pairs_of(grad, filtered), "row", n_row, first)
    right = swap(pairs_of(far, other), "row", n_row, first)
    grad = grad + far + cut(left, 0) + cut(right, 0)
    filtered = filtered + other + cut(left, 1) + cut(right, 1)
    grad_blocks, filtered_blocks = across_cores([grad, filtered], n_row)
    return last_step(both, kept, masked_cols, pair_rows, both_held, grad_blocks, filtered_blocks)


def solution(mesh):
    placed = (P("row", "col"), P("row", "col"), P("row", "col"), P("row", "col"))

    def local(*arrays):
        return on_device(mesh.shape["row"], mesh.shape["col"], *arrays)

    return jax.shard_map(
        local,
        mesh=mesh,
        in_specs=placed,
        out_specs=(P("row", "col"), P("row", "col")),
        check_vma=False,
    )
```

```python
import jax
import jax.numpy as jnp
from jax import lax
from jax.experimental import pallas as pl
from jax.experimental.pallas import tpu as pltpu
from jax.sharding import PartitionSpec as P

IN_HBM = pl.BlockSpec(memory_space=pltpu.HBM)
IN_VMEM = pl.BlockSpec(memory_space=pltpu.VMEM)
SOON = pl.CostEstimate(flops=100_000_000, bytes_accessed=0, transcendentals=0)
LIMIT = pltpu.CompilerParams(vmem_limit_bytes=32 * 1024 * 1024)
EARLY = pl.CostEstimate(flops=6_000_000_000, bytes_accessed=0, transcendentals=0)


def dot(a, b):
    return jnp.dot(a, b, preferred_element_type=jnp.float32)


def mask(density, cotangent, block_pattern, filter_pattern):
    height, width = density.shape
    block_size = height // block_pattern.shape[0]

    def kernel(*refs):
        pattern_refs, dense_refs = refs[:2], refs[2:4]
        pair_ref, kept_ref, pattern_held, dense_held, sems = refs[4:]
        copies = []
        for k in range(2):
            copies.append(pltpu.make_async_copy(pattern_refs[k], pattern_held.at[k], sems.at[k]))
            copies.append(pltpu.make_async_copy(dense_refs[k], dense_held.at[k], sems.at[2 + k]))
        for copy in copies:
            copy.start()
        for copy in copies:
            copy.wait()
        lane = lax.broadcasted_iota(jnp.int32, (block_size, width), 1) // block_size
        for k in range(2):
            for i in range(height // block_size):
                rows = pl.ds(i * block_size, block_size)
                kept = jnp.zeros((block_size, width), jnp.float32)
                for j in range(width // block_size):
                    kept = jnp.where(lane == j, pattern_held[k, i, j].astype(jnp.float32), kept)
                kept_ref[k, rows, :] = kept
                pair_ref[k, rows, :] = (dense_held[k, rows, :].astype(jnp.float32) * kept).astype(pair_ref.dtype)

    inputs = (block_pattern, filter_pattern, density, cotangent)
    return pl.pallas_call(
        kernel,
        out_shape=(
            pltpu.VMEM((2, height, width), density.dtype),
            pltpu.VMEM((2, height, width), jnp.float32),
        ),
        in_specs=[IN_HBM] * 4,
        out_specs=(IN_VMEM, IN_VMEM),
        scratch_shapes=[
            pltpu.SMEM((2,) + block_pattern.shape, jnp.int32),
            pltpu.VMEM((2, height, width), density.dtype),
            pltpu.SemaphoreType.DMA((4,)),
        ],
        compiler_params=LIMIT,
        name="mask",
    )(*(pltpu.with_memory_space_constraint(x, pltpu.HBM) for x in inputs))


def settle(block, hint):
    def kernel(block_ref, out_ref):
        out_ref[...] = block_ref[...]

    return pl.pallas_call(
        kernel,
        out_shape=pltpu.VMEM(block.shape, block.dtype),
        in_specs=[IN_VMEM],
        out_specs=IN_VMEM,
        cost_estimate=hint,
        compiler_params=LIMIT,
        name="settle",
    )(block)


def flips_of(size):
    flips = []
    while 2 ** len(flips) < size:
        flips.insert(0, 2 ** len(flips))
    return flips


def swap(held, axis_name, size, flips):
    return [
        ([at ^ flip for at in ats], lax.ppermute(blocks, axis_name, [(i, i ^ flip) for i in range(size)]))
        for flip in flips
        for ats, blocks in held
    ]


def double(held, axis_name, size, flips):
    for flip in flips:
        ats = [at for entry in held for at in entry[0]]
        blocks = held[0][1] if len(held) == 1 else jnp.concatenate([entry[1] for entry in held])
        held = held + swap([(ats, blocks)], axis_name, size, [flip])
    return held


def forward(held, axis_name, size, flips):
    held = double(held, axis_name, size, flips[:-2])
    far = swap(held, axis_name, size, flips[-2:-1])
    near = swap(held, axis_name, size, flips[-1:])
    return held + far + near + swap(far, axis_name, size, flips[-1:])


def tie(helds):
    arrays = lax.optimization_barrier([[blocks for _, blocks in held] for held in helds])
    return [[(ats, block) for (ats, _), block in zip(held, blocks)] for held, blocks in zip(helds, arrays)]


def exchange(pair, axis_name, size, tied, later=()):
    flips = flips_of(size)
    held = double([([0], pair[None])], axis_name, size, flips[:-2])
    far = swap(held, axis_name, size, flips[-2:-1])
    near = swap(held, axis_name, size, flips[-1:])
    if tied:
        far, near = tie([far, near])
    else:
        near = [(ats, settle(pairs, SOON)) for ats, pairs in near]
    _, later = tie([far, later])
    last = swap(far, axis_name, size, flips[-1:])
    last = [(ats, settle(pairs, EARLY)) for ats, pairs in last]
    held = held + far + near + last
    return [(at, ((pairs, (k, 0)), (pairs, (k, 1)))) for ats, pairs in held for k, at in enumerate(ats)], later


def part(ref, owner, size):
    return ref.at[pl.ds(pl.multiple_of(owner * size, size), size), :]


def settle(block, hint):
    def kernel(block_ref, out_ref):
        out_ref[...] = block_ref[...]

    return pl.pallas_call(
        kernel,
        out_shape=pltpu.VMEM(block.shape, block.dtype),
        in_specs=[IN_VMEM],
        out_specs=IN_VMEM,
        cost_estimate=hint,
        compiler_params=LIMIT,
        name="settle",
    )(block)


def call(kernel, name, fixed, blocks, pairs, out_shape, scratch=(), hint=None):
    arrays, places = [*fixed], {}
    for array, _ in [block for _, block in blocks] + [block for _, two in pairs for block in two]:
        if id(array) not in places:
            places[id(array)] = len(arrays)
            arrays.append(array)

    def body(*refs):
        def ref_of(block):
            return refs[places[id(block[0])]].at[block[1]]

        here = (lax.axis_index("row"), lax.axis_index("col"))
        block_refs = [(at, ref_of(block)) for at, block in blocks]
        pair_refs = [(at, [ref_of(block) for block in two]) for at, two in pairs]
        kernel(here, refs[:len(fixed)], block_refs, pair_refs, refs[len(arrays):])

    return pl.pallas_call(
        body,
        out_shape=out_shape,
        in_specs=[IN_VMEM] * len(arrays),
        out_specs=jax.tree.map(lambda _: IN_VMEM, out_shape),
        scratch_shapes=scratch,
        cost_estimate=hint,
        compiler_params=LIMIT,
        name=name,
    )(*arrays)


def fill_rows(rows_ref, pieces, here_col):
    height, width = rows_ref.shape[0] // 2, rows_ref.shape[1] // len(pieces)
    for at, blocks in pieces:
        columns = pl.ds(pl.multiple_of((here_col ^ at) * width, width), width)
        for k in range(2):
            rows_ref[k * height:(k + 1) * height, columns] = blocks[k][...]


def square_step(pair, kept, masked_blocks, pair_held):
    _, height, width = pair.shape
    n_row = len(masked_blocks)

    def kernel(here, fixed, blocks, pairs, outs):
        pair_ref, kept_ref = fixed
        both_ref, masked_ref, rows_ref = outs
        fill_rows(rows_ref, pairs, here[1])
        for at, block in blocks:
            part(masked_ref, here[0] ^ at, height)[...] = block[...]
        total = dot(rows_ref[...], masked_ref[...])
        both_ref[0] = (total[:height] * kept_ref[1]).astype(both_ref.dtype)
        grad = 3.0 * pair_ref[1].astype(jnp.float32) - 2.0 * total[height:]
        both_ref[1] = (grad * kept_ref[1]).astype(both_ref.dtype)

    out = (
        pltpu.VMEM((2, height, width), pair.dtype),
        pltpu.VMEM((n_row * height, width), pair.dtype),
        pltpu.VMEM((2 * height, len(pair_held) * width), pair.dtype),
    )
    return call(kernel, "square_step", (pair, kept), masked_blocks, pair_held, out)


def last_step(both, kept, masked_cols, pair_rows, both_held, grad_blocks, filtered_blocks):
    _, height, width = both.shape
    n_row = len(grad_blocks)

    def kernel(here, fixed, blocks, pairs, outs):
        both_ref, kept_ref, masked_ref, pair_ref = fixed
        purified_ref, gradient_ref, rows_ref, late_cols = outs
        fill_rows(rows_ref, pairs, here[1])
        for i, (at, block) in enumerate(blocks):
            part(late_cols.at[i // n_row], here[0] ^ at, height)[...] = block[...]
        total = dot(rows_ref[...], masked_ref[...])
        cubic = total[:height] * kept_ref[1]
        purified_ref[...] = (3.0 * both_ref[0].astype(jnp.float32) - 2.0 * cubic).astype(purified_ref.dtype)
        summed = total[height:] + dot(pair_ref[:height], late_cols[0])
        summed = summed - 2.0 * dot(rows_ref[:height], late_cols[1])
        gradient_ref[...] = (summed * kept_ref[0]).astype(gradient_ref.dtype)

    out = jax.ShapeDtypeStruct((height, width), both.dtype)
    scratch = [
        pltpu.VMEM((2 * height, len(both_held) * width), both.dtype),
        pltpu.VMEM((2, n_row * height, width), both.dtype),
    ]
    fixed = (both, kept, masked_cols, pair_rows)
    return call(kernel, "last_step", fixed, grad_blocks + filtered_blocks, both_held, (out, out), scratch)


def take(held, *inner):
    return [(at, (array, (k,) + inner)) for ats, array in held for k, at in enumerate(ats)]


def cut(held, k):
    return [(ats, array[:, k]) for ats, array in held]


def pairs_of(one, two):
    return [(ats, jnp.stack([first, second], 1)) for (ats, first), (_, second) in zip(one, two)]


def across_cores(lists, n_row):
    ats = [[at for ats, _ in held for at in ats] for held in lists]
    assert all(sorted(a) == sorted(ats[0]) for a in ats)
    flips = flips_of(n_row)[-1:]
    sent = jnp.stack([jnp.concatenate([array for _, array in held]) for held in lists])
    got = [lax.ppermute(sent, "row", [(i, i ^ flip) for i in range(n_row)]) for flip in flips]
    return [
        take(held) + [(at ^ flip, (array, (k, i))) for flip, array in zip(flips, got) for i, at in enumerate(own)]
        for k, (held, own) in enumerate(zip(lists, ats))
    ]


def on_device(n_row, n_col, density, cotangent, block_pattern, filter_pattern):
    chip_flips = flips_of(n_row)[:-1]
    lead, first, second = chip_flips[:-2], chip_flips[-2:-1], chip_flips[-1:]
    pair, kept = mask(density, cotangent, block_pattern, filter_pattern)

    own = double([([0], pair[None])], "row", n_row, lead)
    masked, filtered = cut(own, 0), cut(own, 1)
    pair_held, later = exchange(pair, "col", n_col, False, filtered)
    far = swap(masked, "row", n_row, first)
    near = swap(masked, "row", n_row, second)
    masked = masked + far + near + swap(far, "row", n_row, second)
    other = swap(later, "row", n_row, second)
    (masked_blocks,) = across_cores([masked], n_row)
    both, masked_cols, pair_rows = square_step(pair, kept, masked_blocks, pair_held)

    both_held, _ = exchange(both, "col", n_col, True)
    grad = double([([0], both[1:])], "row", n_row, lead)
    far = swap(grad, "row", n_row, second)
    left = swap(pairs_of(grad, filtered), "row", n_row, first)
    right = swap(pairs_of(far, other), "row", n_row, first)
    grad = grad + far + cut(left, 0) + cut(right, 0)
    filtered = filtered + other + cut(left, 1) + cut(right, 1)
    grad_blocks, filtered_blocks = across_cores([grad, filtered], n_row)
    return last_step(both, kept, masked_cols, pair_rows, both_held, grad_blocks, filtered_blocks)


def solution(mesh):
    placed = (P("row", "col"), P("row", "col"), P("row", "col"), P("row", "col"))

    def local(*arrays):
        return on_device(mesh.shape["row"], mesh.shape["col"], *arrays)

    return jax.shard_map(
        local,
        mesh=mesh,
        in_specs=placed,
        out_specs=(P("row", "col"), P("row", "col")),
        check_vma=False,
    )
```

```python
import jax
import jax.numpy as jnp
from jax import lax
from jax.experimental import pallas as pl
from jax.experimental.pallas import tpu as pltpu
from jax.sharding import PartitionSpec as P

IN_HBM = pl.BlockSpec(memory_space=pltpu.HBM)
IN_VMEM = pl.BlockSpec(memory_space=pltpu.VMEM)
SOON = pl.CostEstimate(flops=100_000_000, bytes_accessed=0, transcendentals=0)
LIMIT = pltpu.CompilerParams(vmem_limit_bytes=32 * 1024 * 1024)
EARLY = pl.CostEstimate(flops=6_000_000_000, bytes_accessed=0, transcendentals=0)


def dot(a, b):
    return jnp.dot(a, b, preferred_element_type=jnp.float32)


def mask(density, cotangent, block_pattern, filter_pattern):
    height, width = density.shape
    block_size = height // block_pattern.shape[0]

    def kernel(*refs):
        pattern_refs, dense_refs = refs[:2], refs[2:4]
        pair_ref, kept_ref, pattern_held, dense_held, sems = refs[4:]
        copies = []
        for k in range(2):
            copies.append(pltpu.make_async_copy(pattern_refs[k], pattern_held.at[k], sems.at[k]))
            copies.append(pltpu.make_async_copy(dense_refs[k], dense_held.at[k], sems.at[2 + k]))
        for copy in copies:
            copy.start()
        for copy in copies:
            copy.wait()
        lane = lax.broadcasted_iota(jnp.int32, (block_size, width), 1) // block_size
        for k in range(2):
            for i in range(height // block_size):
                rows = pl.ds(i * block_size, block_size)
                kept = jnp.zeros((block_size, width), jnp.float32)
                for j in range(width // block_size):
                    kept = jnp.where(lane == j, pattern_held[k, i, j].astype(jnp.float32), kept)
                kept_ref[k, rows, :] = kept
                pair_ref[k, rows, :] = (dense_held[k, rows, :].astype(jnp.float32) * kept).astype(pair_ref.dtype)

    inputs = (block_pattern, filter_pattern, density, cotangent)
    return pl.pallas_call(
        kernel,
        out_shape=(
            pltpu.VMEM((2, height, width), density.dtype),
            pltpu.VMEM((2, height, width), jnp.float32),
        ),
        in_specs=[IN_HBM] * 4,
        out_specs=(IN_VMEM, IN_VMEM),
        scratch_shapes=[
            pltpu.SMEM((2,) + block_pattern.shape, jnp.int32),
            pltpu.VMEM((2, height, width), density.dtype),
            pltpu.SemaphoreType.DMA((4,)),
        ],
        compiler_params=LIMIT,
        name="mask",
    )(*(pltpu.with_memory_space_constraint(x, pltpu.HBM) for x in inputs))


def settle(block, hint):
    def kernel(block_ref, out_ref):
        out_ref[...] = block_ref[...]

    return pl.pallas_call(
        kernel,
        out_shape=pltpu.VMEM(block.shape, block.dtype),
        in_specs=[IN_VMEM],
        out_specs=IN_VMEM,
        cost_estimate=hint,
        compiler_params=LIMIT,
        name="settle",
    )(block)


def flips_of(size):
    flips = []
    while 2 ** len(flips) < size:
        flips.insert(0, 2 ** len(flips))
    return flips


def swap(held, axis_name, size, flips):
    return [
        ([at ^ flip for at in ats], lax.ppermute(blocks, axis_name, [(i, i ^ flip) for i in range(size)]))
        for flip in flips
        for ats, blocks in held
    ]


def double(held, axis_name, size, flips):
    for flip in flips:
        ats = [at for entry in held for at in entry[0]]
        blocks = held[0][1] if len(held) == 1 else jnp.concatenate([entry[1] for entry in held])
        held = held + swap([(ats, blocks)], axis_name, size, [flip])
    return held


def forward(held, axis_name, size, flips):
    held = double(held, axis_name, size, flips[:-2])
    far = swap(held, axis_name, size, flips[-2:-1])
    near = swap(held, axis_name, size, flips[-1:])
    return held + far + near + swap(far, axis_name, size, flips[-1:])


def tie(helds):
    arrays = lax.optimization_barrier([[blocks for _, blocks in held] for held in helds])
    return [[(ats, block) for (ats, _), block in zip(held, blocks)] for held, blocks in zip(helds, arrays)]


def exchange(pair, axis_name, size, tied, later=()):
    flips = flips_of(size)
    held = double([([0], pair[None])], axis_name, size, flips[:-2])
    far = swap(held, axis_name, size, flips[-2:-1])
    near = swap(held, axis_name, size, flips[-1:])
    if tied:
        far, near = tie([far, near])
    else:
        near = [(ats, settle(pairs, SOON)) for ats, pairs in near]
    _, later = tie([far, later])
    last = swap(far, axis_name, size, flips[-1:])
    last = [(ats, settle(pairs, EARLY)) for ats, pairs in last]
    held = held + far + near + last
    return [(at, ((pairs, (k, 0)), (pairs, (k, 1)))) for ats, pairs in held for k, at in enumerate(ats)], later


def part(ref, owner, size):
    return ref.at[pl.ds(pl.multiple_of(owner * size, size), size), :]


def settle(block, hint):
    def kernel(block_ref, out_ref):
        out_ref[...] = block_ref[...]

    return pl.pallas_call(
        kernel,
        out_shape=pltpu.VMEM(block.shape, block.dtype),
        in_specs=[IN_VMEM],
        out_specs=IN_VMEM,
        cost_estimate=hint,
        compiler_params=LIMIT,
        name="settle",
    )(block)


def call(kernel, name, fixed, blocks, pairs, out_shape, scratch=(), hint=None):
    arrays, places = [*fixed], {}
    for array, _ in [block for _, block in blocks] + [block for _, two in pairs for block in two]:
        if id(array) not in places:
            places[id(array)] = len(arrays)
            arrays.append(array)

    def body(*refs):
        def ref_of(block):
            return refs[places[id(block[0])]].at[block[1]]

        here = (lax.axis_index("row"), lax.axis_index("col"))
        block_refs = [(at, ref_of(block)) for at, block in blocks]
        pair_refs = [(at, [ref_of(block) for block in two]) for at, two in pairs]
        kernel(here, refs[:len(fixed)], block_refs, pair_refs, refs[len(arrays):])

    return pl.pallas_call(
        body,
        out_shape=out_shape,
        in_specs=[IN_VMEM] * len(arrays),
        out_specs=jax.tree.map(lambda _: IN_VMEM, out_shape),
        scratch_shapes=scratch,
        cost_estimate=hint,
        compiler_params=LIMIT,
        name=name,
    )(*arrays)


def fill_rows(rows_ref, pieces, here_col):
    height, width = rows_ref.shape[0] // 2, rows_ref.shape[1] // len(pieces)
    for at, blocks in pieces:
        columns = pl.ds(pl.multiple_of((here_col ^ at) * width, width), width)
        for k in range(2):
            rows_ref[k * height:(k + 1) * height, columns] = blocks[k][...]


def square_step(pair, kept, masked_blocks, pair_held):
    _, height, width = pair.shape
    n_row = len(masked_blocks)

    def kernel(here, fixed, blocks, pairs, outs):
        pair_ref, kept_ref = fixed
        both_ref, masked_ref, rows_ref = outs
        fill_rows(rows_ref, pairs, here[1])
        for at, block in blocks:
            part(masked_ref, here[0] ^ at, height)[...] = block[...]
        total = dot(rows_ref[...], masked_ref[...])
        both_ref[0] = (total[:height] * kept_ref[1]).astype(both_ref.dtype)
        grad = 3.0 * pair_ref[1].astype(jnp.float32) - 2.0 * total[height:]
        both_ref[1] = (grad * kept_ref[1]).astype(both_ref.dtype)

    out = (
        pltpu.VMEM((2, height, width), pair.dtype),
        pltpu.VMEM((n_row * height, width), pair.dtype),
        pltpu.VMEM((2 * height, len(pair_held) * width), pair.dtype),
    )
    return call(kernel, "square_step", (pair, kept), masked_blocks, pair_held, out)


def last_step(both, kept, masked_cols, pair_rows, both_held, grad_blocks, filtered_blocks):
    _, height, width = both.shape
    n_row = len(grad_blocks)

    def kernel(here, fixed, blocks, pairs, outs):
        both_ref, kept_ref, masked_ref, pair_ref = fixed
        purified_ref, gradient_ref, rows_ref, late_cols = outs
        fill_rows(rows_ref, pairs, here[1])
        for i, (at, block) in enumerate(blocks):
            part(late_cols.at[i // n_row], here[0] ^ at, height)[...] = block[...]
        total = dot(rows_ref[...], masked_ref[...])
        cubic = total[:height] * kept_ref[1]
        purified_ref[...] = (3.0 * both_ref[0].astype(jnp.float32) - 2.0 * cubic).astype(purified_ref.dtype)
        summed = total[height:] + dot(pair_ref[:height], late_cols[0])
        summed = summed - 2.0 * dot(rows_ref[:height], late_cols[1])
        gradient_ref[...] = (summed * kept_ref[0]).astype(gradient_ref.dtype)

    out = jax.ShapeDtypeStruct((height, width), both.dtype)
    scratch = [
        pltpu.VMEM((2 * height, len(both_held) * width), both.dtype),
        pltpu.VMEM((2, n_row * height, width), both.dtype),
    ]
    fixed = (both, kept, masked_cols, pair_rows)
    return call(kernel, "last_step", fixed, grad_blocks + filtered_blocks, both_held, (out, out), scratch)


def take(held, *inner):
    return [(at, (array, (k,) + inner)) for ats, array in held for k, at in enumerate(ats)]


def cut(held, k):
    return [(ats, array[:, k]) for ats, array in held]


def pairs_of(one, two):
    return [(ats, jnp.stack([first, second], 1)) for (ats, first), (_, second) in zip(one, two)]


def across_cores(lists, n_row):
    ats = [[at for ats, _ in held for at in ats] for held in lists]
    assert all(sorted(a) == sorted(ats[0]) for a in ats)
    flips = flips_of(n_row)[-1:]
    sent = jnp.stack([jnp.concatenate([array for _, array in held]) for held in lists])
    got = [lax.ppermute(sent, "row", [(i, i ^ flip) for i in range(n_row)]) for flip in flips]
    return [
        take(held) + [(at ^ flip, (array, (k, i))) for flip, array in zip(flips, got) for i, at in enumerate(own)]
        for k, (held, own) in enumerate(zip(lists, ats))
    ]


def on_device(n_row, n_col, density, cotangent, block_pattern, filter_pattern):
    chip_flips = flips_of(n_row)[:-1]
    lead, first, second = chip_flips[:-2], chip_flips[-2:-1], chip_flips[-1:]
    pair, kept = mask(density, cotangent, block_pattern, filter_pattern)

    own = double([([0], pair[None])], "row", n_row, lead)
    masked, filtered = cut(own, 0), cut(own, 1)
    pair_held, later = exchange(pair, "col", n_col, False, filtered)
    far = swap(masked, "row", n_row, first)
    near = swap(masked, "row", n_row, second)
    masked = masked + far + near + swap(far, "row", n_row, second)
    other = swap(later, "row", n_row, second)
    (masked_blocks,) = across_cores([masked], n_row)
    both, masked_cols, pair_rows = square_step(pair, kept, masked_blocks, pair_held)

    both_held, _ = exchange(both, "col", n_col, True)
    grad = double([([0], both[1:])], "row", n_row, lead)
    far = swap(grad, "row", n_row, second)
    left = swap(pairs_of(grad, filtered), "row", n_row, first)
    right = swap(pairs_of(far, other), "row", n_row, first)
    early = across_cores([grad + far, filtered + other], n_row)
    late = across_cores([cut(left, 0) + cut(right, 0), cut(left, 1) + cut(right, 1)], n_row)
    grad_blocks, filtered_blocks = early[0] + late[0], early[1] + late[1]
    return last_step(both, kept, masked_cols, pair_rows, both_held, grad_blocks, filtered_blocks)


def solution(mesh):
    placed = (P("row", "col"), P("row", "col"), P("row", "col"), P("row", "col"))

    def local(*arrays):
        return on_device(mesh.shape["row"], mesh.shape["col"], *arrays)

    return jax.shard_map(
        local,
        mesh=mesh,
        in_specs=placed,
        out_specs=(P("row", "col"), P("row", "col")),
        check_vma=False,
    )
```

```python
import jax
import jax.numpy as jnp
from jax import lax
from jax.experimental import pallas as pl
from jax.experimental.pallas import tpu as pltpu
from jax.sharding import PartitionSpec as P

IN_HBM = pl.BlockSpec(memory_space=pltpu.HBM)
IN_VMEM = pl.BlockSpec(memory_space=pltpu.VMEM)
SOON = pl.CostEstimate(flops=100_000_000, bytes_accessed=0, transcendentals=0)
LIMIT = pltpu.CompilerParams(vmem_limit_bytes=32 * 1024 * 1024)
EARLY = pl.CostEstimate(flops=6_000_000_000, bytes_accessed=0, transcendentals=0)


def dot(a, b):
    return jnp.dot(a, b, preferred_element_type=jnp.float32)


def mask(density, cotangent, block_pattern, filter_pattern):
    height, width = density.shape
    block_size = height // block_pattern.shape[0]

    def kernel(*refs):
        pattern_refs, dense_refs = refs[:2], refs[2:4]
        pair_ref, kept_ref, pattern_held, dense_held, sems = refs[4:]
        copies = []
        for k in range(2):
            copies.append(pltpu.make_async_copy(pattern_refs[k], pattern_held.at[k], sems.at[k]))
            copies.append(pltpu.make_async_copy(dense_refs[k], dense_held.at[k], sems.at[2 + k]))
        for copy in copies:
            copy.start()
        for copy in copies:
            copy.wait()
        lane = lax.broadcasted_iota(jnp.int32, (block_size, width), 1) // block_size
        for k in range(2):
            for i in range(height // block_size):
                rows = pl.ds(i * block_size, block_size)
                kept = jnp.zeros((block_size, width), jnp.float32)
                for j in range(width // block_size):
                    kept = jnp.where(lane == j, pattern_held[k, i, j].astype(jnp.float32), kept)
                kept_ref[k, rows, :] = kept
                pair_ref[k, rows, :] = (dense_held[k, rows, :].astype(jnp.float32) * kept).astype(pair_ref.dtype)

    inputs = (block_pattern, filter_pattern, density, cotangent)
    return pl.pallas_call(
        kernel,
        out_shape=(
            pltpu.VMEM((2, height, width), density.dtype),
            pltpu.VMEM((2, height, width), jnp.float32),
        ),
        in_specs=[IN_HBM] * 4,
        out_specs=(IN_VMEM, IN_VMEM),
        scratch_shapes=[
            pltpu.SMEM((2,) + block_pattern.shape, jnp.int32),
            pltpu.VMEM((2, height, width), density.dtype),
            pltpu.SemaphoreType.DMA((4,)),
        ],
        compiler_params=LIMIT,
        name="mask",
    )(*(pltpu.with_memory_space_constraint(x, pltpu.HBM) for x in inputs))


def settle(block, hint):
    def kernel(block_ref, out_ref):
        out_ref[...] = block_ref[...]

    return pl.pallas_call(
        kernel,
        out_shape=pltpu.VMEM(block.shape, block.dtype),
        in_specs=[IN_VMEM],
        out_specs=IN_VMEM,
        cost_estimate=hint,
        compiler_params=LIMIT,
        name="settle",
    )(block)


def flips_of(size):
    flips = []
    while 2 ** len(flips) < size:
        flips.insert(0, 2 ** len(flips))
    return flips


def swap(held, axis_name, size, flips):
    return [
        ([at ^ flip for at in ats], lax.ppermute(blocks, axis_name, [(i, i ^ flip) for i in range(size)]))
        for flip in flips
        for ats, blocks in held
    ]


def double(held, axis_name, size, flips):
    for flip in flips:
        ats = [at for entry in held for at in entry[0]]
        blocks = held[0][1] if len(held) == 1 else jnp.concatenate([entry[1] for entry in held])
        held = held + swap([(ats, blocks)], axis_name, size, [flip])
    return held


def forward(held, axis_name, size, flips):
    held = double(held, axis_name, size, flips[:-2])
    far = swap(held, axis_name, size, flips[-2:-1])
    near = swap(held, axis_name, size, flips[-1:])
    return held + far + near + swap(far, axis_name, size, flips[-1:])


def tie(helds):
    arrays = lax.optimization_barrier([[blocks for _, blocks in held] for held in helds])
    return [[(ats, block) for (ats, _), block in zip(held, blocks)] for held, blocks in zip(helds, arrays)]


def exchange(pair, axis_name, size, tied, later=()):
    flips = flips_of(size)
    held = double([([0], pair[None])], axis_name, size, flips[:-2])
    far = swap(held, axis_name, size, flips[-2:-1])
    near = swap(held, axis_name, size, flips[-1:])
    if tied:
        far, near = tie([far, near])
    else:
        near = [(ats, settle(pairs, SOON)) for ats, pairs in near]
    _, later = tie([far, later])
    last = swap(far, axis_name, size, flips[-1:])
    last = [(ats, settle(pairs, EARLY)) for ats, pairs in last]
    held = held + far + near + last
    return [(at, ((pairs, (k, 0)), (pairs, (k, 1)))) for ats, pairs in held for k, at in enumerate(ats)], later


def part(ref, owner, size):
    return ref.at[pl.ds(pl.multiple_of(owner * size, size), size), :]


def settle(block, hint):
    def kernel(block_ref, out_ref):
        out_ref[...] = block_ref[...]

    return pl.pallas_call(
        kernel,
        out_shape=pltpu.VMEM(block.shape, block.dtype),
        in_specs=[IN_VMEM],
        out_specs=IN_VMEM,
        cost_estimate=hint,
        compiler_params=LIMIT,
        name="settle",
    )(block)


def call(kernel, name, fixed, blocks, pairs, out_shape, scratch=(), hint=None):
    arrays, places = [*fixed], {}
    for array, _ in [block for _, block in blocks] + [block for _, two in pairs for block in two]:
        if id(array) not in places:
            places[id(array)] = len(arrays)
            arrays.append(array)

    def body(*refs):
        def ref_of(block):
            return refs[places[id(block[0])]].at[block[1]]

        here = (lax.axis_index("row"), lax.axis_index("col"))
        block_refs = [(at, ref_of(block)) for at, block in blocks]
        pair_refs = [(at, [ref_of(block) for block in two]) for at, two in pairs]
        kernel(here, refs[:len(fixed)], block_refs, pair_refs, refs[len(arrays):])

    return pl.pallas_call(
        body,
        out_shape=out_shape,
        in_specs=[IN_VMEM] * len(arrays),
        out_specs=jax.tree.map(lambda _: IN_VMEM, out_shape),
        scratch_shapes=scratch,
        cost_estimate=hint,
        compiler_params=LIMIT,
        name=name,
    )(*arrays)


def fill_rows(rows_ref, pieces, here_col):
    height, width = rows_ref.shape[0] // 2, rows_ref.shape[1] // len(pieces)
    for at, blocks in pieces:
        columns = pl.ds(pl.multiple_of((here_col ^ at) * width, width), width)
        for k in range(2):
            rows_ref[k * height:(k + 1) * height, columns] = blocks[k][...]


def square_step(pair, kept, masked_blocks, pair_held):
    _, height, width = pair.shape
    n_row = len(masked_blocks)

    def kernel(here, fixed, blocks, pairs, outs):
        pair_ref, kept_ref = fixed
        both_ref, masked_ref, rows_ref = outs
        fill_rows(rows_ref, pairs, here[1])
        for at, block in blocks:
            part(masked_ref, here[0] ^ at, height)[...] = block[...]
        total = dot(rows_ref[...], masked_ref[...])
        both_ref[0] = (total[:height] * kept_ref[1]).astype(both_ref.dtype)
        grad = 3.0 * pair_ref[1].astype(jnp.float32) - 2.0 * total[height:]
        both_ref[1] = (grad * kept_ref[1]).astype(both_ref.dtype)

    out = (
        pltpu.VMEM((2, height, width), pair.dtype),
        pltpu.VMEM((n_row * height, width), pair.dtype),
        pltpu.VMEM((2 * height, len(pair_held) * width), pair.dtype),
    )
    return call(kernel, "square_step", (pair, kept), masked_blocks, pair_held, out)


def last_step(both, kept, masked_cols, pair_rows, both_held, grad_blocks, filtered_blocks):
    _, height, width = both.shape
    n_row = len(grad_blocks)

    def kernel(here, fixed, blocks, pairs, outs):
        both_ref, kept_ref, masked_ref, pair_ref = fixed
        purified_ref, gradient_ref, rows_ref, late_cols = outs
        fill_rows(rows_ref, pairs, here[1])
        for i, (at, block) in enumerate(blocks):
            part(late_cols.at[i // n_row], here[0] ^ at, height)[...] = block[...]
        total = dot(rows_ref[...], masked_ref[...])
        cubic = total[:height] * kept_ref[1]
        purified_ref[...] = (3.0 * both_ref[0].astype(jnp.float32) - 2.0 * cubic).astype(purified_ref.dtype)
        summed = total[height:] + dot(pair_ref[:height], late_cols[0])
        summed = summed - 2.0 * dot(rows_ref[:height], late_cols[1])
        gradient_ref[...] = (summed * kept_ref[0]).astype(gradient_ref.dtype)

    out = jax.ShapeDtypeStruct((height, width), both.dtype)
    scratch = [
        pltpu.VMEM((2 * height, len(both_held) * width), both.dtype),
        pltpu.VMEM((2, n_row * height, width), both.dtype),
    ]
    fixed = (both, kept, masked_cols, pair_rows)
    return call(kernel, "last_step", fixed, grad_blocks + filtered_blocks, both_held, (out, out), scratch)


def take(held, *inner):
    return [(at, (array, (k,) + inner)) for ats, array in held for k, at in enumerate(ats)]


def cut(held, k):
    return [(ats, array[:, k]) for ats, array in held]


def pairs_of(one, two):
    return [(ats, jnp.stack([first, second], 1)) for (ats, first), (_, second) in zip(one, two)]


def across_cores(lists, n_row):
    ats = [[at for ats, _ in held for at in ats] for held in lists]
    assert all(sorted(a) == sorted(ats[0]) for a in ats)
    flips = flips_of(n_row)[-1:]
    sent = jnp.stack([jnp.concatenate([array for _, array in held]) for held in lists])
    got = [lax.ppermute(sent, "row", [(i, i ^ flip) for i in range(n_row)]) for flip in flips]
    return [
        take(held) + [(at ^ flip, (array, (k, i))) for flip, array in zip(flips, got) for i, at in enumerate(own)]
        for k, (held, own) in enumerate(zip(lists, ats))
    ]


def on_device(n_row, n_col, density, cotangent, block_pattern, filter_pattern):
    chip_flips = flips_of(n_row)[:-1]
    lead, first, second = chip_flips[:-2], chip_flips[-2:-1], chip_flips[-1:]
    pair, kept = mask(density, cotangent, block_pattern, filter_pattern)

    own = double([([0], pair[None])], "row", n_row, lead)
    masked, filtered = cut(own, 0), cut(own, 1)
    pair_held, later = exchange(pair, "col", n_col, False, filtered)
    far = swap(masked, "row", n_row, first)
    near = swap(masked, "row", n_row, second)
    masked = masked + far + near + swap(far, "row", n_row, second)
    other = swap(later, "row", n_row, second)
    (got,) = across_cores([masked + filtered], n_row)
    half, count = len(got) // 2, len(take(masked))
    masked_blocks = got[:count] + got[half:half + count]
    filtered_blocks = got[count:half] + got[half + count:]
    both, masked_cols, pair_rows = square_step(pair, kept, masked_blocks, pair_held)

    both_held, _ = exchange(both, "col", n_col, True)
    grad = double([([0], both[1:])], "row", n_row, lead)
    far = swap(grad, "row", n_row, second)
    left = swap(pairs_of(grad, filtered), "row", n_row, first)
    right = swap(pairs_of(far, other), "row", n_row, first)
    grad = grad + far + cut(left, 0) + cut(right, 0)
    filtered = other + cut(left, 1) + cut(right, 1)
    (got,) = across_cores([grad + filtered], n_row)
    half, count = len(got) // 2, len(take(grad))
    grad_blocks = got[:count] + got[half:half + count]
    filtered_blocks = filtered_blocks + got[count:half] + got[half + count:]
    return last_step(both, kept, masked_cols, pair_rows, both_held, grad_blocks, filtered_blocks)


def solution(mesh):
    placed = (P("row", "col"), P("row", "col"), P("row", "col"), P("row", "col"))

    def local(*arrays):
        return on_device(mesh.shape["row"], mesh.shape["col"], *arrays)

    return jax.shard_map(
        local,
        mesh=mesh,
        in_specs=placed,
        out_specs=(P("row", "col"), P("row", "col")),
        check_vma=False,
    )
```
